32 devices in a mesh: ctx: 4 (over y, x), head: 4 (over z), var: 2 (over core).
Axes of the slice: x: 2, y: 2, z: 4, core: 2. Of those that a mesh axis runs over, the one named last changes fastest.
Arguments:
- sequence: bfloat16 [2048, 1536], P('ctx', 'head'), may hold values from -8 to 8
- deletions: int32 [8, 2], P('var'), parts along dimension 0, may hold values from 0 to 2048, as said below
- conv_taps: float32 [3, 1536], P(None, 'head'), may hold values from -3 to 3
- conv_bias: float32 [1536], P('head'), may hold values from -3 to 3
- w_proj: bfloat16 [1536, 3584], P(None, 'head'), may hold values from -1 to 1
- w_out: bfloat16 [1536, 1536], P('head'), may hold values from -0.15625 to 0.15625
- w_pair: bfloat16 [1536, 256], P('head'), may hold values from -0.15625 to 0.15625
- dist_table: float32 [16, 128], replicated, may hold values from -3 to 3
Outputs:
- pair_map: bfloat16 [8, 512, 512, 128], P('var', 'ctx', 'head'), parts along dimension 0
The draws below stay inside these ranges and needn't reach their ends.
There are 2 independent parts, one for each index of `var`. The reference program is written for one: setup_inputs(seed, part) draws one part's arguments, and reference() takes and returns one part's arrays. A program takes and returns all parts, laid end to end along the dimension named above; an argument that names none is the same for every part. Nothing has to cross between parts.
Inputs may be any that keep to these rules, and one draw needn't show every extreme that they name: `deletions`: each variant deletes 1 to 128 consecutive tokens, some variant deletes exactly 128, and some variant's deletion ends at the last token of the locus.
All inputs are finite; a program needn't handle non-finite values.
Results may differ from the reference program's by a relative error of at most 0.025.
Values may be sent and summed in bfloat16 or wider, within the bound.
No kernel may reach another device: no remote copies, remote signals or barrier semaphores. Data moves between devices by JAX's collectives and lax.ppermute only.
A program may use at most 128 MiB of HBM per device.

```python
import math
import jax
import jax.numpy as jnp
from jax import lax

MODEL_WIDTH = 1536
H = 8
HD = 128
VD = 192
C = 128
NB = 16
POOL = 4
VARS = 4
LOCUS_TOKENS = 2048
DILATION_STEP = 256
DEL_MAX = 128
PAIR_ROWS = 512
N_HEAD = 4


def draw_sequence(key, part):
    return jnp.clip(jax.random.normal(key, (LOCUS_TOKENS, MODEL_WIDTH), jnp.float32), -6.0, 6.0).astype(jnp.bfloat16)


def draw_w_proj(key, part):
    first_key = jax.random.fold_in(key, 0)
    spread = 1.0 / math.sqrt(MODEL_WIDTH)
    normal_part = jnp.clip(jax.random.normal(first_key, (MODEL_WIDTH, H * (2 * HD + VD)), jnp.float32), -6.0, 6.0)
    return (normal_part * spread).astype(jnp.bfloat16)


def draw_deletions(key, part):
    first_key, second_key, third_key, fourth_key = jax.random.split(key, 4)
    starts = jax.random.randint(first_key, (VARS,), 0, LOCUS_TOKENS - DEL_MAX + 1)
    lengths = jax.random.randint(second_key, (VARS,), 1, DEL_MAX + 1)
    chosen = jax.random.randint(third_key, (), 0, VARS)
    lengths = jnp.where(jnp.arange(VARS) == chosen, DEL_MAX, lengths)
    at_end = jax.random.randint(fourth_key, (), 0, VARS)
    starts = jnp.where(jnp.arange(VARS) == at_end, LOCUS_TOKENS - lengths, starts)
    return jnp.stack([starts, starts + lengths], 1).astype(jnp.int32)


def shard_levels(rng, dims, pieces, low, high):
    def one(axis_at, blocks):
        steps = jax.random.uniform(jax.random.fold_in(jax.random.fold_in(rng, 6), axis_at), (blocks,), jnp.float32, low / len(pieces), high / len(pieces))
        return jnp.repeat(jnp.exp(steps), dims[axis_at] // blocks).reshape((-1,) + (1,) * (len(dims) - axis_at - 1))

    loudness = one(*pieces[0])
    for cut in pieces[1:]:
        loudness = loudness * one(*cut)
    return loudness


def bell_draw(rng, extent, deviation, reach, cuts=(), kind=jnp.bfloat16):
    drawn = deviation * jax.random.normal(rng, extent, jnp.float32)
    if cuts:
        drawn = drawn * shard_levels(rng, extent, cuts, -0.22, 0.18)
    return jnp.clip(drawn, -reach, reach).astype(kind)


def setup_inputs(seed: int = 0, part: int = 0) -> dict:
    splits = jax.random.split(jax.random.key(seed), 9)
    part_splits = jax.random.split(jax.random.fold_in(splits[8], part), 9)
    sequence = draw_sequence(jax.random.fold_in(splits[8], 71), part)
    deletions = draw_deletions(jax.random.fold_in(jax.random.fold_in(splits[8], part), 71), part)
    conv_taps = bell_draw(splits[2], (3, MODEL_WIDTH), 0.5, 3.0, ((1, 4),), jnp.float32)
    conv_bias = bell_draw(splits[3], (MODEL_WIDTH,), 0.5, 3.0, ((0, 4),), jnp.float32)
    w_proj = draw_w_proj(jax.random.fold_in(splits[8], 71), part)
    w_out = bell_draw(splits[5], (H * VD, MODEL_WIDTH), (H * VD) ** -0.5, 0.15625, ((0, 4),))
    w_pair = bell_draw(splits[6], (MODEL_WIDTH, 2 * C), MODEL_WIDTH ** -0.5, 0.15625, ((0, 4),))
    dist_table = bell_draw(splits[7], (NB, C), 0.5, 3.0, (), jnp.float32)
    return dict(sequence=sequence, deletions=deletions, conv_taps=conv_taps, conv_bias=conv_bias, w_proj=w_proj, w_out=w_out, w_pair=w_pair, dist_table=dist_table)


def bucket_of(distance):
    buckets = jnp.zeros(distance.shape, jnp.int32)
    for power_index in range(NB - 1):
        buckets = buckets + (distance >= 2 ** power_index).astype(jnp.int32)
    return buckets

def attend_head(operands):
    queries, key_rows, value_rows = operands
    scores = jnp.dot(queries, key_rows.T, preferred_element_type=jnp.float32) / math.sqrt(HD)
    row_max = scores.max(1, keepdims=True)
    weights = jnp.exp(scores - row_max)
    row_sum = weights.sum(1, keepdims=True)
    return jnp.dot(weights.astype(jnp.bfloat16), value_rows, preferred_element_type=jnp.float32) / row_sum

def one_variant(deletion, sequence, conv_taps, conv_bias, w_proj, w_out, w_pair, dist_table):
    positions = jnp.arange(LOCUS_TOKENS, dtype=jnp.int32)
    kept_bins = jnp.logical_or(positions < deletion[0], positions >= deletion[1])
    masked = jnp.where(kept_bins[:, None], sequence, jnp.zeros((), sequence.dtype))
    widened_rows = masked.astype(jnp.float32)
    zeroed_rows = jnp.zeros((DILATION_STEP, MODEL_WIDTH), jnp.float32)
    preceding_rows = jnp.concatenate([zeroed_rows, widened_rows[:LOCUS_TOKENS - DILATION_STEP]], 0)
    following_rows = jnp.concatenate([widened_rows[DILATION_STEP:], zeroed_rows], 0)
    convolved = conv_taps[0] * preceding_rows + conv_taps[1] * widened_rows + conv_taps[2] * following_rows + conv_bias
    trunk_out = (widened_rows + jax.nn.gelu(convolved, approximate=True)).astype(jnp.bfloat16)
    projected = jnp.dot(trunk_out, w_proj, preferred_element_type=jnp.float32).astype(jnp.bfloat16)
    projected = projected.reshape(LOCUS_TOKENS, H, 2 * HD + VD).transpose(1, 0, 2)
    head_out = lax.map(attend_head, (projected[:, :, :HD], projected[:, :, HD:2 * HD], projected[:, :, 2 * HD:]))
    head_out = head_out.transpose(1, 0, 2).reshape(LOCUS_TOKENS, H * VD).astype(jnp.bfloat16)
    group_width = H // N_HEAD * VD
    grouped = head_out.reshape(LOCUS_TOKENS, N_HEAD, group_width).transpose(1, 0, 2)
    w_groups = w_out.reshape(N_HEAD, group_width, MODEL_WIDTH)
    partial_value = jnp.einsum('gtc,gcd->gtd', grouped.astype(jnp.float32), w_groups.astype(jnp.float32)).astype(jnp.bfloat16)
    residual = trunk_out.astype(jnp.float32) + partial_value.astype(jnp.float32).sum(0)
    pooled = residual.reshape(PAIR_ROWS, POOL, MODEL_WIDTH).mean(1).astype(jnp.bfloat16)
    pair_proj = jnp.dot(pooled, w_pair, preferred_element_type=jnp.float32)
    pair_ids = jnp.arange(PAIR_ROWS, dtype=jnp.int32)
    distance = jnp.abs(pair_ids[:, None] - pair_ids[None, :])
    rel_table = dist_table[bucket_of(distance)]
    return (pair_proj[:, None, :C] + pair_proj[None, :, C:] + rel_table).astype(jnp.bfloat16)

def reference(sequence, deletions, conv_taps, conv_bias, w_proj, w_out, w_pair, dist_table):
    return lax.map(lambda deletion: one_variant(deletion, sequence, conv_taps, conv_bias, w_proj, w_out, w_pair, dist_table), deletions)
```

```python
import functools
import math

import jax
import jax.numpy as jnp
from jax import lax
from jax.experimental import pallas as pl
from jax.experimental.pallas import tpu as pltpu
from jax.sharding import PartitionSpec as P

HD = 128
VD = 192
VP = 256
C = 128
NB = 16
POOL = 4
WIN = 144
ALIGN = 16
SHIFTS = 8
ROWS = 16
MIB = 1024 * 1024
QSCALE = math.log2(math.e) / math.sqrt(HD)
GELU_A = math.sqrt(2.0 / math.pi)
GELU_B = GELU_A * 0.044715


def trunk_of(taps, low, middle, high):
    convolved = taps[0:1] * low + taps[1:2] * middle + taps[2:3] * high + taps[3:4]
    half = 0.5 * convolved
    bent = jnp.tanh(convolved * (GELU_A + GELU_B * (convolved * convolved)))
    return (middle + (half + half * bent)).astype(jnp.bfloat16)


def masked_trunk(rows, taps, h, start, count, step, first, last):
    tokens = start + lax.broadcasted_iota(jnp.int32, (count, 1), 0)
    parts = []
    for shift in (-step, 0, step):
        part = rows[h, pl.ds(pl.multiple_of(start + step + shift, ALIGN), count), :]
        kept = jnp.logical_or(tokens + shift < first, tokens + shift >= last)
        parts.append(jnp.where(kept, part.astype(jnp.float32), 0.0))
    return trunk_of(taps[h], *parts)


def window_starts(first, step, tokens):
    base = (first // ALIGN) * ALIGN
    return [
        pl.multiple_of(jnp.clip(base + shift, 0, tokens - WIN), ALIGN)
        for shift in (-step, 0, step)
    ]


def pool_matrix(count):
    wide = lax.broadcasted_iota(jnp.int32, (count // POOL, count), 1) // POOL
    tall = lax.broadcasted_iota(jnp.int32, (count // POOL, count), 0)
    return jnp.where(wide == tall, 1.0 / POOL, 0.0).astype(jnp.bfloat16)


def project_kernel(
    heads, dels, place, gathered, taps, weights, base_out, delta_out, pooled_out,
    rows, left, right, sems,
):
    n_ctx, n_head, n_var, step, width = gathered.shape
    tiles = n_ctx * n_var
    tokens = tiles * step
    variants = delta_out.shape[0]
    copies = []
    for tile in range(tiles):
        group = []
        for h in range(n_head):
            copy = pltpu.make_async_copy(
                gathered.at[tile // n_var, h, tile % n_var],
                rows.at[h, pl.ds((tile + 1) * step, step)],
                sems.at[tile, h],
            )
            copy.start()
            group.append(copy)
        copies.append(group)
    rows[:, 0:step] = jnp.zeros((n_head, step, width), jnp.bfloat16)
    rows[:, tokens + step :] = jnp.zeros((n_head, step, width), jnp.bfloat16)
    columns = weights.shape[1]
    at = lax.broadcasted_iota(jnp.int32, (1, columns), 1)
    ones = jnp.zeros((1, columns), jnp.float32)
    scale = jnp.where(at >= heads * (HD + VP), QSCALE, 1.0)
    for h in range(heads):
        ones = jnp.where(at == heads * HD + h * VP + VD, 1.0, ones)

    def wait_tile(tile):
        if tile < tiles:
            for copy in copies[tile]:
                copy.wait()

    def make_tile(tile, into):
        low = tile * step
        for h in range(n_head):
            into[0:step, h * width : (h + 1) * width] = trunk_of(
                taps[h],
                rows[h, low : low + step].astype(jnp.float32),
                rows[h, low + step : low + 2 * step].astype(jnp.float32),
                rows[h, low + 2 * step : low + 3 * step].astype(jnp.float32),
            )

    def make_delta(variant, into):
        first, last = dels[variant, 0], dels[variant, 1]
        for index, start in enumerate(window_starts(first, step, tokens)):
            for h in range(n_head):
                into[index * WIN : (index + 1) * WIN, h * width : (h + 1) * width] = masked_trunk(
                    rows, taps, h, start, WIN, step, first, last
                )

    def project(block, count):
        product = jnp.dot(block[0:count], weights[...], preferred_element_type=jnp.float32)
        return (product * scale + ones).astype(jnp.bfloat16)

    slots = (left, right)
    stages = [("tile", t) for t in range(tiles)] + [("delta", v) for v in range(variants)]

    def make(index):
        kind, which = stages[index]
        if kind == "tile":
            if which == 0:
                wait_tile(0)
            wait_tile(which + 1)
            make_tile(which, slots[index % 2])
        else:
            make_delta(which, slots[index % 2])

    make(0)
    for index, (kind, which) in enumerate(stages):
        if index + 1 < len(stages):
            make(index + 1)
        if kind == "tile":
            base_out[which * step : (which + 1) * step] = project(slots[index % 2], step)
        else:
            delta_out[which] = project(slots[index % 2], 3 * WIN)

    pool = pool_matrix(step)
    mine, ours = place[0], place[1]

    def pool_own(index, carry):
        variant, part = index // n_var, index % n_var
        start = (mine * n_var + part) * step
        block = masked_trunk(
            rows, taps, ours, start, step, step, dels[variant, 0], dels[variant, 1]
        )
        pooled = jnp.dot(pool, block, preferred_element_type=jnp.float32)
        count = step // POOL
        pooled_out[variant, pl.ds(pl.multiple_of(part * count, count), count)] = pooled.astype(
            jnp.bfloat16
        )
        return carry

    lax.fori_loop(0, variants * n_var, pool_own, 0)


def attend_kernel(heads, step, dels, place, base, delta, pooled, w_mix, w_pair, out, kvq):
    tokens = base.shape[0]
    variants = delta.shape[0]
    own = pooled.shape[1] * POOL
    tile = min(own, 256)
    own_start = place[0] * own
    pool = pool_matrix(tile)
    kvq[...] = base[...]

    def scores(h, part):
        low = heads * (HD + VP) + h * HD
        queries = kvq[pl.ds(pl.multiple_of(own_start + part * tile, tile), tile), low : low + HD]
        return lax.dot_general(
            queries,
            kvq[:, h * HD : (h + 1) * HD],
            (((1,), (1,)), ((), ())),
            preferred_element_type=jnp.float32,
        )

    def finish(h, found):
        low = heads * HD + h * VP
        row_max = jnp.max(found, axis=1, keepdims=True)
        weights = jnp.exp2(found - row_max).astype(jnp.bfloat16)
        mixed = jnp.dot(weights, kvq[:, low : low + VP], preferred_element_type=jnp.float32)
        mixed = (mixed * (1.0 / mixed[:, VD : VD + 1])).astype(jnp.bfloat16)
        return jnp.dot(pool, mixed, preferred_element_type=jnp.float32).astype(jnp.bfloat16)

    def one_variant(variant, carry):
        starts = window_starts(dels[variant, 0], step, tokens)
        for index, start in enumerate(starts):
            kvq[pl.ds(start, WIN)] = delta[variant, index * WIN : (index + 1) * WIN]
        chains = [(part, h) for part in range(own // tile) for h in range(heads)]
        ready = scores(chains[0][1], chains[0][0])
        for index, (part, h) in enumerate(chains):
            now = ready
            if index + 1 < len(chains):
                ready = scores(chains[index + 1][1], chains[index + 1][0])
            rows = slice(part * (tile // POOL), (part + 1) * (tile // POOL))
            if h == 0:
                total = jnp.dot(
                    pooled[variant, rows], w_pair[...], preferred_element_type=jnp.float32
                )
            total = total + jnp.dot(
                finish(h, now), w_mix[h], preferred_element_type=jnp.float32
            )
            if h == heads - 1:
                out[variant, rows] = total.astype(out.dtype)
        for start in starts:
            kvq[pl.ds(start, WIN)] = base[pl.ds(start, WIN)]
        return carry

    lax.fori_loop(0, variants, one_variant, 0)


def pair_kernel(place, row_feats, col_feats, table, out):
    block = pl.program_id(0)
    side = col_feats.shape[1]
    rows = table.shape[1] - side
    for r in range(ROWS):
        back = rows - 1 - (block * ROWS + r)
        low = pl.multiple_of((back // SHIFTS) * SHIFTS, SHIFTS)
        relative = table[(rows - 1 - r) % SHIFTS, pl.ds(low, side), :]
        for variant in range(out.shape[0]):
            out[variant, r] = (
                row_feats[variant, r : r + 1, :] + (col_feats[variant] + relative)
            ).astype(jnp.bfloat16)


def distance_table(dist_table, row_start, col_start, rows, cols):
    at = jnp.arange(SHIFTS, dtype=jnp.int32)[:, None] + jnp.arange(
        rows + cols, dtype=jnp.int32
    )
    distance = jnp.abs(row_start - col_start + rows - 1 - at)
    buckets = jnp.zeros(distance.shape, jnp.int32)
    for power_index in range(NB - 1):
        buckets = buckets + (distance >= 2**power_index).astype(jnp.int32)
    one_hot = (buckets[:, :, None] == jnp.arange(NB, dtype=jnp.int32)).astype(jnp.float32)
    return jnp.einsum("skb,bc->skc", one_hot, dist_table, precision=lax.Precision.HIGHEST)


def head_columns(w_proj, heads):
    by_head = w_proj.reshape(w_proj.shape[0], heads, 2 * HD + VD)
    queries = by_head[:, :, :HD].reshape(-1, heads * HD)
    keys = by_head[:, :, HD : 2 * HD].reshape(-1, heads * HD)
    values = jnp.pad(by_head[:, :, 2 * HD :], ((0, 0), (0, 0), (0, VP - VD)))
    return jnp.concatenate([keys, values.reshape(-1, heads * VP), queries], axis=1)


def whole(memory=pltpu.VMEM):
    return pl.BlockSpec(memory_space=memory)


def local(sequence, deletions, conv_taps, conv_bias, w_proj, w_out, w_pair, dist_table):
    own, width = sequence.shape
    variants = deletions.shape[0]
    heads = w_out.shape[0] // VD
    n_ctx, n_head, n_var = (lax.axis_size(name) for name in ("ctx", "head", "var"))
    step = own // 2
    tokens = n_ctx * own
    mine, ours, core = (lax.axis_index(name) for name in ("ctx", "head", "var"))
    place = jnp.stack([mine, ours]).astype(jnp.int32)

    half = lax.dynamic_slice_in_dim(sequence, core * step, step, 0)
    gathered = lax.all_gather(half, ("ctx", "head", "var"), axis=0, tiled=False)
    gathered = gathered.reshape(n_ctx, n_head, n_var, step, width)
    taps = lax.all_gather(
        jnp.concatenate([conv_taps, conv_bias[None], jnp.zeros((4, width), jnp.float32)], 0),
        "head",
        axis=0,
        tiled=False,
    )
    weights = head_columns(w_proj, heads)
    columns = weights.shape[1]
    base, delta, pooled = pl.pallas_call(
        functools.partial(project_kernel, heads),
        out_shape=(
            jax.ShapeDtypeStruct((tokens, columns), jnp.bfloat16),
            jax.ShapeDtypeStruct((variants, 3 * WIN, columns), jnp.bfloat16),
            jax.ShapeDtypeStruct((variants, own // POOL, width), jnp.bfloat16),
        ),
        in_specs=[whole(pltpu.SMEM), whole(pltpu.SMEM), whole(pl.ANY), whole(), whole()],
        out_specs=(whole(), whole(), whole()),
        scratch_shapes=[
            pltpu.VMEM((n_head, tokens + 2 * step, width), jnp.bfloat16),
            pltpu.VMEM((3 * WIN, n_head * width), jnp.bfloat16),
            pltpu.VMEM((3 * WIN, n_head * width), jnp.bfloat16),
            pltpu.SemaphoreType.DMA((n_ctx * n_var, n_head)),
        ],
        compiler_params=pltpu.CompilerParams(vmem_limit_bytes=56 * MIB),
        name="project",
    )(deletions, place, gathered, taps, weights)

    w_pair_all = lax.all_gather(w_pair, "head", axis=0, tiled=True)
    w_mix = jnp.dot(w_out, w_pair_all, preferred_element_type=jnp.float32).astype(jnp.bfloat16)
    w_mix = jnp.pad(w_mix.reshape(heads, VD, 2 * C), ((0, 0), (0, VP - VD), (0, 0)))
    partial = pl.pallas_call(
        functools.partial(attend_kernel, heads, step),
        out_shape=jax.ShapeDtypeStruct((variants, own // POOL, 2 * C), jnp.bfloat16),
        in_specs=[whole(pltpu.SMEM), whole(pltpu.SMEM)] + [whole()] * 5,
        out_specs=whole(),
        scratch_shapes=[pltpu.VMEM((tokens, columns), jnp.bfloat16)],
        compiler_params=pltpu.CompilerParams(vmem_limit_bytes=56 * MIB),
        name="attend",
    )(deletions, place, base, delta, pooled, w_mix, w_pair)

    pair_rows = own // POOL
    summed = lax.psum_scatter(
        partial.reshape(variants * pair_rows, 2 * C), "head", scatter_dimension=0, tiled=True
    )
    feats = lax.all_gather(summed, ("ctx", "head"), axis=0, tiled=False)
    feats = feats.reshape(n_ctx, variants, pair_rows, 2 * C).astype(jnp.float32)
    col_count = n_ctx * pair_rows // n_head
    row_feats = lax.dynamic_index_in_dim(feats, mine, 0, keepdims=False)[:, :, :C]
    col_feats = lax.dynamic_slice_in_dim(
        feats[..., C:].transpose(1, 0, 2, 3).reshape(variants, n_ctx * pair_rows, C),
        ours * col_count,
        col_count,
        1,
    )
    table = distance_table(
        dist_table, mine * pair_rows, ours * col_count, pair_rows, col_count
    )
    return pl.pallas_call(
        pair_kernel,
        grid=(pair_rows // ROWS,),
        out_shape=jax.ShapeDtypeStruct((variants, pair_rows, col_count, C), jnp.bfloat16),
        in_specs=[
            whole(pltpu.SMEM),
            pl.BlockSpec((variants, ROWS, C), lambda i: (0, i, 0)),
            pl.BlockSpec((variants, col_count, C), lambda i: (0, 0, 0)),
            pl.BlockSpec((SHIFTS, pair_rows + col_count, C), lambda i: (0, 0, 0)),
        ],
        out_specs=pl.BlockSpec((variants, ROWS, col_count, C), lambda i: (0, i, 0, 0)),
        compiler_params=pltpu.CompilerParams(vmem_limit_bytes=48 * MIB),
        name="pair_map",
    )(place, row_feats, col_feats, table)


def solution(mesh):
    in_specs = (
        P("ctx", "head"),
        P("var", None),
        P(None, "head"),
        P("head"),
        P(None, "head"),
        P("head", None),
        P("head", None),
        P(),
    )
    out_specs = P("var", "ctx", "head", None)
    return jax.shard_map(local, mesh=mesh, in_specs=in_specs, out_specs=out_specs, check_vma=False)
```

```python
import functools
import math

import jax
import jax.numpy as jnp
from jax import lax
from jax.experimental import pallas as pl
from jax.experimental.pallas import tpu as pltpu
from jax.sharding import PartitionSpec as P

HD = 128
VD = 192
VP = 256
C = 128
NB = 16
POOL = 4
WIN = 144
ALIGN = 16
GROUPS = 2
CHUNK = 512
SHIFTS = 8
ROWS = 16
MIB = 1024 * 1024
QSCALE = math.log2(math.e) / math.sqrt(HD)
GELU_A = math.sqrt(2.0 / math.pi)
GELU_B = GELU_A * 0.044715


def trunk_of(taps, low, middle, high):
    convolved = taps[0:1] * low + taps[1:2] * middle + taps[2:3] * high + taps[3:4]
    half = 0.5 * convolved
    bent = jnp.tanh(convolved * (GELU_A + GELU_B * (convolved * convolved)))
    return middle + (half + half * bent)


def masked_trunk(rows, taps, h, start, count, step, first, last):
    tokens = start + lax.broadcasted_iota(jnp.int32, (count, 1), 0)
    parts = []
    for shift in (-step, 0, step):
        part = rows[h, pl.ds(pl.multiple_of(start + step + shift, ALIGN), count), :]
        kept = jnp.logical_or(tokens + shift < first, tokens + shift >= last)
        parts.append(part * jnp.where(kept, 1.0, 0.0).astype(jnp.bfloat16))
    return trunk_of(taps.astype(jnp.bfloat16), *parts)


def pool_matrix(count):
    wide = lax.broadcasted_iota(jnp.int32, (count // POOL, count), 1) // POOL
    tall = lax.broadcasted_iota(jnp.int32, (count // POOL, count), 0)
    return jnp.where(wide == tall, 1.0 / POOL, 0.0).astype(jnp.bfloat16)


def window_table(deletions, step, tokens):
    variants = deletions.shape[0]
    count = -(-tokens // WIN)
    count += -(count + 3 * variants) % 3
    base = jnp.minimum(jnp.arange(count, dtype=jnp.int32) * WIN, tokens - WIN)
    none = jnp.full((count,), tokens, jnp.int32)
    lows = (deletions[:, :1] // ALIGN) * ALIGN + jnp.array([-step, 0, step], jnp.int32)
    lows = jnp.clip(lows, 0, tokens - WIN).reshape(-1)
    places = tokens + WIN * jnp.arange(3 * variants, dtype=jnp.int32)
    return jnp.concatenate(
        [
            jnp.stack([base, base, none, none], 1),
            jnp.stack(
                [lows, places, jnp.repeat(deletions[:, 0], 3), jnp.repeat(deletions[:, 1], 3)], 1
            ),
        ],
        0,
    )


def project_kernel(
    heads, n_var, count, dels, table, place, taps, weights, *refs
):
    pieces = refs[: 2 * count]
    out, pooled_out, rows, left, right, sems = refs[2 * count :]
    n_head, step, width = pieces[0].shape
    tokens = rows.shape[1] - 2 * step
    variants = dels.shape[0]
    ours, core = place[0], place[1]
    copies = []
    for index, piece in enumerate(pieces):
        half = core if index < count else 1 - core
        at = (place[2 + index % count] * n_var + half + 1) * step
        for s in range(n_head):
            copy = pltpu.make_async_copy(
                piece.at[s],
                rows.at[lax.rem(ours + n_head - s, n_head), pl.ds(pl.multiple_of(at, step), step)],
                sems.at[index, s],
            )
            copy.start()
            copies.append(copy)
    rows[:, 0:step] = jnp.zeros((n_head, step, width), jnp.bfloat16)
    rows[:, tokens + step :] = jnp.zeros((n_head, step, width), jnp.bfloat16)
    columns = weights.shape[1]
    at = lax.broadcasted_iota(jnp.int32, (1, columns), 1)
    ones = jnp.zeros((1, columns), jnp.float32)
    scale = jnp.where(at >= heads * (HD + VP), QSCALE, 1.0)
    for h in range(heads):
        ones = jnp.where(at == heads * HD + h * VP + VD, 1.0, ones)
    for copy in copies:
        copy.wait()

    def taps_at(h):
        return taps[lax.rem(ours + n_head - h, n_head)]

    def make(stage, into):
        for part in range(3):
            window = stage * 3 + part
            start = pl.multiple_of(table[window, 0], ALIGN)
            for h in range(n_head):
                into[part * WIN : (part + 1) * WIN, h * width : (h + 1) * width] = masked_trunk(
                    rows, taps_at(h), h, start, WIN, step, table[window, 2], table[window, 3]
                )

    def project(stage, block):
        product = jnp.dot(block[...], weights[...], preferred_element_type=jnp.float32)
        product = (product * scale + ones).astype(jnp.bfloat16)
        for part in range(3):
            place_at = pl.multiple_of(table[stage * 3 + part, 1], ALIGN)
            out[pl.ds(place_at, WIN)] = product[part * WIN : (part + 1) * WIN]

    stages = table.shape[0] // 3
    make(0, left)

    def two_stages(n, carry):
        make(2 * n + 1, right)
        project(2 * n, left)
        make(jnp.minimum(2 * n + 2, stages - 1), left)
        project(2 * n + 1, right)
        return carry

    lax.fori_loop(0, stages // 2, two_stages, 0)
    if stages % 2:
        project(stages - 1, left)

    pool = pool_matrix(step)
    mine = place[2]

    def pool_own(index, carry):
        variant, part = index // n_var, index % n_var
        start = (mine * n_var + part) * step
        block = masked_trunk(
            rows, taps[0], ours, start, step, step, dels[variant, 0], dels[variant, 1]
        )
        pooled = jnp.dot(pool, block, preferred_element_type=jnp.float32)
        size = step // POOL
        pooled_out[variant, pl.ds(pl.multiple_of(part * size, size), size)] = pooled.astype(
            jnp.bfloat16
        )
        return carry

    lax.fori_loop(0, variants * n_var, pool_own, 0)


def attend_kernel(
    heads, tokens, first_variant, table, place, projected, pooled, w_mix, w_pair,
    row_out, col_out, kvq, scores_a, scores_b, top_a, top_b, total,
):
    variants = row_out.shape[0]
    own = pooled.shape[1] * POOL
    own_start = pl.multiple_of(place[2] * own, own)
    chunk = scores_a.shape[2]
    steps = tokens // chunk
    skipped = table.shape[0] - 3 * pooled.shape[0]
    key_cols, value_cols = heads * HD, heads * (HD + VP)
    kvq[...] = projected[0:tokens]
    pool = pool_matrix(own)
    scores, tops = (scores_a, scores_b), (top_a, top_b)
    chains = [(v, h) for v in range(variants) for h in range(heads)]

    def overlay(variant, columns, back):
        for part in range(3):
            row = skipped + 3 * (first_variant + variant) + part
            start = pl.multiple_of(table[row, 0], ALIGN)
            source = start if back else pl.multiple_of(table[row, 1], ALIGN)
            for low, high in columns:
                kvq[pl.ds(start, WIN), low:high] = projected[pl.ds(source, WIN), low:high]

    key_query = [(0, key_cols), (value_cols, value_cols + heads * HD)]
    values = [(key_cols, value_cols)]

    def score(index, c):
        h = chains[index][1]
        low = value_cols + h * HD
        found = lax.dot_general(
            kvq[pl.ds(own_start, own), low : low + HD],
            kvq[pl.ds(pl.multiple_of(c * chunk, chunk), chunk), h * HD : (h + 1) * HD],
            (((1,), (1,)), ((), ())),
            preferred_element_type=jnp.float32,
        )
        scores[index % 2][c] = found
        best = found[:, 0:128]
        for low in range(128, chunk, 128):
            best = jnp.maximum(best, found[:, low : low + 128])
        top = tops[index % 2]
        top[...] = jnp.maximum(top[...], best)

    def prepare(index):
        variant, h = chains[index]
        if h == 0:
            if variant > 0:
                overlay(variant - 1, key_query, True)
            overlay(variant, key_query, False)
        tops[index % 2][...] = jnp.full(top_a.shape, -jnp.inf, jnp.float32)

    prepare(0)

    def first_scores(c, carry):
        score(0, c)
        return carry

    lax.fori_loop(0, steps, first_scores, 0)
    for index, (variant, h) in enumerate(chains):
        if h == 0:
            if variant > 0:
                overlay(variant - 1, values, True)
            overlay(variant, values, False)
        more = index + 1 < len(chains)
        if more:
            prepare(index + 1)
        row_max = jnp.max(tops[index % 2][...], axis=1, keepdims=True)
        total[...] = jnp.zeros(total.shape, jnp.float32)
        low = key_cols + h * VP

        def weigh(c, carry):
            weights = jnp.exp2(scores[index % 2][c] - row_max).astype(jnp.bfloat16)
            if more:
                score(index + 1, c)
            total[...] += jnp.dot(
                weights,
                kvq[pl.ds(pl.multiple_of(c * chunk, chunk), chunk), low : low + VP],
                preferred_element_type=jnp.float32,
            )
            return carry

        lax.fori_loop(0, steps, weigh, 0)
        mixed = total[...]
        mixed = (mixed * (1.0 / mixed[:, VD : VD + 1])).astype(jnp.bfloat16)
        mixed = jnp.dot(pool, mixed, preferred_element_type=jnp.float32).astype(jnp.bfloat16)
        if h == 0:
            pair = jnp.dot(
                pooled[first_variant + variant], w_pair[...], preferred_element_type=jnp.float32
            )
        pair = pair + jnp.dot(mixed, w_mix[h], preferred_element_type=jnp.float32)
        if h == heads - 1:
            row_out[variant] = pair[:, :C].astype(jnp.bfloat16)
            col_out[variant] = pair[:, C:].astype(jnp.bfloat16)


def pair_kernel(n_head, n_ctx, table, *refs):
    row_feats = refs[:n_head]
    col_feats = refs[n_head : n_head + n_ctx]
    out, cols = refs[-2:]
    block = pl.program_id(0)
    side = cols.shape[1]

    @pl.when(block == 0)
    def _():
        cols[...] = sum(ref[...].astype(jnp.float32) for ref in col_feats)

    row_sums = sum(ref[...].astype(jnp.float32) for ref in row_feats)
    rows = table.shape[1] - side
    for r in range(ROWS):
        back = rows - 1 - (block * ROWS + r)
        low = pl.multiple_of((back // SHIFTS) * SHIFTS, SHIFTS)
        relative = table[(rows - 1 - r) % SHIFTS, pl.ds(low, side), :]
        for variant in range(out.shape[0]):
            out[variant, r] = (
                row_sums[variant, r : r + 1, :] + (cols[variant] + relative)
            ).astype(jnp.bfloat16)


def distance_table(dist_table, row_start, col_start, rows, cols):
    at = jnp.arange(SHIFTS, dtype=jnp.int32)[:, None] + jnp.arange(
        rows + cols, dtype=jnp.int32
    )
    distance = jnp.abs(row_start - col_start + rows - 1 - at)
    buckets = jnp.zeros(distance.shape, jnp.int32)
    for power_index in range(NB - 1):
        buckets = buckets + (distance >= 2**power_index).astype(jnp.int32)
    one_hot = (buckets[:, :, None] == jnp.arange(NB, dtype=jnp.int32)).astype(jnp.float32)
    return jnp.einsum("skb,bc->skc", one_hot, dist_table, precision=lax.Precision.HIGHEST)


def head_columns(w_proj, heads):
    by_head = w_proj.reshape(w_proj.shape[0], heads, 2 * HD + VD)
    queries = by_head[:, :, :HD].reshape(-1, heads * HD)
    keys = by_head[:, :, HD : 2 * HD].reshape(-1, heads * HD)
    values = jnp.pad(by_head[:, :, 2 * HD :], ((0, 0), (0, 0), (0, VP - VD)))
    return jnp.concatenate([keys, values.reshape(-1, heads * VP), queries], axis=1)


def whole(memory=pltpu.VMEM):
    return pl.BlockSpec(memory_space=memory)


def shifts(array, axis):
    size = lax.axis_size(axis)
    return [array] + [
        lax.ppermute(array, axis, [(k, (k + s) % size) for k in range(size)])
        for s in range(1, size)
    ]


def gather_rows(block, n_ctx, n_var, mine):
    slab = jnp.stack(shifts(block, "head"))
    if n_ctx == 4 and n_var == 2:
        over_x = lax.ppermute(slab, "ctx", [(k, k ^ 1) for k in range(4)])
        over_y = lax.ppermute(slab, "ctx", [(k, k ^ 2) for k in range(4)])
        both = ("ctx", "var")
        corner_x = lax.ppermute(over_y, both, [(2 * k, 2 * (k ^ 1)) for k in range(4)])
        corner_y = lax.ppermute(over_x, both, [(2 * k + 1, 2 * (k ^ 2) + 1) for k in range(4)])
        return [slab, over_x, over_y, corner_x + corner_y], [mine ^ k for k in range(4)]
    return shifts(slab, "ctx"), [(mine + n_ctx - s) % n_ctx for s in range(n_ctx)]


def local(sequence, deletions, conv_taps, conv_bias, w_proj, w_out, w_pair, dist_table):
    own, width = sequence.shape
    variants = deletions.shape[0]
    heads = w_out.shape[0] // VD
    n_ctx, n_head, n_var = (lax.axis_size(name) for name in ("ctx", "head", "var"))
    if n_ctx != n_head or n_var != 2:
        raise ValueError("mesh shape")
    step = own // n_var
    tokens = n_ctx * own
    pair_rows = own // POOL
    mine, ours, core = (lax.axis_index(name) for name in ("ctx", "head", "var"))

    half = lax.dynamic_slice_in_dim(sequence, core * step, step, 0)
    pieces, blocks = gather_rows(half, n_ctx, n_var, mine)
    crossed = [lax.ppermute(piece, "var", [(0, 1), (1, 0)]) for piece in pieces]
    place = jnp.stack([ours, core] + blocks).astype(jnp.int32)
    taps = jnp.concatenate([conv_taps, conv_bias[None], jnp.zeros((4, width), jnp.float32)], 0)
    taps = jnp.stack(shifts(taps, "head"))
    weights = head_columns(w_proj, heads)
    columns = weights.shape[1]
    windows = window_table(deletions, step, tokens)
    projected, pooled = pl.pallas_call(
        functools.partial(project_kernel, heads, n_var, len(pieces)),
        out_shape=(
            jax.ShapeDtypeStruct((tokens + 3 * WIN * variants, columns), jnp.bfloat16),
            jax.ShapeDtypeStruct((variants, pair_rows, width), jnp.bfloat16),
        ),
        in_specs=[whole(pltpu.SMEM)] * 3 + [whole()] * 2 + [whole(pl.ANY)] * (2 * len(pieces)),
        out_specs=(whole(), whole()),
        scratch_shapes=[
            pltpu.VMEM((n_head, tokens + 2 * step, width), jnp.bfloat16),
            pltpu.VMEM((3 * WIN, n_head * width), jnp.bfloat16),
            pltpu.VMEM((3 * WIN, n_head * width), jnp.bfloat16),
            pltpu.SemaphoreType.DMA((2 * len(pieces), n_head)),
        ],
        compiler_params=pltpu.CompilerParams(vmem_limit_bytes=56 * MIB),
        name="project",
    )(deletions, windows, place, taps, weights, *pieces, *crossed)

    late_pair, _ = lax.optimization_barrier((w_pair, pieces[0]))
    w_mix = jnp.zeros((heads * VD, 2 * C), jnp.float32)
    for s, part in enumerate(shifts(late_pair, "head")):
        from_head = (ours + n_head - s) % n_head
        w_mix += jnp.dot(
            lax.dynamic_slice_in_dim(w_out, from_head * width, width, 1),
            part,
            preferred_element_type=jnp.float32,
        )
    w_mix = w_mix.astype(jnp.bfloat16).reshape(heads, VD, 2 * C)
    w_mix = jnp.pad(w_mix, ((0, 0), (0, VP - VD), (0, 0)))
    table = distance_table(dist_table, mine * pair_rows, ours * pair_rows, pair_rows, pair_rows)

    group = variants // GROUPS
    chunk = min(tokens, CHUNK)
    feats = []
    for g in range(GROUPS):
        row_part, col_part = pl.pallas_call(
            functools.partial(attend_kernel, heads, tokens, g * group),
            out_shape=[jax.ShapeDtypeStruct((group, pair_rows, C), jnp.bfloat16)] * 2,
            in_specs=[whole(pltpu.SMEM)] * 2 + [whole()] * 4,
            out_specs=[whole(), whole()],
            scratch_shapes=[
                pltpu.VMEM((tokens, columns), jnp.bfloat16),
                pltpu.VMEM((tokens // chunk, own, chunk), jnp.float32),
                pltpu.VMEM((tokens // chunk, own, chunk), jnp.float32),
                pltpu.VMEM((own, 128), jnp.float32),
                pltpu.VMEM((own, 128), jnp.float32),
                pltpu.VMEM((own, VP), jnp.float32),
            ],
            compiler_params=pltpu.CompilerParams(vmem_limit_bytes=56 * MIB),
            name="attend",
        )(windows, place, projected, pooled, w_mix, w_pair)
        turned = lax.ppermute(
            col_part,
            ("ctx", "head"),
            [(i * n_head + h, h * n_head + i) for i in range(n_ctx) for h in range(n_head)],
        )
        feats.append(shifts(row_part, "head") + shifts(turned, "ctx"))

    result = []
    for g in range(GROUPS):
        result = [
            pl.pallas_call(
                functools.partial(pair_kernel, n_head, n_ctx),
                grid=(pair_rows // ROWS,),
                out_shape=jax.ShapeDtypeStruct((variants, pair_rows, pair_rows, C), jnp.bfloat16),
                in_specs=[pl.BlockSpec((SHIFTS, 2 * pair_rows, C), lambda i: (0, 0, 0))]
                + [pl.BlockSpec((group, ROWS, C), lambda i: (0, i, 0))] * n_head
                + [pl.BlockSpec((group, pair_rows, C), lambda i: (0, 0, 0))] * n_ctx
                + [whole(pl.ANY)] * len(result),
                out_specs=pl.BlockSpec(
                    (group, ROWS, pair_rows, C), functools.partial(lambda g, i: (g, i, 0, 0), g)
                ),
                scratch_shapes=[pltpu.VMEM((group, pair_rows, C), jnp.float32)],
                input_output_aliases={1 + n_head + n_ctx: 0} if result else {},
                compiler_params=pltpu.CompilerParams(vmem_limit_bytes=48 * MIB),
                name="pair_map",
            )(table, *feats[g], *result)
        ]
    return result[0]


def solution(mesh):
    in_specs = (
        P("ctx", "head"),
        P("var", None),
        P(None, "head"),
        P("head"),
        P(None, "head"),
        P("head", None),
        P("head", None),
        P(),
    )
    out_specs = P("var", "ctx", "head", None)
    return jax.shard_map(local, mesh=mesh, in_specs=in_specs, out_specs=out_specs, check_vma=False)
```

```python
import functools
import math

import jax
import jax.numpy as jnp
from jax import lax
from jax.experimental import pallas as pl
from jax.experimental.pallas import tpu as pltpu
from jax.sharding import PartitionSpec as P

HD = 128
VD = 192
VP = 256
C = 128
NB = 16
POOL = 4
WIN = 144
ALIGN = 16
CHUNK = 512
SHIFTS = 8
ROWS = 16
MIB = 1024 * 1024
QSCALE = math.log2(math.e) / math.sqrt(HD)
GELU_A = math.sqrt(2.0 / math.pi)
GELU_B = GELU_A * 0.044715


def trunk_of(taps, low, middle, high):
    convolved = taps[0:1] * low + taps[1:2] * middle + taps[2:3] * high + taps[3:4]
    half = 0.5 * convolved
    bent = jnp.tanh(convolved * (GELU_A + GELU_B * (convolved * convolved)))
    return middle + (half + half * bent)


def masked_trunk(rows, taps, h, start, count, step, first, last):
    tokens = start + lax.broadcasted_iota(jnp.int32, (count, 1), 0)
    parts = []
    for shift in (-step, 0, step):
        part = rows[h, pl.ds(pl.multiple_of(start + step + shift, ALIGN), count), :]
        kept = jnp.logical_or(tokens + shift < first, tokens + shift >= last)
        parts.append(part * jnp.where(kept, 1.0, 0.0).astype(jnp.bfloat16))
    return trunk_of(taps.astype(jnp.bfloat16), *parts)


def pool_matrix(count):
    wide = lax.broadcasted_iota(jnp.int32, (count // POOL, count), 1) // POOL
    tall = lax.broadcasted_iota(jnp.int32, (count // POOL, count), 0)
    return jnp.where(wide == tall, 1.0 / POOL, 0.0).astype(jnp.bfloat16)


def project_kernel(
    heads, n_var, count, n_head, dels, place, w_proj, *refs
):
    taps = refs[:n_head]
    pieces = refs[n_head : n_head + 2 * count]
    out, pooled_out, weights, rows, left, right, sems = refs[n_head + 2 * count :]
    step, width = pieces[0].shape[1:]
    tokens = out.shape[0]
    ours, core, variant = place[0], place[1], place[2]
    copies = []
    for index, piece in enumerate(pieces):
        half = core if index < count else 1 - core
        at = (place[3 + index % count] * n_var + half + 1) * step
        for s in range(n_head):
            copy = pltpu.make_async_copy(
                piece.at[s],
                rows.at[lax.rem(ours + n_head - s, n_head), pl.ds(pl.multiple_of(at, step), step)],
                sems.at[index, s],
            )
            copy.start()
            copies.append(copy)
    rows[:, 0:step] = jnp.zeros((n_head, step, width), jnp.bfloat16)
    rows[:, tokens + step :] = jnp.zeros((n_head, step, width), jnp.bfloat16)
    columns = weights.shape[1]
    for h in range(heads):
        low, key, value = h * (2 * HD + VD), h * HD, heads * HD + h * VP
        query = heads * (HD + VP) + h * HD
        weights[:, key : key + HD] = w_proj[:, low + HD : low + 2 * HD]
        weights[:, value : value + VD] = w_proj[:, low + 2 * HD : low + 2 * HD + VD]
        weights[:, value + VD : value + VP] = jnp.zeros((weights.shape[0], VP - VD), jnp.bfloat16)
        weights[:, query : query + HD] = w_proj[:, low : low + HD]
    at = lax.broadcasted_iota(jnp.int32, (1, columns), 1)
    ones = jnp.zeros((1, columns), jnp.float32)
    scale = jnp.where(at >= heads * (HD + VP), QSCALE, 1.0)
    for h in range(heads):
        ones = jnp.where(at == heads * HD + h * VP + VD, 1.0, ones)
    for copy in copies:
        copy.wait()

    first, last = dels[variant, 0], dels[variant, 1]
    plain = -(-tokens // WIN)
    plain += -(plain + 3) % 6
    stages = (plain + 3) // 3

    def window(index):
        moved = (first // ALIGN) * ALIGN + (index - plain - 1) * step
        start = jnp.where(index < plain, index * WIN, moved)
        start = pl.multiple_of(jnp.clip(start, 0, tokens - WIN), ALIGN)
        return start, jnp.where(index < plain, tokens, first), jnp.where(index < plain, tokens, last)

    def taps_at(h):
        values = taps[0][...]
        for s in range(1, n_head):
            values = jnp.where(lax.rem(ours + n_head - h, n_head) == s, taps[s][...], values)
        return values

    all_taps = [taps_at(h) for h in range(n_head)]

    def make(stage, into):
        for part in range(3):
            start, low, high = window(stage * 3 + part)
            for h in range(n_head):
                into[part * WIN : (part + 1) * WIN, h * width : (h + 1) * width] = masked_trunk(
                    rows, all_taps[h], h, start, WIN, step, low, high
                )

    def project(stage, block):
        product = jnp.dot(block[...], weights[...], preferred_element_type=jnp.float32)
        product = (product * scale + ones).astype(jnp.bfloat16)
        for part in range(3):
            out[pl.ds(window(stage * 3 + part)[0], WIN)] = product[part * WIN : (part + 1) * WIN]

    make(0, left)

    def two_stages(n, carry):
        make(2 * n + 1, right)
        project(2 * n, left)
        make(2 * n + 2, left)
        project(2 * n + 1, right)
        return carry

    lax.fori_loop(0, stages // 2 - 1, two_stages, 0)
    make(stages - 1, right)
    project(stages - 2, left)
    project(stages - 1, right)

    pool = pool_matrix(step)

    def pool_rows(tile, carry):
        block = masked_trunk(
            rows, taps[0][...], ours, pl.multiple_of(tile * step, step), step, step, first, last
        )
        pooled = jnp.dot(pool, block, preferred_element_type=jnp.float32)
        size = step // POOL
        pooled_out[pl.ds(pl.multiple_of(tile * size, size), size)] = pooled.astype(jnp.bfloat16)
        return carry

    lax.fori_loop(0, tokens // step, pool_rows, 0)


def attend_kernel(
    heads, own, order, kvq, pooled, w_mix, w_pair,
    out, scores_a, scores_b, top_a, top_b, total,
):
    tokens = kvq.shape[0]
    chunk = scores_a.shape[2]
    steps = tokens // chunk
    key_cols, value_cols = heads * HD, heads * (HD + VP)
    pool = pool_matrix(own)
    scores, tops = (scores_a, scores_b), (top_a, top_b)
    chains = [(n, h) for n in range(out.shape[0]) for h in range(heads)]

    def score(index, c):
        n, h = chains[index]
        low = value_cols + h * HD
        found = lax.dot_general(
            kvq[pl.ds(pl.multiple_of(order[n] * own, own), own), low : low + HD],
            kvq[pl.ds(pl.multiple_of(c * chunk, chunk), chunk), h * HD : (h + 1) * HD],
            (((1,), (1,)), ((), ())),
            preferred_element_type=jnp.float32,
        )
        scores[index % 2][c] = found
        best = found[:, 0:128]
        for low in range(128, chunk, 128):
            best = jnp.maximum(best, found[:, low : low + 128])
        top = tops[index % 2]
        top[...] = jnp.maximum(top[...], best)

    def clear(index):
        tops[index % 2][...] = jnp.full(top_a.shape, -jnp.inf, jnp.float32)

    clear(0)

    def first_scores(c, carry):
        score(0, c)
        return carry

    lax.fori_loop(0, steps, first_scores, 0)
    for index, (n, h) in enumerate(chains):
        more = index + 1 < len(chains)
        if more:
            clear(index + 1)
        row_max = jnp.max(tops[index % 2][...], axis=1, keepdims=True)
        total[...] = jnp.zeros(total.shape, jnp.float32)
        low = key_cols + h * VP

        def weigh(c, carry):
            weights = jnp.exp2((scores[index % 2][c] - row_max).astype(jnp.bfloat16))
            if more:
                score(index + 1, c)
            total[...] += jnp.dot(
                weights,
                kvq[pl.ds(pl.multiple_of(c * chunk, chunk), chunk), low : low + VP],
                preferred_element_type=jnp.float32,
            )
            return carry

        lax.fori_loop(0, steps, weigh, 0)
        mixed = total[...]
        mixed = (mixed * (1.0 / mixed[:, VD : VD + 1])).astype(jnp.bfloat16)
        mixed = jnp.dot(pool, mixed, preferred_element_type=jnp.float32).astype(jnp.bfloat16)
        if h == 0:
            size = own // POOL
            pair = jnp.dot(
                pooled[pl.ds(pl.multiple_of(order[n] * size, size), size)],
                w_pair[...],
                preferred_element_type=jnp.float32,
            )
        pair = pair + jnp.dot(mixed, w_mix[h], preferred_element_type=jnp.float32)
        if h == heads - 1:
            out[n] = pair.astype(out.dtype)


def pair_kernel(variants, order, table, *refs):
    row_feats = refs[:variants]
    col_feats = refs[variants : 2 * variants]
    out, rows, cols = refs[2 * variants :]
    block = pl.program_id(0)
    side = cols.shape[1]

    @pl.when(block == 0)
    def _():
        for s in range(variants):
            rows[order[s]] = row_feats[s][...].astype(jnp.float32)
            cols[order[variants + s]] = col_feats[s][...].astype(jnp.float32)

    count = table.shape[1] - side
    for r in range(ROWS):
        back = count - 1 - (block * ROWS + r)
        low = pl.multiple_of((back // SHIFTS) * SHIFTS, SHIFTS)
        relative = table[(count - 1 - r) % SHIFTS, pl.ds(low, side), :]
        for variant in range(variants):
            row = rows[variant, pl.ds(block * ROWS + r, 1), :]
            out[variant, r] = (row + (cols[variant] + relative)).astype(jnp.bfloat16)


def distance_table(dist_table, row_start, col_start, rows, cols):
    at = jnp.arange(SHIFTS, dtype=jnp.int32)[:, None] + jnp.arange(
        rows + cols, dtype=jnp.int32
    )
    distance = jnp.abs(row_start - col_start + rows - 1 - at)
    buckets = jnp.zeros(distance.shape, jnp.int32)
    for power_index in range(NB - 1):
        buckets = buckets + (distance >= 2**power_index).astype(jnp.int32)
    one_hot = (buckets[:, :, None] == jnp.arange(NB, dtype=jnp.int32)).astype(jnp.float32)
    return jnp.einsum("skb,bc->skc", one_hot, dist_table, precision=lax.Precision.HIGHEST)


def whole(memory=pltpu.VMEM):
    return pl.BlockSpec(memory_space=memory)


def shifts(array, axis):
    size = lax.axis_size(axis)
    return [array] + [
        lax.ppermute(array, axis, [(k, (k + s) % size) for k in range(size)])
        for s in range(1, size)
    ]


def gather_rows(block, n_ctx, n_var, mine):
    slab = jnp.stack(shifts(block, "head"))
    if n_ctx == 4 and n_var == 2:
        over_x = lax.ppermute(slab, "ctx", [(k, k ^ 1) for k in range(4)])
        over_y = lax.ppermute(slab, "ctx", [(k, k ^ 2) for k in range(4)])
        both = ("ctx", "var")
        corner_x = lax.ppermute(over_y, both, [(2 * k, 2 * (k ^ 1)) for k in range(4)])
        corner_y = lax.ppermute(over_x, both, [(2 * k + 1, 2 * (k ^ 2) + 1) for k in range(4)])
        return [slab, over_x, over_y, corner_x + corner_y], [mine ^ k for k in range(4)]
    return shifts(slab, "ctx"), [(mine + n_ctx - s) % n_ctx for s in range(n_ctx)]


def local(sequence, deletions, conv_taps, conv_bias, w_proj, w_out, w_pair, dist_table):
    own, width = sequence.shape
    variants = deletions.shape[0]
    heads = w_out.shape[0] // VD
    n_ctx, n_head, n_var = (lax.axis_size(name) for name in ("ctx", "head", "var"))
    if n_ctx != n_head or n_var != 2 or n_ctx % variants:
        raise ValueError("mesh shape")
    step = own // n_var
    tokens = n_ctx * own
    pair_rows = own // POOL
    columns = heads * (2 * HD + VP)
    splits = n_ctx // variants
    mine, ours, core = (lax.axis_index(name) for name in ("ctx", "head", "var"))

    half = lax.dynamic_slice_in_dim(sequence, core * step, step, 0)
    pieces, blocks = gather_rows(half, n_ctx, n_var, mine)
    crossed = [lax.ppermute(piece, "var", [(0, 1), (1, 0)]) for piece in pieces]
    place = jnp.stack([ours, core, mine // splits] + blocks).astype(jnp.int32)
    taps = shifts(jnp.concatenate([conv_taps, conv_bias[None]], 0), "head")
    stage_rows = 3 * WIN
    kvq, pooled = pl.pallas_call(
        functools.partial(project_kernel, heads, n_var, len(pieces), n_head),
        out_shape=(
            jax.ShapeDtypeStruct((tokens, columns), jnp.bfloat16),
            jax.ShapeDtypeStruct((tokens // POOL, width), jnp.bfloat16),
        ),
        in_specs=[whole(pltpu.SMEM)] * 2
        + [whole()] * (1 + n_head)
        + [whole(pl.ANY)] * (2 * len(pieces)),
        out_specs=(whole(), whole()),
        scratch_shapes=[
            pltpu.VMEM((n_head * width, columns), jnp.bfloat16),
            pltpu.VMEM((n_head, tokens + 2 * step, width), jnp.bfloat16),
            pltpu.VMEM((stage_rows, n_head * width), jnp.bfloat16),
            pltpu.VMEM((stage_rows, n_head * width), jnp.bfloat16),
            pltpu.SemaphoreType.DMA((2 * len(pieces), n_head)),
        ],
        compiler_params=pltpu.CompilerParams(vmem_limit_bytes=40 * MIB),
        cost_estimate=pl.CostEstimate(
            flops=2 * (tokens + stage_rows) * n_head * width * columns,
            bytes_accessed=4 * tokens * n_head * width,
            transcendentals=tokens * n_head * width,
        ),
        name="project",
    )(deletions, place, w_proj, *taps, *pieces, *crossed)

    late_pair, _ = lax.optimization_barrier((w_pair, pieces[0]))
    w_mix = jnp.zeros((heads * VD, 2 * C), jnp.float32)
    for s, part in enumerate(shifts(late_pair, "head")):
        from_head = (ours + n_head - s) % n_head
        w_mix += jnp.dot(
            lax.dynamic_slice_in_dim(w_out, from_head * width, width, 1),
            part,
            preferred_element_type=jnp.float32,
        )
    w_mix = w_mix.astype(jnp.bfloat16).reshape(heads, VD, 2 * C)
    w_mix = jnp.pad(w_mix, ((0, 0), (0, VP - VD), (0, 0)))
    table = distance_table(dist_table, mine * pair_rows, ours * pair_rows, pair_rows, pair_rows)

    chunk = min(tokens, CHUNK)

    def attend(order, dtype):
        count = order.shape[0]
        return pl.pallas_call(
            functools.partial(attend_kernel, heads, own),
            out_shape=jax.ShapeDtypeStruct((count, pair_rows, 2 * C), dtype),
            in_specs=[whole(pltpu.SMEM)] + [whole()] * 4,
            out_specs=whole(),
            scratch_shapes=[
                pltpu.VMEM((tokens // chunk, own, chunk), jnp.float32),
                pltpu.VMEM((tokens // chunk, own, chunk), jnp.float32),
                pltpu.VMEM((own, 128), jnp.float32),
                pltpu.VMEM((own, 128), jnp.float32),
                pltpu.VMEM((own, VP), jnp.float32),
            ],
            compiler_params=pltpu.CompilerParams(vmem_limit_bytes=40 * MIB),
            cost_estimate=pl.CostEstimate(
                flops=2 * count * heads * own * tokens * (2 * HD + VP),
                bytes_accessed=2 * tokens * columns,
                transcendentals=count * heads * own * tokens,
            ),
            name="attend",
        )(order.astype(jnp.int32), kvq, pooled, w_mix, w_pair)

    if splits == 1:
        sent = attend((ours + jnp.arange(1, n_head)) % n_head, jnp.bfloat16)
        summed = attend(ours[None], jnp.float32)[0]
        for s in range(1, n_head):
            pairs = [(k, (k + s) % n_head) for k in range(n_head)]
            summed += lax.ppermute(sent[s - 1], "head", pairs).astype(jnp.float32)
        turned = lax.ppermute(
            summed[:, :C].astype(jnp.bfloat16),
            ("ctx", "head"),
            [(i * n_head + h, h * n_head + i) for i in range(n_ctx) for h in range(n_head)],
        )
        row_feats = shifts(turned, "head")
        col_feats = shifts(summed[:, C:].astype(jnp.bfloat16), "ctx")
        order = [(at + n_ctx - s) % n_ctx for at in (ours, mine) for s in range(variants)]
    else:
        blocks_here = n_ctx // splits
        part = attend((mine % splits) * blocks_here + jnp.arange(blocks_here), jnp.bfloat16)
        feats = lax.all_gather(lax.psum(part, "head"), "ctx", axis=0, tiled=False)
        feats = feats.reshape(variants, n_ctx, pair_rows, 2 * C)
        row_feats = lax.dynamic_index_in_dim(feats, mine, 1, keepdims=False)[:, :, :C]
        col_feats = lax.dynamic_index_in_dim(feats, ours, 1, keepdims=False)[:, :, C:]
        row_feats, col_feats = list(row_feats), list(col_feats)
        order = list(range(variants)) * 2

    return pl.pallas_call(
        functools.partial(pair_kernel, variants),
        grid=(pair_rows // ROWS,),
        out_shape=jax.ShapeDtypeStruct((variants, pair_rows, pair_rows, C), jnp.bfloat16),
        in_specs=[
            whole(pltpu.SMEM),
            pl.BlockSpec((SHIFTS, 2 * pair_rows, C), lambda i: (0, 0, 0)),
        ]
        + [pl.BlockSpec((pair_rows, C), lambda i: (0, 0))] * (2 * variants),
        out_specs=pl.BlockSpec((variants, ROWS, pair_rows, C), lambda i: (0, i, 0, 0)),
        scratch_shapes=[pltpu.VMEM((variants, pair_rows, C), jnp.float32)] * 2,
        compiler_params=pltpu.CompilerParams(vmem_limit_bytes=24 * MIB),
        name="pair_map",
    )(jnp.stack(order).astype(jnp.int32) if splits == 1 else jnp.array(order, jnp.int32),
      table, *row_feats, *col_feats)


def solution(mesh):
    in_specs = (
        P("ctx", "head"),
        P("var", None),
        P(None, "head"),
        P("head"),
        P(None, "head"),
        P("head", None),
        P("head", None),
        P(),
    )
    out_specs = P("var", "ctx", "head", None)
    return jax.shard_map(local, mesh=mesh, in_specs=in_specs, out_specs=out_specs, check_vma=False)
```

```python
import functools
import math

import jax
import jax.numpy as jnp
from jax import lax
from jax.experimental import pallas as pl
from jax.experimental.pallas import tpu as pltpu
from jax.sharding import PartitionSpec as P

HD = 128
VD = 192
VP = 256
C = 128
NB = 16
POOL = 4
WIN = 160
ALIGN = 32
CHUNK = 512
SHIFTS = 8
ROWS = 16
MIB = 1024 * 1024
QSCALE = math.log2(math.e) / math.sqrt(HD)
GELU_A = math.sqrt(2.0 / math.pi)
GELU_B = GELU_A * 0.044715


def trunk_of(taps, low, middle, high):
    convolved = taps[0:1] * low + taps[1:2] * middle + taps[2:3] * high + taps[3:4]
    half = 0.5 * convolved
    bent = jnp.tanh(convolved * (GELU_A + GELU_B * (convolved * convolved)))
    return middle + (half + half * bent)


def pool_matrix(count):
    wide = lax.broadcasted_iota(jnp.int32, (count // POOL, count), 1) // POOL
    tall = lax.broadcasted_iota(jnp.int32, (count // POOL, count), 0)
    return jnp.where(wide == tall, 1.0 / POOL, 0.0).astype(jnp.bfloat16)


def project_kernel(
    heads, n_var, n_head, count, tiles, finish, dels, place, chosen, w_proj, *refs
):
    taps = refs[:n_head]
    pieces = refs[n_head : n_head + 2 * count]
    rest = refs[n_head + 2 * count :]
    done_kvq, done_pooled = (rest[0], rest[1]) if finish == 2 else (None, None)
    out, pooled_out, weights, rows, left, right, sems, done_sems = rest[2 if finish == 2 else 0 :]
    step, width = pieces[0].shape[1:]
    tokens = rows.shape[1] - 2 * step
    size = step // POOL
    ours, core, variant = place[0], place[1], place[2]

    copies = []
    corners = count == 5
    for index in range(2 * count):
        which = index % count
        half = core if index < count else 1 - core
        at = pl.multiple_of((place[3 + which] * n_var + half + 1) * step, step)
        for s in range(n_head):
            if corners and which >= 3:
                copy = pltpu.make_async_copy(
                    pieces[index].at[s], rows.at[s, pl.ds(at, step)], sems.at[index - which + 3, s]
                )
                pl.when(half == which - 3)(copy.start)
                if which == 3:
                    copies.append(copy)
                continue
            copy = pltpu.make_async_copy(
                pieces[index].at[s], rows.at[s, pl.ds(at, step)], sems.at[index, s]
            )
            copy.start()
            copies.append(copy)
    if finish == 2:
        others = done_kvq.shape[0] // step
        done_copies = []
        for index in range(others):
            at = pl.multiple_of(chosen[tiles + index] * step, step)
            copy = pltpu.make_async_copy(
                done_kvq.at[pl.ds(index * step, step)], out.at[pl.ds(at, step)], done_sems.at[index]
            )
            copy.start()
            done_copies.append(copy)
            small = pl.multiple_of(chosen[tiles + index] * size, size)
            pooled_out[pl.ds(small, size)] = done_pooled[index * size : (index + 1) * size]
    rows[:, 0:step] = jnp.zeros((n_head, step, width), jnp.bfloat16)
    rows[:, tokens + step :] = jnp.zeros((n_head, step, width), jnp.bfloat16)
    columns = weights.shape[1]
    for s in range(n_head):
        source = pl.ds(pl.multiple_of(lax.rem(ours + n_head - s, n_head) * width, ALIGN), width)
        into = slice(s * width, (s + 1) * width)
        for h in range(heads):
            low, key, value = h * (2 * HD + VD), h * HD, heads * HD + h * VP
            query = heads * (HD + VP) + h * HD
            weights[into, key : key + HD] = w_proj[source, low + HD : low + 2 * HD]
            weights[into, value : value + VD] = w_proj[source, low + 2 * HD : low + 2 * HD + VD]
            weights[into, value + VD : value + VP] = jnp.zeros((width, VP - VD), jnp.bfloat16)
            weights[into, query : query + HD] = w_proj[source, low : low + HD]
    at = lax.broadcasted_iota(jnp.int32, (1, columns), 1)
    ones = jnp.zeros((1, columns), jnp.float32)
    scale = jnp.where(at >= heads * (HD + VP), QSCALE, 1.0)
    for h in range(heads):
        ones = jnp.where(at == heads * HD + h * VP + VD, 1.0, ones)
    low_taps = [tap[...].astype(jnp.bfloat16) for tap in taps]
    for copy in copies:
        copy.wait()

    def make(stage, into):
        for part in range(2):
            start = chosen[stage * 2 + part] * step
            for s in range(n_head):
                into[part * step : (part + 1) * step, s * width : (s + 1) * width] = trunk_of(
                    low_taps[s],
                    *(
                        rows[s, pl.ds(pl.multiple_of(start + shift, step), step), :]
                        for shift in (0, step, 2 * step)
                    ),
                )

    def product_of(block):
        product = jnp.dot(block, weights[...], preferred_element_type=jnp.float32)
        return (product * scale + ones).astype(jnp.bfloat16)

    def project(stage, block):
        product = product_of(block[...])
        for part in range(2):
            at = chosen[stage * 2 + part] if finish else stage * 2 + part
            rows_here = slice(part * step, (part + 1) * step)
            out[pl.ds(pl.multiple_of(at * step, step), step)] = product[rows_here]
            pooled_out[pl.ds(pl.multiple_of(at * size, size), size)] = jnp.dot(
                pool_matrix(step), block[rows_here, 0:width], preferred_element_type=jnp.float32
            )

    first, last = dels[variant, 0], dels[variant, 1]

    def window(index):
        start = (first // ALIGN) * ALIGN + (index - 1) * step
        return pl.multiple_of(jnp.clip(start, 0, tokens - WIN), ALIGN)

    def make_windows(into):
        for index in range(3):
            start = window(index)
            at = start + lax.broadcasted_iota(jnp.int32, (WIN, 1), 0)
            kept = [
                jnp.where(
                    jnp.logical_or(at + shift < first, at + shift >= last), 1.0, 0.0
                ).astype(jnp.bfloat16)
                for shift in (-step, 0, step)
            ]
            for s in range(n_head):
                into[index * WIN : (index + 1) * WIN, s * width : (s + 1) * width] = trunk_of(
                    low_taps[s],
                    *(
                        rows[s, pl.ds(pl.multiple_of(start + shift, ALIGN), WIN), :] * keep
                        for shift, keep in zip((0, step, 2 * step), kept)
                    ),
                )

    stages = tiles // 2
    make(0, left)

    def two_stages(n, carry):
        make(2 * n + 1, right)
        project(2 * n, left)
        make(2 * n + 2, left)
        project(2 * n + 1, right)
        return carry

    if stages > 2:
        lax.fori_loop(0, stages // 2 - 1, two_stages, 0)
    make(stages - 1, right)
    project(stages - 2, left)
    if finish:
        make_windows(left)
    project(stages - 1, right)
    if finish:
        product = product_of(left[0 : 3 * WIN])
        if finish == 2:
            for copy in done_copies:
                copy.wait()
        for index in range(3):
            rows_here = slice(index * WIN, (index + 1) * WIN)
            out[pl.ds(window(index), WIN)] = product[rows_here]
            small = pl.multiple_of(window(index) // POOL, ALIGN // POOL)
            pooled_out[pl.ds(small, WIN // POOL)] = jnp.dot(
                pool_matrix(WIN), left[rows_here, 0:width], preferred_element_type=jnp.float32
            )


def attend_kernel(
    heads, own, order, kvq, pooled, w_mix, w_pair,
    out, scores_a, scores_b, top_a, top_b, total,
):
    tokens = kvq.shape[0]
    chunk = scores_a.shape[2]
    steps = tokens // chunk
    key_cols, value_cols = heads * HD, heads * (HD + VP)
    pool = pool_matrix(own)
    scores, tops = (scores_a, scores_b), (top_a, top_b)
    chains = [(n, h) for n in range(out.shape[0]) for h in range(heads)]

    def score(index, c):
        n, h = chains[index]
        low = value_cols + h * HD
        found = lax.dot_general(
            kvq[pl.ds(pl.multiple_of(order[n] * own, own), own), low : low + HD],
            kvq[pl.ds(pl.multiple_of(c * chunk, chunk), chunk), h * HD : (h + 1) * HD],
            (((1,), (1,)), ((), ())),
            preferred_element_type=jnp.float32,
        )
        scores[index % 2][c] = found
        best = found[:, 0:128]
        for low in range(128, chunk, 128):
            best = jnp.maximum(best, found[:, low : low + 128])
        top = tops[index % 2]
        top[...] = jnp.maximum(top[...], best)

    def clear(index):
        tops[index % 2][...] = jnp.full(top_a.shape, -jnp.inf, jnp.float32)

    clear(0)

    def first_scores(c, carry):
        score(0, c)
        return carry

    lax.fori_loop(0, steps, first_scores, 0)
    for index, (n, h) in enumerate(chains):
        more = index + 1 < len(chains)
        if more:
            clear(index + 1)
        row_max = jnp.max(tops[index % 2][...], axis=1, keepdims=True)
        total[...] = jnp.zeros(total.shape, jnp.float32)
        low = key_cols + h * VP

        def weigh(c, carry):
            weights = jnp.exp2((scores[index % 2][c] - row_max).astype(jnp.bfloat16))
            if more:
                score(index + 1, c)
            total[...] += jnp.dot(
                weights,
                kvq[pl.ds(pl.multiple_of(c * chunk, chunk), chunk), low : low + VP],
                preferred_element_type=jnp.float32,
            )
            return carry

        lax.fori_loop(0, steps, weigh, 0)
        mixed = total[...]
        mixed = (mixed * (1.0 / mixed[:, VD : VD + 1])).astype(jnp.bfloat16)
        mixed = jnp.dot(pool, mixed, preferred_element_type=jnp.float32).astype(jnp.bfloat16)
        if h == 0:
            size = own // POOL
            pair = jnp.dot(
                pooled[pl.ds(pl.multiple_of(order[n] * size, size), size)].astype(jnp.bfloat16),
                w_pair[...],
                preferred_element_type=jnp.float32,
            )
        pair = pair + jnp.dot(mixed, w_mix[h], preferred_element_type=jnp.float32)
        if h == heads - 1:
            out[n] = pair.astype(out.dtype)


def pair_kernel(variants, order, table, *refs):
    row_feats = refs[:variants]
    col_feats = refs[variants : 2 * variants]
    out, rows, cols = refs[2 * variants :]
    block = pl.program_id(0)
    side = cols.shape[1]

    @pl.when(block == 0)
    def _():
        for s in range(variants):
            rows[order[s]] = row_feats[s][...].astype(jnp.float32)
            cols[order[variants + s]] = col_feats[s][...].astype(jnp.float32)

    count = table.shape[1] - side
    for r in range(ROWS):
        back = count - 1 - (block * ROWS + r)
        low = pl.multiple_of((back // SHIFTS) * SHIFTS, SHIFTS)
        relative = table[(count - 1 - r) % SHIFTS, pl.ds(low, side), :]
        for variant in range(variants):
            row = rows[variant, pl.ds(block * ROWS + r, 1), :]
            out[variant, r] = (row + (cols[variant] + relative)).astype(jnp.bfloat16)


def distance_table(dist_table, row_start, col_start, rows, cols):
    at = jnp.arange(SHIFTS, dtype=jnp.int32)[:, None] + jnp.arange(
        rows + cols, dtype=jnp.int32
    )
    distance = jnp.abs(row_start - col_start + rows - 1 - at)
    buckets = jnp.zeros(distance.shape, jnp.int32)
    for power_index in range(NB - 1):
        buckets = buckets + (distance >= 2**power_index).astype(jnp.int32)
    one_hot = (buckets[:, :, None] == jnp.arange(NB, dtype=jnp.int32)).astype(jnp.float32)
    return jnp.einsum("skb,bc->skc", one_hot, dist_table, precision=lax.Precision.HIGHEST)


def whole(memory=pltpu.VMEM):
    return pl.BlockSpec(memory_space=memory)


def shifts(array, axis):
    size = lax.axis_size(axis)
    return [array] + [
        lax.ppermute(array, axis, [(k, (k + s) % size) for k in range(size)])
        for s in range(1, size)
    ]


def gather_rows(block, taps, n_ctx, n_var, mine):
    slab = jnp.stack(shifts(block, "head"))
    slab, taps = lax.optimization_barrier((slab, shifts(taps, "head")))
    if n_ctx == 4 and n_var == 2:
        over_x = lax.ppermute(slab, "ctx", [(k, k ^ 1) for k in range(4)])
        over_y = lax.ppermute(slab, "ctx", [(k, k ^ 2) for k in range(4)])
        both = ("ctx", "var")
        corner_x = lax.ppermute(over_y, both, [(2 * k, 2 * (k ^ 1)) for k in range(4)])
        corner_y = lax.ppermute(over_x, both, [(2 * k + 1, 2 * (k ^ 2) + 1) for k in range(4)])
        pieces = [slab, over_x, over_y]
        crossed = [lax.ppermute(piece, "var", [(0, 1), (1, 0)]) for piece in pieces]
        pieces += [corner_x, corner_y]
        return pieces, crossed, [mine, mine ^ 1, mine ^ 2, mine ^ 3, mine ^ 3], taps
    pieces = shifts(slab, "ctx")
    crossed = [lax.ppermute(piece, "var", [(0, 1), (1, 0)]) for piece in pieces]
    return pieces, crossed, [(mine + n_ctx - s) % n_ctx for s in range(n_ctx)], taps


def local(sequence, deletions, conv_taps, conv_bias, w_proj, w_out, w_pair, dist_table):
    own, width = sequence.shape
    variants = deletions.shape[0]
    heads = w_out.shape[0] // VD
    n_ctx, n_head, n_var = (lax.axis_size(name) for name in ("ctx", "head", "var"))
    if n_ctx != n_head or n_var != 2 or n_ctx % variants:
        raise ValueError("mesh shape")
    step = own // n_var
    tokens = n_ctx * own
    pair_rows = own // POOL
    columns = heads * (2 * HD + VP)
    splits = n_ctx // variants
    mine, ours, core = (lax.axis_index(name) for name in ("ctx", "head", "var"))

    half = lax.dynamic_slice_in_dim(sequence, core * step, step, 0)
    taps = jnp.concatenate([conv_taps, conv_bias[None]], 0)
    pieces, crossed, blocks, taps = gather_rows(half, taps, n_ctx, n_var, mine)
    place = jnp.stack([ours, core, mine // splits] + blocks).astype(jnp.int32)
    all_tiles = n_ctx * n_var

    def project(count, tiles, finish, chosen, done):
        out_tiles = all_tiles if finish else tiles
        return pl.pallas_call(
            functools.partial(project_kernel, heads, n_var, n_head, count, tiles, finish),
            out_shape=(
                jax.ShapeDtypeStruct((out_tiles * step, columns), jnp.bfloat16),
                jax.ShapeDtypeStruct((out_tiles * step // POOL, width), jnp.float32),
            ),
            in_specs=[whole(pltpu.SMEM)] * 3
            + [whole()] * (1 + n_head)
            + [whole(pl.ANY)] * (2 * count)
            + ([whole(pl.ANY), whole()] if done else []),
            out_specs=(whole(), whole()),
            scratch_shapes=[
                pltpu.VMEM((n_head * width, columns), jnp.bfloat16),
                pltpu.VMEM((n_head, tokens + 2 * step, width), jnp.bfloat16),
                pltpu.VMEM((2 * step, n_head * width), jnp.bfloat16),
                pltpu.VMEM((2 * step, n_head * width), jnp.bfloat16),
                pltpu.SemaphoreType.DMA((2 * count, n_head)),
                pltpu.SemaphoreType.DMA((all_tiles,)),
            ],
            compiler_params=pltpu.CompilerParams(vmem_limit_bytes=40 * MIB),
            cost_estimate=pl.CostEstimate(
                flops=4 * tiles * step * n_head * width * columns,
                bytes_accessed=4 * tokens * n_head * width,
                transcendentals=tiles * step * n_head * width,
            ),
            name="project",
        )(
            deletions, place, chosen, w_proj, *taps,
            *pieces[:count], *crossed[:count], *(done or ()),
        )

    if len(pieces) == 5:
        early = jnp.array([[0, 1, 2, 3], [0, 1, 2, 7], [0, 5, 6, 7], [4, 5, 6, 7]], jnp.int32)[mine]
        late = jnp.array([[4, 5, 6, 7], [3, 4, 5, 6], [1, 2, 3, 4], [0, 1, 2, 3]], jnp.int32)[mine]
        done = project(3, 4, 0, early, None)
        (corner_x, corner_y), done = lax.optimization_barrier((pieces[3:], done))
        pieces = pieces[:3] + [corner_x, corner_y]
        crossed = crossed + [
            lax.ppermute(corner_x, "var", [(0, 1)]),
            lax.ppermute(corner_y, "var", [(1, 0)]),
        ]
        kvq, pooled = project(5, 4, 2, jnp.concatenate([late, early]), done)
    else:
        chosen = jnp.arange(all_tiles, dtype=jnp.int32)
        kvq, pooled = project(len(pieces), all_tiles, 1, chosen, None)

    late_pair, _ = lax.optimization_barrier((w_pair, crossed[1]))
    w_mix = jnp.zeros((heads * VD, 2 * C), jnp.float32)
    pair_parts, _ = lax.optimization_barrier((shifts(late_pair, "head"), pooled))
    for s, part in enumerate(pair_parts):
        from_head = (ours + n_head - s) % n_head
        w_mix += jnp.dot(
            lax.dynamic_slice_in_dim(w_out, from_head * width, width, 1),
            part,
            preferred_element_type=jnp.float32,
        )
    w_mix = w_mix.astype(jnp.bfloat16).reshape(heads, VD, 2 * C)
    w_mix = jnp.pad(w_mix, ((0, 0), (0, VP - VD), (0, 0)))
    table = distance_table(dist_table, mine * pair_rows, ours * pair_rows, pair_rows, pair_rows)

    chunk = min(tokens, CHUNK)

    def attend(order, dtype):
        count = order.shape[0]
        return pl.pallas_call(
            functools.partial(attend_kernel, heads, own),
            out_shape=jax.ShapeDtypeStruct((count, pair_rows, 2 * C), dtype),
            in_specs=[whole(pltpu.SMEM)] + [whole()] * 4,
            out_specs=whole(),
            scratch_shapes=[
                pltpu.VMEM((tokens // chunk, own, chunk), jnp.float32),
                pltpu.VMEM((tokens // chunk, own, chunk), jnp.float32),
                pltpu.VMEM((own, 128), jnp.float32),
                pltpu.VMEM((own, 128), jnp.float32),
                pltpu.VMEM((own, VP), jnp.float32),
            ],
            compiler_params=pltpu.CompilerParams(vmem_limit_bytes=40 * MIB),
            cost_estimate=pl.CostEstimate(
                flops=2 * count * heads * own * tokens * (2 * HD + VP),
                bytes_accessed=2 * tokens * columns,
                transcendentals=count * heads * own * tokens,
            ),
            name="attend",
        )(order.astype(jnp.int32), kvq, pooled, w_mix, w_pair)

    if splits == 1:
        sent = attend((ours + jnp.arange(1, n_head)) % n_head, jnp.bfloat16)
        summed = attend(ours[None], jnp.float32)[0]
        for s in range(1, n_head):
            pairs = [(k, (k + s) % n_head) for k in range(n_head)]
            summed += lax.ppermute(sent[s - 1], "head", pairs).astype(jnp.float32)
        turned = lax.ppermute(
            summed[:, :C].astype(jnp.bfloat16),
            ("ctx", "head"),
            [(i * n_head + h, h * n_head + i) for i in range(n_ctx) for h in range(n_head)],
        )
        row_feats = shifts(turned, "head")
        col_feats = shifts(summed[:, C:].astype(jnp.bfloat16), "ctx")
        order = [(at + n_ctx - s) % n_ctx for at in (ours, mine) for s in range(variants)]
    else:
        blocks_here = n_ctx // splits
        part = attend((mine % splits) * blocks_here + jnp.arange(blocks_here), jnp.bfloat16)
        feats = lax.all_gather(lax.psum(part, "head"), "ctx", axis=0, tiled=False)
        feats = feats.reshape(variants, n_ctx, pair_rows, 2 * C)
        row_feats = lax.dynamic_index_in_dim(feats, mine, 1, keepdims=False)[:, :, :C]
        col_feats = lax.dynamic_index_in_dim(feats, ours, 1, keepdims=False)[:, :, C:]
        row_feats, col_feats = list(row_feats), list(col_feats)
        order = list(range(variants)) * 2

    return pl.pallas_call(
        functools.partial(pair_kernel, variants),
        grid=(pair_rows // ROWS,),
        out_shape=jax.ShapeDtypeStruct((variants, pair_rows, pair_rows, C), jnp.bfloat16),
        in_specs=[
            whole(pltpu.SMEM),
            pl.BlockSpec((SHIFTS, 2 * pair_rows, C), lambda i: (0, 0, 0)),
        ]
        + [pl.BlockSpec((pair_rows, C), lambda i: (0, 0))] * (2 * variants),
        out_specs=pl.BlockSpec((variants, ROWS, pair_rows, C), lambda i: (0, i, 0, 0)),
        scratch_shapes=[pltpu.VMEM((variants, pair_rows, C), jnp.float32)] * 2,
        compiler_params=pltpu.CompilerParams(vmem_limit_bytes=24 * MIB),
        name="pair_map",
    )(jnp.stack(order).astype(jnp.int32) if splits == 1 else jnp.array(order, jnp.int32),
      table, *row_feats, *col_feats)


def solution(mesh):
    in_specs = (
        P("ctx", "head"),
        P("var", None),
        P(None, "head"),
        P("head"),
        P(None, "head"),
        P("head", None),
        P("head", None),
        P(),
    )
    out_specs = P("var", "ctx", "head", None)
    return jax.shard_map(local, mesh=mesh, in_specs=in_specs, out_specs=out_specs, check_vma=False)
```

```python
import functools
import math

import jax
import jax.numpy as jnp
from jax import lax
from jax.experimental import pallas as pl
from jax.experimental.pallas import tpu as pltpu
from jax.sharding import PartitionSpec as P

HD = 128
VD = 192
VP = 256
C = 128
NB = 16
POOL = 4
WIN = 160
ALIGN = 32
CHUNK = 512
SHIFTS = 16
ROWS = 16
MIB = 1024 * 1024
QSCALE = math.log2(math.e) / math.sqrt(HD)
GELU_A = math.sqrt(2.0 / math.pi)
GELU_B = GELU_A * 0.044715


def trunk_of(taps, low, middle, high):
    convolved = taps[0:1] * low + taps[1:2] * middle + taps[2:3] * high + taps[3:4]
    half = 0.5 * convolved
    bent = jnp.tanh(convolved * (GELU_A + GELU_B * (convolved * convolved)))
    return middle + (half + half * bent)


def pool_matrix(count):
    wide = lax.broadcasted_iota(jnp.int32, (count // POOL, count), 1) // POOL
    tall = lax.broadcasted_iota(jnp.int32, (count // POOL, count), 0)
    return jnp.where(wide == tall, 1.0 / POOL, 0.0).astype(jnp.bfloat16)


def project_kernel(
    heads, n_var, n_head, count, tiles, finish, dels, place, chosen, w_proj, *refs
):
    taps = refs[:n_head]
    pieces = refs[n_head : n_head + 2 * count]
    rest = refs[n_head + 2 * count :]
    done_kvq, done_pooled = (rest[0], rest[1]) if finish == 2 else (None, None)
    out, pooled_out, given, weights, rows, left, right, sems, done_sems = rest[
        2 if finish == 2 else 0 :
    ]
    step, width = pieces[0].shape[1:]
    tokens = rows.shape[1] - 2 * step
    size = step // POOL
    ours, core, variant = place[0], place[1], place[2]

    given_copy = pltpu.make_async_copy(w_proj, given, done_sems.at[done_sems.shape[0] - 1])
    given_copy.start()
    copies = []
    corners = count == 5
    for index in range(2 * count):
        which = index % count
        half = core if index < count else 1 - core
        at = pl.multiple_of((place[3 + which] * n_var + half + 1) * step, step)
        for s in range(n_head):
            if corners and which >= 3:
                copy = pltpu.make_async_copy(
                    pieces[index].at[s], rows.at[s, pl.ds(at, step)], sems.at[index - which + 3, s]
                )
                pl.when(half == which - 3)(copy.start)
                if which == 3:
                    copies.append(copy)
                continue
            copy = pltpu.make_async_copy(
                pieces[index].at[s], rows.at[s, pl.ds(at, step)], sems.at[index, s]
            )
            copy.start()
            copies.append(copy)
    if finish == 2:
        others = done_kvq.shape[0] // step
        done_copies = []
        for index in range(others):
            at = pl.multiple_of(chosen[tiles + index] * step, step)
            copy = pltpu.make_async_copy(
                done_kvq.at[pl.ds(index * step, step)], out.at[pl.ds(at, step)], done_sems.at[index]
            )
            copy.start()
            done_copies.append(copy)
            small = pl.multiple_of(chosen[tiles + index] * size, size)
            pooled_out[pl.ds(small, size)] = done_pooled[index * size : (index + 1) * size]
    rows[:, 0:step] = jnp.zeros((n_head, step, width), jnp.bfloat16)
    rows[:, tokens + step :] = jnp.zeros((n_head, step, width), jnp.bfloat16)
    columns = weights.shape[1]
    given_copy.wait()
    for s, back in enumerate(head_order(n_head)):
        source = pl.ds(pl.multiple_of(lax.rem(ours + n_head - back, n_head) * width, ALIGN), width)
        into = slice(s * width, (s + 1) * width)
        for h in range(heads):
            low, key, value = h * (2 * HD + VD), h * HD, heads * HD + h * VP
            query = heads * (HD + VP) + h * HD
            weights[into, key : key + HD] = given[source, low + HD : low + 2 * HD]
            weights[into, value : value + VD] = given[source, low + 2 * HD : low + 2 * HD + VD]
            weights[into, value + VD : value + VP] = jnp.zeros((width, VP - VD), jnp.bfloat16)
            weights[into, query : query + HD] = given[source, low : low + HD]
    at = lax.broadcasted_iota(jnp.int32, (1, columns), 1)
    ones = jnp.zeros((1, columns), jnp.float32)
    scale = jnp.where(at >= heads * (HD + VP), QSCALE, 1.0)
    for h in range(heads):
        ones = jnp.where(at == heads * HD + h * VP + VD, 1.0, ones)
    low_taps = [tap[...].astype(jnp.bfloat16) for tap in taps]
    for copy in copies:
        copy.wait()

    def make(stage, into):
        for part in range(2):
            start = chosen[stage * 2 + part] * step
            for s in range(n_head):
                into[part * step : (part + 1) * step, s * width : (s + 1) * width] = trunk_of(
                    low_taps[s],
                    *(
                        rows[s, pl.ds(pl.multiple_of(start + shift, step), step), :]
                        for shift in (0, step, 2 * step)
                    ),
                )

    def product_of(block):
        product = jnp.dot(block, weights[...], preferred_element_type=jnp.float32)
        return (product * scale + ones).astype(jnp.bfloat16)

    def project(stage, block):
        product = product_of(block[...])
        for part in range(2):
            at = chosen[stage * 2 + part] if finish else stage * 2 + part
            rows_here = slice(part * step, (part + 1) * step)
            out[pl.ds(pl.multiple_of(at * step, step), step)] = product[rows_here]
            pooled_out[pl.ds(pl.multiple_of(at * size, size), size)] = jnp.dot(
                pool_matrix(step), block[rows_here, 0:width], preferred_element_type=jnp.float32
            )

    first, last = dels[variant, 0], dels[variant, 1]

    def window(index):
        start = (first // ALIGN) * ALIGN + (index - 1) * step
        return pl.multiple_of(jnp.clip(start, 0, tokens - WIN), ALIGN)

    def make_windows(into):
        for index in range(3):
            start = window(index)
            at = start + lax.broadcasted_iota(jnp.int32, (WIN, 1), 0)
            kept = [
                jnp.where(
                    jnp.logical_or(at + shift < first, at + shift >= last), 1.0, 0.0
                ).astype(jnp.bfloat16)
                for shift in (-step, 0, step)
            ]
            for s in range(n_head):
                into[index * WIN : (index + 1) * WIN, s * width : (s + 1) * width] = trunk_of(
                    low_taps[s],
                    *(
                        rows[s, pl.ds(pl.multiple_of(start + shift, ALIGN), WIN), :] * keep
                        for shift, keep in zip((0, step, 2 * step), kept)
                    ),
                )

    stages = tiles // 2
    make(0, left)

    def two_stages(n, carry):
        make(2 * n + 1, right)
        project(2 * n, left)
        make(2 * n + 2, left)
        project(2 * n + 1, right)
        return carry

    if stages > 2:
        lax.fori_loop(0, stages // 2 - 1, two_stages, 0)
    make(stages - 1, right)
    project(stages - 2, left)
    if finish:
        make_windows(left)
    project(stages - 1, right)
    if finish:
        product = product_of(left[0 : 3 * WIN])
        if finish == 2:
            for copy in done_copies:
                copy.wait()
        for index in range(3):
            rows_here = slice(index * WIN, (index + 1) * WIN)
            out[pl.ds(window(index), WIN)] = product[rows_here]
            small = pl.multiple_of(window(index) // POOL, ALIGN // POOL)
            pooled_out[pl.ds(small, WIN // POOL)] = jnp.dot(
                pool_matrix(WIN), left[rows_here, 0:width], preferred_element_type=jnp.float32
            )


def attend_kernel(
    heads, own, order, kvq, pooled, w_mix, w_pair,
    out, scores_a, scores_b, top_a, top_b, total,
):
    tokens = kvq.shape[0]
    chunk = scores_a.shape[2]
    steps = tokens // chunk
    key_cols, value_cols = heads * HD, heads * (HD + VP)
    pool = pool_matrix(own)
    scores, tops = (scores_a, scores_b), (top_a, top_b)
    chains = [(n, h) for n in range(out.shape[0]) for h in range(heads)]

    def score(index, c):
        n, h = chains[index]
        low = value_cols + h * HD
        found = lax.dot_general(
            kvq[pl.ds(pl.multiple_of(order[n] * own, own), own), low : low + HD],
            kvq[pl.ds(pl.multiple_of(c * chunk, chunk), chunk), h * HD : (h + 1) * HD],
            (((1,), (1,)), ((), ())),
            preferred_element_type=jnp.float32,
        )
        scores[index % 2][c] = found
        best = found[:, 0:128]
        for low in range(128, chunk, 128):
            best = jnp.maximum(best, found[:, low : low + 128])
        top = tops[index % 2]
        top[...] = jnp.maximum(top[...], best)

    def clear(index):
        tops[index % 2][...] = jnp.full(top_a.shape, -jnp.inf, jnp.float32)

    clear(0)

    def first_scores(c, carry):
        score(0, c)
        return carry

    lax.fori_loop(0, steps, first_scores, 0)
    for index, (n, h) in enumerate(chains):
        more = index + 1 < len(chains)
        if more:
            clear(index + 1)
        row_max = jnp.max(tops[index % 2][...], axis=1, keepdims=True)
        total[...] = jnp.zeros(total.shape, jnp.float32)
        low = key_cols + h * VP

        def weigh(c, carry):
            weights = jnp.exp2((scores[index % 2][c] - row_max).astype(jnp.bfloat16))
            if more:
                score(index + 1, c)
            total[...] += jnp.dot(
                weights,
                kvq[pl.ds(pl.multiple_of(c * chunk, chunk), chunk), low : low + VP],
                preferred_element_type=jnp.float32,
            )
            return carry

        lax.fori_loop(0, steps, weigh, 0)
        mixed = total[...]
        mixed = (mixed * (1.0 / mixed[:, VD : VD + 1])).astype(jnp.bfloat16)
        mixed = jnp.dot(pool, mixed, preferred_element_type=jnp.float32).astype(jnp.bfloat16)
        if h == 0:
            size = own // POOL
            pair = jnp.dot(
                pooled[pl.ds(pl.multiple_of(order[n] * size, size), size)].astype(jnp.bfloat16),
                w_pair[...],
                preferred_element_type=jnp.float32,
            )
        pair = pair + jnp.dot(mixed, w_mix[h], preferred_element_type=jnp.float32)
        if h == heads - 1:
            out[n] = pair.astype(out.dtype)


def pair_kernel(variants, order, table, *refs):
    row_feats = refs[:variants]
    col_feats = refs[variants : 2 * variants]
    out, rows, cols = refs[2 * variants :]
    block = pl.program_id(0)
    side = cols.shape[1]

    @pl.when(block == 0)
    def _():
        for s in range(variants):
            rows[order[s]] = row_feats[s][...].astype(jnp.float32)
            cols[order[variants + s]] = col_feats[s][...]

    count = table.shape[1] - side
    for r in range(ROWS):
        back = count - 1 - (block * ROWS + r)
        low = pl.multiple_of((back // SHIFTS) * SHIFTS, SHIFTS)
        relative = table[(count - 1 - r) % SHIFTS, pl.ds(low, side), :]
        for variant in range(variants):
            row = rows[variant, pl.ds(block * ROWS + r, 1), :]
            row = jnp.broadcast_to(row, (SHIFTS, C)).astype(jnp.bfloat16)
            found = (cols[variant] + relative).reshape(side // SHIFTS, SHIFTS, C) + row[None]
            out[variant, r] = found.reshape(side, C)


def distance_table(dist_table, row_start, col_start, rows, cols):
    at = jnp.arange(SHIFTS, dtype=jnp.int32)[:, None] + jnp.arange(
        rows + cols, dtype=jnp.int32
    )
    distance = jnp.abs(row_start - col_start + rows - 1 - at)
    buckets = jnp.zeros(distance.shape, jnp.int32)
    for power_index in range(NB - 1):
        buckets = buckets + (distance >= 2**power_index).astype(jnp.int32)
    one_hot = (buckets[:, :, None] == jnp.arange(NB, dtype=jnp.int32)).astype(jnp.float32)
    return jnp.einsum("skb,bc->skc", one_hot, dist_table, precision=lax.Precision.HIGHEST).astype(
        jnp.bfloat16
    )


def whole(memory=pltpu.VMEM):
    return pl.BlockSpec(memory_space=memory)


def shifts(array, axis):
    size = lax.axis_size(axis)
    return [array] + [
        lax.ppermute(array, axis, [(k, (k + s) % size) for k in range(size)])
        for s in range(1, size)
    ]


def head_order(n_head):
    return [0, 1, 3, 2] if n_head == 4 else list(range(n_head))


def gather_rows(block, taps, n_ctx, n_var, n_head, mine):
    if n_ctx == 4 and n_head == 4 and n_var == 2:
        shift = lambda array, s: lax.ppermute(array, "head", [(k, (k + s) % 4) for k in range(4)])
        over = lambda array, bit: lax.ppermute(array, "ctx", [(k, k ^ bit) for k in range(4)])
        first = shift(block, 1)
        near = jnp.stack([block, first, shift(block, 3)])
        later, _ = lax.optimization_barrier((block, first))
        far = shift(later, 2)[None]
        slab, over_x, over_y = (
            jnp.concatenate(pair)
            for pair in (
                (near, far), (over(near, 1), over(far, 1)), (over(near, 2), over(far, 2))
            )
        )
        taps, over_x, over_y = lax.optimization_barrier((shifts(taps, "head"), over_x, over_y))
        both = ("ctx", "var")
        corner_x = lax.ppermute(over_y, both, [(2 * k, 2 * (k ^ 1)) for k in range(4)])
        corner_y = lax.ppermute(over_x, both, [(2 * k + 1, 2 * (k ^ 2) + 1) for k in range(4)])
        pieces = [slab, over_x, over_y]
        crossed = [lax.ppermute(piece, "var", [(0, 1), (1, 0)]) for piece in pieces]
        pieces += [corner_x, corner_y]
        return pieces, crossed, [mine, mine ^ 1, mine ^ 2, mine ^ 3, mine ^ 3], taps
    pieces = shifts(jnp.stack(shifts(block, "head")), "ctx")
    crossed = [lax.ppermute(piece, "var", [(0, 1), (1, 0)]) for piece in pieces]
    blocks = [(mine + n_ctx - s) % n_ctx for s in range(n_ctx)]
    return pieces, crossed, blocks, shifts(taps, "head")


def local(sequence, deletions, conv_taps, conv_bias, w_proj, w_out, w_pair, dist_table):
    own, width = sequence.shape
    variants = deletions.shape[0]
    heads = w_out.shape[0] // VD
    n_ctx, n_head, n_var = (lax.axis_size(name) for name in ("ctx", "head", "var"))
    if n_ctx != n_head or n_var != 2 or n_ctx % variants:
        raise ValueError("mesh shape")
    step = own // n_var
    tokens = n_ctx * own
    pair_rows = own // POOL
    columns = heads * (2 * HD + VP)
    splits = n_ctx // variants
    mine, ours, core = (lax.axis_index(name) for name in ("ctx", "head", "var"))

    half = lax.dynamic_slice_in_dim(sequence, core * step, step, 0)
    taps = jnp.concatenate([conv_taps, conv_bias[None]], 0)
    pieces, crossed, blocks, taps = gather_rows(half, taps, n_ctx, n_var, n_head, mine)
    taps = [taps[s] for s in head_order(n_head)]
    place = jnp.stack([ours, core, mine // splits] + blocks).astype(jnp.int32)
    all_tiles = n_ctx * n_var
    project_vmem = (34 if splits == 1 else 52) * MIB

    def project(count, tiles, finish, chosen, done):
        out_tiles = all_tiles if finish else tiles
        return pl.pallas_call(
            functools.partial(project_kernel, heads, n_var, n_head, count, tiles, finish),
            out_shape=(
                jax.ShapeDtypeStruct((out_tiles * step, columns), jnp.bfloat16),
                jax.ShapeDtypeStruct((out_tiles * step // POOL, width), jnp.float32),
            ),
            in_specs=[whole(pltpu.SMEM)] * 3
            + [whole(pl.ANY)]
            + [whole()] * n_head
            + [whole(pl.ANY)] * (2 * count)
            + ([whole(pl.ANY), whole()] if done else []),
            out_specs=(whole(), whole()),
            scratch_shapes=[
                pltpu.VMEM(w_proj.shape, jnp.bfloat16),
                pltpu.VMEM((n_head * width, columns), jnp.bfloat16),
                pltpu.VMEM((n_head, tokens + 2 * step, width), jnp.bfloat16),
                pltpu.VMEM((2 * step, n_head * width), jnp.bfloat16),
                pltpu.VMEM((2 * step, n_head * width), jnp.bfloat16),
                pltpu.SemaphoreType.DMA((2 * count, n_head)),
                pltpu.SemaphoreType.DMA((all_tiles + 1,)),
            ],
            compiler_params=pltpu.CompilerParams(vmem_limit_bytes=project_vmem),
            cost_estimate=pl.CostEstimate(
                flops=4 * tiles * step * n_head * width * columns,
                bytes_accessed=4 * tokens * n_head * width,
                transcendentals=tiles * step * n_head * width,
            ),
            name="project",
        )(
            deletions, place, chosen, w_proj, *taps,
            *pieces[:count], *crossed[:count], *(done or ()),
        )

    if len(pieces) == 5:
        early = jnp.array([[0, 1, 2, 3], [0, 1, 2, 7], [0, 5, 6, 7], [4, 5, 6, 7]], jnp.int32)[mine]
        late = jnp.array([[4, 5, 6, 7], [3, 4, 5, 6], [1, 2, 3, 4], [0, 1, 2, 3]], jnp.int32)[mine]
        done = project(3, 4, 0, early, None)
        late_pair, _ = lax.optimization_barrier((w_pair, pieces[0]))
        (corner_x, corner_y), done, pair_parts = lax.optimization_barrier(
            (pieces[3:], done, shifts(late_pair, "head"))
        )
        pieces = pieces[:3] + [corner_x, corner_y]
        crossed = crossed + [
            lax.ppermute(corner_x, "var", [(0, 1)]),
            lax.ppermute(corner_y, "var", [(1, 0)]),
        ]
        kvq, pooled = project(5, 4, 2, jnp.concatenate([late, early]), done)
    else:
        chosen = jnp.arange(all_tiles, dtype=jnp.int32)
        kvq, pooled = project(len(pieces), all_tiles, 1, chosen, None)
        pair_parts = shifts(w_pair, "head")

    w_mix = jnp.zeros((heads * VD, 2 * C), jnp.float32)
    pair_parts, _ = lax.optimization_barrier((pair_parts, pooled))
    for s, part in enumerate(pair_parts):
        from_head = (ours + n_head - s) % n_head
        w_mix += jnp.dot(
            lax.dynamic_slice_in_dim(w_out, from_head * width, width, 1),
            part,
            preferred_element_type=jnp.float32,
        )
    w_mix = w_mix.astype(jnp.bfloat16).reshape(heads, VD, 2 * C)
    w_mix = jnp.pad(w_mix, ((0, 0), (0, VP - VD), (0, 0)))
    table = distance_table(dist_table, mine * pair_rows, ours * pair_rows, pair_rows, pair_rows)

    chunk = min(tokens, CHUNK)

    def attend(order, dtype):
        count = order.shape[0]
        return pl.pallas_call(
            functools.partial(attend_kernel, heads, own),
            out_shape=jax.ShapeDtypeStruct((count, pair_rows, 2 * C), dtype),
            in_specs=[whole(pltpu.SMEM)] + [whole()] * 4,
            out_specs=whole(),
            scratch_shapes=[
                pltpu.VMEM((tokens // chunk, own, chunk), jnp.float32),
                pltpu.VMEM((tokens // chunk, own, chunk), jnp.float32),
                pltpu.VMEM((own, 128), jnp.float32),
                pltpu.VMEM((own, 128), jnp.float32),
                pltpu.VMEM((own, VP), jnp.float32),
            ],
            compiler_params=pltpu.CompilerParams(vmem_limit_bytes=(20 if splits == 1 else 52) * MIB),
            cost_estimate=pl.CostEstimate(
                flops=2 * count * heads * own * tokens * (2 * HD + VP),
                bytes_accessed=2 * tokens * columns,
                transcendentals=count * heads * own * tokens,
            ),
            name="attend",
        )(order.astype(jnp.int32), kvq, pooled, w_mix, w_pair)

    if splits == 1:
        sent = attend((ours + jnp.arange(1, n_head)) % n_head, jnp.bfloat16)
        last_block, table = lax.optimization_barrier((ours[None], table))
        summed = attend(last_block, jnp.float32)[0]
        for s in range(1, n_head):
            pairs = [(k, (k + s) % n_head) for k in range(n_head)]
            summed += lax.ppermute(sent[s - 1], "head", pairs).astype(jnp.float32)
        turned = lax.ppermute(
            summed[:, :C].astype(jnp.bfloat16),
            ("ctx", "head"),
            [(i * n_head + h, h * n_head + i) for i in range(n_ctx) for h in range(n_head)],
        )
        row_feats = shifts(turned, "head")
        col_feats = shifts(summed[:, C:].astype(jnp.bfloat16), "ctx")
        order = [(at + n_ctx - s) % n_ctx for at in (ours, mine) for s in range(variants)]
    else:
        blocks_here = n_ctx // splits
        part = attend((mine % splits) * blocks_here + jnp.arange(blocks_here), jnp.bfloat16)
        feats = lax.all_gather(lax.psum(part, "head"), "ctx", axis=0, tiled=False)
        feats = feats.reshape(variants, n_ctx, pair_rows, 2 * C)
        row_feats = lax.dynamic_index_in_dim(feats, mine, 1, keepdims=False)[:, :, :C]
        col_feats = lax.dynamic_index_in_dim(feats, ours, 1, keepdims=False)[:, :, C:]
        row_feats, col_feats = list(row_feats), list(col_feats)
        order = list(range(variants)) * 2

    return pl.pallas_call(
        functools.partial(pair_kernel, variants),
        grid=(pair_rows // ROWS,),
        out_shape=jax.ShapeDtypeStruct((variants, pair_rows, pair_rows, C), jnp.bfloat16),
        in_specs=[
            whole(pltpu.SMEM),
            pl.BlockSpec((SHIFTS, 2 * pair_rows, C), lambda i: (0, 0, 0)),
        ]
        + [pl.BlockSpec((pair_rows, C), lambda i: (0, 0))] * (2 * variants),
        out_specs=pl.BlockSpec((variants, ROWS, pair_rows, C), lambda i: (0, i, 0, 0)),
        scratch_shapes=[
            pltpu.VMEM((variants, pair_rows, C), jnp.float32),
            pltpu.VMEM((variants, pair_rows, C), jnp.bfloat16),
        ],
        compiler_params=pltpu.CompilerParams(vmem_limit_bytes=24 * MIB),
        name="pair_map",
    )(jnp.stack(order).astype(jnp.int32) if splits == 1 else jnp.array(order, jnp.int32),
      table, *row_feats, *col_feats)


def solution(mesh):
    in_specs = (
        P("ctx", "head"),
        P("var", None),
        P(None, "head"),
        P("head"),
        P(None, "head"),
        P("head", None),
        P("head", None),
        P(),
    )
    out_specs = P("var", "ctx", "head", None)
    return jax.shard_map(local, mesh=mesh, in_specs=in_specs, out_specs=out_specs, check_vma=False)
```

```python
import functools
import math

import jax
import jax.numpy as jnp
from jax import lax
from jax.experimental import pallas as pl
from jax.experimental.pallas import tpu as pltpu
from jax.sharding import PartitionSpec as P

HD = 128
VD = 192
VP = 256
C = 128
NB = 16
POOL = 4
WIN = 160
ALIGN = 32
CHUNK = 512
SHIFTS = 16
ROWS = 16
TAP_ROWS = 16
MIB = 1024 * 1024
QSCALE = math.log2(math.e) / math.sqrt(HD)
GELU_A = math.sqrt(2.0 / math.pi)
GELU_B = GELU_A * 0.044715


def trunk_of(taps, low, middle, high):
    convolved = taps[0:1] * low + taps[1:2] * middle + taps[2:3] * high + taps[3:4]
    half = 0.5 * convolved
    bent = jnp.tanh(convolved * (GELU_A + GELU_B * (convolved * convolved)))
    return middle + (half + half * bent)


def pool_matrix(count):
    wide = lax.broadcasted_iota(jnp.int32, (count // POOL, count), 1) // POOL
    tall = lax.broadcasted_iota(jnp.int32, (count // POOL, count), 0)
    return jnp.where(wide == tall, 1.0 / POOL, 0.0).astype(jnp.bfloat16)


def project_kernel(
    heads, n_var, n_head, count, tiles, finish, dels, place, chosen, w_proj, *refs
):
    taps = refs[0]
    pieces = refs[1 : 1 + 2 * count]
    rest = refs[1 + 2 * count :]
    done_kvq, done_pooled = (rest[0], rest[1]) if finish == 2 else (None, None)
    out, pooled_out, given, weights, rows, left, right, sems, done_sems = rest[
        2 if finish == 2 else 0 :
    ]
    step, width = pieces[0].shape[1:]
    tokens = rows.shape[1] - 2 * step
    size = step // POOL
    ours, core, variant = place[0], place[1], place[2]

    given_copy = pltpu.make_async_copy(w_proj, given, done_sems.at[done_sems.shape[0] - 1])
    given_copy.start()
    copies = []
    for index, piece in enumerate(pieces):
        half = core if index < count else 1 - core
        at = pl.multiple_of((place[3 + index % count] * n_var + half + 1) * step, step)
        for s in range(n_head):
            copy = pltpu.make_async_copy(
                piece.at[s], rows.at[s, pl.ds(at, step)], sems.at[index, s]
            )
            copy.start()
            copies.append(copy)
    if finish == 2:
        others = done_kvq.shape[0] // step
        done_copies = []
        for index in range(others):
            at = pl.multiple_of(chosen[tiles + index] * step, step)
            copy = pltpu.make_async_copy(
                done_kvq.at[pl.ds(index * step, step)], out.at[pl.ds(at, step)], done_sems.at[index]
            )
            copy.start()
            done_copies.append(copy)
            small = pl.multiple_of(chosen[tiles + index] * size, size)
            pooled_out[pl.ds(small, size)] = done_pooled[index * size : (index + 1) * size]
    rows[:, 0:step] = jnp.zeros((n_head, step, width), jnp.bfloat16)
    rows[:, tokens + step :] = jnp.zeros((n_head, step, width), jnp.bfloat16)
    columns = weights.shape[1]
    given_copy.wait()
    for s, back in enumerate(head_order(n_head)):
        source = pl.ds(pl.multiple_of(lax.rem(ours + n_head - back, n_head) * width, ALIGN), width)
        into = slice(s * width, (s + 1) * width)
        for h in range(heads):
            low, key, value = h * (2 * HD + VD), h * HD, heads * HD + h * VP
            query = heads * (HD + VP) + h * HD
            weights[into, key : key + HD] = given[source, low + HD : low + 2 * HD]
            weights[into, value : value + VD] = given[source, low + 2 * HD : low + 2 * HD + VD]
            weights[into, value + VD : value + VP] = jnp.zeros((width, VP - VD), jnp.bfloat16)
            weights[into, query : query + HD] = given[source, low : low + HD]
    at = lax.broadcasted_iota(jnp.int32, (1, columns), 1)
    ones = jnp.zeros((1, columns), jnp.float32)
    scale = jnp.where(at >= heads * (HD + VP), QSCALE, 1.0)
    for h in range(heads):
        ones = jnp.where(at == heads * HD + h * VP + VD, 1.0, ones)
    low_taps = [
        (taps[s, 0:4].astype(jnp.float32) + taps[s, 4:8].astype(jnp.float32)).astype(jnp.bfloat16)
        for s in range(n_head)
    ]
    for copy in copies:
        copy.wait()

    def make(stage, into):
        for part in range(2):
            start = chosen[stage * 2 + part] * step
            for s in range(n_head):
                into[part * step : (part + 1) * step, s * width : (s + 1) * width] = trunk_of(
                    low_taps[s],
                    *(
                        rows[s, pl.ds(pl.multiple_of(start + shift, step), step), :]
                        for shift in (0, step, 2 * step)
                    ),
                )

    def product_of(block):
        product = jnp.dot(block, weights[...], preferred_element_type=jnp.float32)
        return (product * scale + ones).astype(jnp.bfloat16)

    def project(stage, block):
        product = product_of(block[...])
        for part in range(2):
            at = chosen[stage * 2 + part] if finish else stage * 2 + part
            rows_here = slice(part * step, (part + 1) * step)
            out[pl.ds(pl.multiple_of(at * step, step), step)] = product[rows_here]
            pooled_out[pl.ds(pl.multiple_of(at * size, size), size)] = jnp.dot(
                pool_matrix(step), block[rows_here, 0:width], preferred_element_type=jnp.float32
            )

    first, last = dels[variant, 0], dels[variant, 1]

    def window(index):
        start = (first // ALIGN) * ALIGN + (index - 1) * step
        return pl.multiple_of(jnp.clip(start, 0, tokens - WIN), ALIGN)

    def make_windows(into):
        for index in range(3):
            start = window(index)
            at = start + lax.broadcasted_iota(jnp.int32, (WIN, 1), 0)
            kept = [
                jnp.where(
                    jnp.logical_or(at + shift < first, at + shift >= last), 1.0, 0.0
                ).astype(jnp.bfloat16)
                for shift in (-step, 0, step)
            ]
            for s in range(n_head):
                into[index * WIN : (index + 1) * WIN, s * width : (s + 1) * width] = trunk_of(
                    low_taps[s],
                    *(
                        rows[s, pl.ds(pl.multiple_of(start + shift, ALIGN), WIN), :] * keep
                        for shift, keep in zip((0, step, 2 * step), kept)
                    ),
                )

    stages = tiles // 2
    make(0, left)

    def two_stages(n, carry):
        make(2 * n + 1, right)
        project(2 * n, left)
        make(2 * n + 2, left)
        project(2 * n + 1, right)
        return carry

    if stages > 2:
        lax.fori_loop(0, stages // 2 - 1, two_stages, 0)
    make(stages - 1, right)
    project(stages - 2, left)
    if finish:
        make_windows(left)
    project(stages - 1, right)
    if finish:
        product = product_of(left[0 : 3 * WIN])
        if finish == 2:
            for copy in done_copies:
                copy.wait()
        for index in range(3):
            rows_here = slice(index * WIN, (index + 1) * WIN)
            out[pl.ds(window(index), WIN)] = product[rows_here]
            small = pl.multiple_of(window(index) // POOL, ALIGN // POOL)
            pooled_out[pl.ds(small, WIN // POOL)] = jnp.dot(
                pool_matrix(WIN), left[rows_here, 0:width], preferred_element_type=jnp.float32
            )


def attend_kernel(
    heads, own, order, kvq, pooled, w_mix, w_pair,
    out, scores_a, scores_b, top_a, top_b, total,
):
    tokens = kvq.shape[0]
    chunk = scores_a.shape[2]
    steps = tokens // chunk
    key_cols, value_cols = heads * HD, heads * (HD + VP)
    pool = pool_matrix(own)
    scores, tops = (scores_a, scores_b), (top_a, top_b)
    chains = [(n, h) for n in range(out.shape[0]) for h in range(heads)]

    def score(index, c):
        n, h = chains[index]
        low = value_cols + h * HD
        found = lax.dot_general(
            kvq[pl.ds(pl.multiple_of(order[n] * own, own), own), low : low + HD],
            kvq[pl.ds(pl.multiple_of(c * chunk, chunk), chunk), h * HD : (h + 1) * HD],
            (((1,), (1,)), ((), ())),
            preferred_element_type=jnp.float32,
        )
        scores[index % 2][c] = found
        best = found[:, 0:128]
        for low in range(128, chunk, 128):
            best = jnp.maximum(best, found[:, low : low + 128])
        top = tops[index % 2]
        top[...] = jnp.maximum(top[...], best)

    def clear(index):
        tops[index % 2][...] = jnp.full(top_a.shape, -jnp.inf, jnp.float32)

    clear(0)

    def first_scores(c, carry):
        score(0, c)
        return carry

    lax.fori_loop(0, steps, first_scores, 0)
    for index, (n, h) in enumerate(chains):
        more = index + 1 < len(chains)
        if more:
            clear(index + 1)
        row_max = jnp.max(tops[index % 2][...], axis=1, keepdims=True)
        total[...] = jnp.zeros(total.shape, jnp.float32)
        low = key_cols + h * VP

        def weigh(c, carry):
            weights = jnp.exp2((scores[index % 2][c] - row_max).astype(jnp.bfloat16))
            if more:
                score(index + 1, c)
            total[...] += jnp.dot(
                weights,
                kvq[pl.ds(pl.multiple_of(c * chunk, chunk), chunk), low : low + VP],
                preferred_element_type=jnp.float32,
            )
            return carry

        lax.fori_loop(0, steps, weigh, 0)
        mixed = total[...]
        mixed = (mixed * (1.0 / mixed[:, VD : VD + 1])).astype(jnp.bfloat16)
        mixed = jnp.dot(pool, mixed, preferred_element_type=jnp.float32).astype(jnp.bfloat16)
        if h == 0:
            size = own // POOL
            pair = jnp.dot(
                pooled[pl.ds(pl.multiple_of(order[n] * size, size), size)].astype(jnp.bfloat16),
                w_pair[...],
                preferred_element_type=jnp.float32,
            )
        pair = pair + jnp.dot(mixed, w_mix[h], preferred_element_type=jnp.float32)
        if h == heads - 1:
            out[n] = pair.astype(out.dtype)


def pair_kernel(variants, order, table, *refs):
    row_feats = refs[:variants]
    col_feats = refs[variants : 2 * variants]
    out, rows, cols, blocks, sems = refs[2 * variants :]
    side = cols.shape[1]
    count = rows.shape[1]
    for s in range(variants):
        rows[order[s]] = row_feats[s][...].astype(jnp.float32)
        cols[order[variants + s]] = col_feats[s][...]

    def write(block, slot, variant):
        into = out.at[variant, pl.ds(block * ROWS, ROWS)]
        return pltpu.make_async_copy(blocks.at[slot, variant], into, sems.at[slot, variant])

    def one_block(block, carry):
        slot = lax.rem(block, 2)
        for variant in range(variants):
            pl.when(block >= 2)(write(block, slot, variant).wait)
            for r in range(ROWS):
                back = count - 1 - (block * ROWS + r)
                low = pl.multiple_of((back // SHIFTS) * SHIFTS, SHIFTS)
                relative = table[(count - 1 - r) % SHIFTS, pl.ds(low, side), :]
                row = rows[variant, pl.ds(block * ROWS + r, 1), :]
                row = jnp.broadcast_to(row, (SHIFTS, C)).astype(jnp.bfloat16)
                found = (cols[variant] + relative).reshape(side // SHIFTS, SHIFTS, C) + row[None]
                blocks[slot, variant, r] = found.reshape(side, C)
            write(block, slot, variant).start()
        return carry

    total = count // ROWS
    lax.fori_loop(0, total, one_block, 0)
    for block in range(max(total - 2, 0), total):
        for variant in range(variants):
            write(block, block % 2, variant).wait()


def distance_table(dist_table, row_start, col_start, rows, cols):
    at = jnp.arange(SHIFTS, dtype=jnp.int32)[:, None] + jnp.arange(
        rows + cols, dtype=jnp.int32
    )
    distance = jnp.abs(row_start - col_start + rows - 1 - at)
    buckets = jnp.zeros(distance.shape, jnp.int32)
    for power_index in range(NB - 1):
        buckets = buckets + (distance >= 2**power_index).astype(jnp.int32)
    one_hot = (buckets[:, :, None] == jnp.arange(NB, dtype=jnp.int32)).astype(jnp.float32)
    return jnp.einsum("skb,bc->skc", one_hot, dist_table, precision=lax.Precision.HIGHEST).astype(
        jnp.bfloat16
    )


def whole(memory=pltpu.VMEM):
    return pl.BlockSpec(memory_space=memory)


def shifts(array, axis):
    size = lax.axis_size(axis)
    return [array] + [
        lax.ppermute(array, axis, [(k, (k + s) % size) for k in range(size)])
        for s in range(1, size)
    ]


def head_order(n_head):
    return [0, 1, 3, 2] if n_head == 4 else list(range(n_head))


def tap_rows(conv_taps, conv_bias):
    taps = jnp.concatenate([conv_taps, conv_bias[None]], 0)
    high = taps.astype(jnp.bfloat16)
    low = (taps - high.astype(jnp.float32)).astype(jnp.bfloat16)
    rest = jnp.zeros((TAP_ROWS - 8, taps.shape[1]), jnp.bfloat16)
    return jnp.concatenate([high, low, rest], 0)


def gather_rows(block, n_ctx, n_var, n_head, mine, core):
    if n_ctx == 4 and n_head == 4 and n_var == 2:
        shift = lambda array, s: lax.ppermute(array, "head", [(k, (k + s) % 4) for k in range(4)])
        over = lambda array, bit: lax.ppermute(array, "ctx", [(k, k ^ bit) for k in range(4)])
        crossing = lambda array: lax.ppermute(array, "var", [(0, 1), (1, 0)])
        step = block.shape[0] - TAP_ROWS
        first = shift(block, 1)
        near = jnp.stack([block, first, shift(block, 3)])
        later, _ = lax.optimization_barrier((block, first))
        far = shift(later, 2)[None]
        taps = jnp.concatenate([near[:, step:], far[:, step:]])
        near, far = near[:, :step], far[:, :step]
        slab, over_x, over_y = (
            jnp.concatenate(pair)
            for pair in (
                (near, far), (over(near, 1), over(far, 1)), (over(near, 2), over(far, 2))
            )
        )
        own_crossed = crossing(slab)
        over_x, over_y, own_crossed = lax.optimization_barrier((over_x, over_y, own_crossed))
        pairs = [(2 * k + c, 2 * (k ^ (c + 1)) + c) for k in range(4) for c in range(2)]
        corner = lax.ppermute(jnp.where(core == 0, over_y, over_x), ("ctx", "var"), pairs)
        sides = jnp.stack([over_x, over_y])
        sides_crossed = crossing(sides)
        pieces = [slab, over_x, over_y, corner]
        crossed = [own_crossed, sides_crossed[0], sides_crossed[1]]
        return pieces, crossed, [mine, mine ^ 1, mine ^ 2, mine ^ 3], taps
    slab = jnp.stack(shifts(block, "head"))
    taps = slab[:, -TAP_ROWS:]
    pieces = shifts(slab[:, :-TAP_ROWS], "ctx")
    crossed = [lax.ppermute(piece, "var", [(0, 1), (1, 0)]) for piece in pieces]
    return pieces, crossed, [(mine + n_ctx - s) % n_ctx for s in range(n_ctx)], taps


def local(sequence, deletions, conv_taps, conv_bias, w_proj, w_out, w_pair, dist_table):
    own, width = sequence.shape
    variants = deletions.shape[0]
    heads = w_out.shape[0] // VD
    n_ctx, n_head, n_var = (lax.axis_size(name) for name in ("ctx", "head", "var"))
    if n_ctx != n_head or n_var != 2 or n_ctx % variants:
        raise ValueError("mesh shape")
    step = own // n_var
    tokens = n_ctx * own
    pair_rows = own // POOL
    columns = heads * (2 * HD + VP)
    splits = n_ctx // variants
    mine, ours, core = (lax.axis_index(name) for name in ("ctx", "head", "var"))

    half = lax.dynamic_slice_in_dim(sequence, core * step, step, 0)
    half = jnp.concatenate([half, tap_rows(conv_taps, conv_bias)], 0)
    pieces, crossed, blocks, taps = gather_rows(half, n_ctx, n_var, n_head, mine, core)
    place = jnp.stack([ours, core, mine // splits] + blocks).astype(jnp.int32)
    all_tiles = n_ctx * n_var
    project_vmem = 60 * MIB

    def project(count, tiles, finish, chosen, done):
        out_tiles = all_tiles if finish else tiles
        return pl.pallas_call(
            functools.partial(project_kernel, heads, n_var, n_head, count, tiles, finish),
            out_shape=(
                jax.ShapeDtypeStruct((out_tiles * step, columns), jnp.bfloat16),
                jax.ShapeDtypeStruct((out_tiles * step // POOL, width), jnp.float32),
            ),
            in_specs=[whole(pltpu.SMEM)] * 3
            + [whole(pl.ANY)]
            + [whole()]
            + [whole(pl.ANY)] * (2 * count)
            + ([whole(pl.ANY), whole()] if done else []),
            out_specs=(whole(), whole()),
            scratch_shapes=[
                pltpu.VMEM(w_proj.shape, jnp.bfloat16),
                pltpu.VMEM((n_head * width, columns), jnp.bfloat16),
                pltpu.VMEM((n_head, tokens + 2 * step, width), jnp.bfloat16),
                pltpu.VMEM((2 * step, n_head * width), jnp.bfloat16),
                pltpu.VMEM((2 * step, n_head * width), jnp.bfloat16),
                pltpu.SemaphoreType.DMA((2 * count, n_head)),
                pltpu.SemaphoreType.DMA((all_tiles + 1,)),
            ],
            compiler_params=pltpu.CompilerParams(vmem_limit_bytes=project_vmem),
            name="project",
        )(
            deletions, place, chosen, w_proj, taps,
            *pieces[:count], *crossed[:count], *(done or ()),
        )

    if splits == 1 and len(pieces) == 4:
        early = jnp.array([[0, 1, 2, 3], [0, 1, 2, 7], [0, 5, 6, 7], [4, 5, 6, 7]], jnp.int32)[mine]
        late = jnp.array([[4, 5, 6, 7], [3, 4, 5, 6], [1, 2, 3, 4], [0, 1, 2, 3]], jnp.int32)[mine]
        done = project(3, 4, 0, early, None)
        corner, done = lax.optimization_barrier((pieces[3], done))
        pieces = pieces[:3] + [corner]
        crossed = crossed + [lax.ppermute(corner, "var", [(0, 1), (1, 0)])]
        kvq, pooled = project(4, 4, 2, jnp.concatenate([late, early]), done)
    else:
        chosen = jnp.arange(all_tiles, dtype=jnp.int32)
        kvq, pooled = project(len(pieces), all_tiles, 1, chosen, None)
    late_pair, _ = lax.optimization_barrier((w_pair, pieces[0]))
    filled = -(-width // 512) * 512
    late_pair = jnp.pad(late_pair, ((0, filled - width), (0, 0)))
    pair_all, _ = lax.optimization_barrier(
        (lax.all_gather(late_pair, "head", axis=0, tiled=False), pooled)
    )
    w_mix = jnp.dot(
        w_out, pair_all[:, :width].reshape(-1, 2 * C), preferred_element_type=jnp.float32
    )
    w_mix = w_mix.astype(jnp.bfloat16).reshape(heads, VD, 2 * C)
    w_mix = jnp.pad(w_mix, ((0, 0), (0, VP - VD), (0, 0)))
    table = distance_table(dist_table, mine * pair_rows, ours * pair_rows, pair_rows, pair_rows)

    chunk = min(tokens, CHUNK)

    def attend(order, dtype):
        count = order.shape[0]
        return pl.pallas_call(
            functools.partial(attend_kernel, heads, own),
            out_shape=jax.ShapeDtypeStruct((count, pair_rows, 2 * C), dtype),
            in_specs=[whole(pltpu.SMEM)] + [whole()] * 4,
            out_specs=whole(),
            scratch_shapes=[
                pltpu.VMEM((tokens // chunk, own, chunk), jnp.float32),
                pltpu.VMEM((tokens // chunk, own, chunk), jnp.float32),
                pltpu.VMEM((own, 128), jnp.float32),
                pltpu.VMEM((own, 128), jnp.float32),
                pltpu.VMEM((own, VP), jnp.float32),
            ],
            compiler_params=pltpu.CompilerParams(vmem_limit_bytes=(20 if splits == 1 else 52) * MIB),
            cost_estimate=pl.CostEstimate(
                flops=2 * count * heads * own * tokens * (2 * HD + VP),
                bytes_accessed=2 * tokens * columns,
                transcendentals=count * heads * own * tokens,
            ),
            name="attend",
        )(order.astype(jnp.int32), kvq, pooled, w_mix, w_pair)

    if splits == 1:
        sent = attend((ours + jnp.arange(1, n_head)) % n_head, jnp.bfloat16)
        last_block, table = lax.optimization_barrier((ours[None], table))
        summed = attend(last_block, jnp.float32)[0]
        for s in range(1, n_head):
            pairs = [(k, (k + s) % n_head) for k in range(n_head)]
            summed += lax.ppermute(sent[s - 1], "head", pairs).astype(jnp.float32)
        turned = lax.ppermute(
            summed[:, :C].astype(jnp.bfloat16),
            ("ctx", "head"),
            [(i * n_head + h, h * n_head + i) for i in range(n_ctx) for h in range(n_head)],
        )
        row_feats = shifts(turned, "head")
        col_feats = shifts(summed[:, C:].astype(jnp.bfloat16), "ctx")
        order = [(at + n_ctx - s) % n_ctx for at in (ours, mine) for s in range(variants)]
    else:
        blocks_here = n_ctx // splits
        part = attend((mine % splits) * blocks_here + jnp.arange(blocks_here), jnp.bfloat16)
        feats = lax.all_gather(lax.psum(part, "head"), "ctx", axis=0, tiled=False)
        feats = feats.reshape(variants, n_ctx, pair_rows, 2 * C)
        row_feats = lax.dynamic_index_in_dim(feats, mine, 1, keepdims=False)[:, :, :C]
        col_feats = lax.dynamic_index_in_dim(feats, ours, 1, keepdims=False)[:, :, C:]
        row_feats, col_feats = list(row_feats), list(col_feats)
        order = list(range(variants)) * 2

    return pl.pallas_call(
        functools.partial(pair_kernel, variants),
        out_shape=jax.ShapeDtypeStruct((variants, pair_rows, pair_rows, C), jnp.bfloat16),
        in_specs=[whole(pltpu.SMEM)] + [whole()] * (1 + 2 * variants),
        out_specs=whole(pl.ANY),
        scratch_shapes=[
            pltpu.VMEM((variants, pair_rows, C), jnp.float32),
            pltpu.VMEM((variants, pair_rows, C), jnp.bfloat16),
            pltpu.VMEM((2, variants, ROWS, pair_rows, C), jnp.bfloat16),
            pltpu.SemaphoreType.DMA((2, variants)),
        ],
        compiler_params=pltpu.CompilerParams(vmem_limit_bytes=24 * MIB),
        name="pair_map",
    )(jnp.stack(order).astype(jnp.int32) if splits == 1 else jnp.array(order, jnp.int32),
      table, *row_feats, *col_feats)


def solution(mesh):
    in_specs = (
        P("ctx", "head"),
        P("var", None),
        P(None, "head"),
        P("head"),
        P(None, "head"),
        P("head", None),
        P("head", None),
        P(),
    )
    out_specs = P("var", "ctx", "head", None)
    return jax.shard_map(local, mesh=mesh, in_specs=in_specs, out_specs=out_specs, check_vma=False)
```

```python
import functools
import math

import jax
import jax.numpy as jnp
from jax import lax
from jax.experimental import pallas as pl
from jax.experimental.pallas import tpu as pltpu
from jax.sharding import PartitionSpec as P

HD = 128
VD = 192
VP = 256
C = 128
NB = 16
POOL = 4
WIN = 160
ALIGN = 32
CHUNK = 512
SHIFTS = 16
ROWS = 16
TAP_ROWS = 16
MIB = 1024 * 1024
QSCALE = math.log2(math.e) / math.sqrt(HD)
GELU_A = math.sqrt(2.0 / math.pi)
GELU_B = GELU_A * 0.044715


def trunk_of(taps, low, middle, high):
    convolved = taps[0:1] * low + taps[1:2] * middle + taps[2:3] * high + taps[3:4]
    half = 0.5 * convolved
    bent = jnp.tanh(convolved * (GELU_A + GELU_B * (convolved * convolved)))
    return middle + (half + half * bent)


def pool_matrix(count):
    wide = lax.broadcasted_iota(jnp.int32, (count // POOL, count), 1) // POOL
    tall = lax.broadcasted_iota(jnp.int32, (count // POOL, count), 0)
    return jnp.where(wide == tall, 1.0 / POOL, 0.0).astype(jnp.bfloat16)


def project_kernel(heads, n_var, n_head, blocks, first_piece, tiles, finish, scalars, taps, *refs):
    count = (blocks - first_piece) if finish else 3
    pieces, rest = refs[: 2 * count], refs[2 * count :]
    if first_piece:
        weights, rows, out, pooled_out, left, right, sems = rest[0], *rest[4:]
    else:
        w_proj, weights, rows, out, pooled_out, given, left, right, sems = rest
    step, width = pieces[0].shape[1:]
    tokens = rows.shape[1] - 2 * step
    size = step // POOL
    ours, core, first, last = (scalars[k] for k in range(4))

    def block_of(index):
        return scalars[4 + first_piece + index]

    def chosen(index):
        return scalars[4 + blocks + (tiles if first_piece else 0) + index]

    copies = []
    for index, piece in enumerate(pieces):
        half = core if index < count else 1 - core
        at = pl.multiple_of((block_of(index % count) * n_var + half + 1) * step, step)
        for s in range(n_head):
            copy = pltpu.make_async_copy(
                piece.at[s], rows.at[s, pl.ds(at, step)], sems.at[index, s]
            )
            copy.start()
            copies.append(copy)
    if not first_piece:
        given_copy = pltpu.make_async_copy(w_proj, given, sems.at[2 * count, 0])
        given_copy.start()
        rows[:, 0:step] = jnp.zeros((n_head, step, width), jnp.bfloat16)
        rows[:, tokens + step :] = jnp.zeros((n_head, step, width), jnp.bfloat16)
    columns = weights.shape[1]
    if not first_piece:
        given_copy.wait()
        for s, back in enumerate(head_order(n_head)):
            source = pl.ds(pl.multiple_of(lax.rem(ours + n_head - back, n_head) * width, ALIGN), width)
            into = slice(s * width, (s + 1) * width)
            for h in range(heads):
                low, key, value = h * (2 * HD + VD), h * HD, heads * HD + h * VP
                query = heads * (HD + VP) + h * HD
                weights[into, key : key + HD] = given[source, low + HD : low + 2 * HD]
                weights[into, value : value + VD] = given[source, low + 2 * HD : low + 2 * HD + VD]
                weights[into, value + VD : value + VP] = jnp.zeros((width, VP - VD), jnp.bfloat16)
                weights[into, query : query + HD] = given[source, low : low + HD]
    at = lax.broadcasted_iota(jnp.int32, (1, columns), 1)
    ones = jnp.zeros((1, columns), jnp.float32)
    scale = jnp.where(at >= heads * (HD + VP), QSCALE, 1.0)
    for h in range(heads):
        ones = jnp.where(at == heads * HD + h * VP + VD, 1.0, ones)
    low_taps = [taps[s, 0:4] for s in range(n_head)]
    for copy in copies:
        copy.wait()

    def make(stage, into):
        for part in range(2):
            start = chosen(stage * 2 + part) * step
            for s in range(n_head):
                into[part * step : (part + 1) * step, s * width : (s + 1) * width] = trunk_of(
                    low_taps[s],
                    *(
                        rows[s, pl.ds(pl.multiple_of(start + shift, step), step), :]
                        for shift in (0, step, 2 * step)
                    ),
                )

    def product_of(block):
        product = jnp.dot(block, weights[...], preferred_element_type=jnp.float32)
        return (product * scale + ones).astype(jnp.bfloat16)

    def project(stage, block):
        product = product_of(block[...])
        for part in range(2):
            at = chosen(stage * 2 + part)
            rows_here = slice(part * step, (part + 1) * step)
            out[pl.ds(pl.multiple_of(at * step, step), step)] = product[rows_here]
            pooled_out[pl.ds(pl.multiple_of(at * size, size), size)] = jnp.dot(
                pool_matrix(step), block[rows_here, 0:width], preferred_element_type=jnp.float32
            )

    def window(index):
        start = (first // ALIGN) * ALIGN + (index - 1) * step
        return pl.multiple_of(jnp.clip(start, 0, tokens - WIN), ALIGN)

    def make_windows(into):
        for index in range(3):
            start = window(index)
            at = start + lax.broadcasted_iota(jnp.int32, (WIN, 1), 0)
            kept = [
                jnp.where(
                    jnp.logical_or(at + shift < first, at + shift >= last), 1.0, 0.0
                ).astype(jnp.bfloat16)
                for shift in (-step, 0, step)
            ]
            for s in range(n_head):
                into[index * WIN : (index + 1) * WIN, s * width : (s + 1) * width] = trunk_of(
                    low_taps[s],
                    *(
                        rows[s, pl.ds(pl.multiple_of(start + shift, ALIGN), WIN), :] * keep
                        for shift, keep in zip((0, step, 2 * step), kept)
                    ),
                )

    stages = tiles // 2
    make(0, left)

    def two_stages(n, carry):
        make(2 * n + 1, right)
        project(2 * n, left)
        make(2 * n + 2, left)
        project(2 * n + 1, right)
        return carry

    if stages > 2:
        lax.fori_loop(0, stages // 2 - 1, two_stages, 0)
    make(stages - 1, right)
    project(stages - 2, left)
    if finish:
        make_windows(left)
    project(stages - 1, right)
    if finish:
        product = product_of(left[0 : 3 * WIN])
        for index in range(3):
            rows_here = slice(index * WIN, (index + 1) * WIN)
            out[pl.ds(window(index), WIN)] = product[rows_here]
            small = pl.multiple_of(window(index) // POOL, ALIGN // POOL)
            pooled_out[pl.ds(small, WIN // POOL)] = jnp.dot(
                pool_matrix(WIN), left[rows_here, 0:width], preferred_element_type=jnp.float32
            )


def attend_kernel(
    heads, own, order, kvq, pooled, w_mix, w_pair,
    out, scores_a, scores_b, top_a, top_b, total,
):
    tokens = kvq.shape[0]
    chunk = scores_a.shape[2]
    steps = tokens // chunk
    key_cols, value_cols = heads * HD, heads * (HD + VP)
    pool = pool_matrix(own)
    scores, tops = (scores_a, scores_b), (top_a, top_b)
    chains = [(n, h) for n in range(out.shape[0]) for h in range(heads)]

    def score(index, c):
        n, h = chains[index]
        low = value_cols + h * HD
        found = lax.dot_general(
            kvq[pl.ds(pl.multiple_of(order[n] * own, own), own), low : low + HD],
            kvq[pl.ds(pl.multiple_of(c * chunk, chunk), chunk), h * HD : (h + 1) * HD],
            (((1,), (1,)), ((), ())),
            preferred_element_type=jnp.float32,
        )
        scores[index % 2][c] = found
        best = found[:, 0:128]
        for low in range(128, chunk, 128):
            best = jnp.maximum(best, found[:, low : low + 128])
        top = tops[index % 2]
        top[...] = jnp.maximum(top[...], best)

    def clear(index):
        tops[index % 2][...] = jnp.full(top_a.shape, -jnp.inf, jnp.float32)

    clear(0)

    def first_scores(c, carry):
        score(0, c)
        return carry

    lax.fori_loop(0, steps, first_scores, 0)
    for index, (n, h) in enumerate(chains):
        more = index + 1 < len(chains)
        if more:
            clear(index + 1)
        row_max = jnp.max(tops[index % 2][...], axis=1, keepdims=True)
        total[...] = jnp.zeros(total.shape, jnp.float32)
        low = key_cols + h * VP

        def weigh(c, carry):
            weights = jnp.exp2((scores[index % 2][c] - row_max).astype(jnp.bfloat16))
            if more:
                score(index + 1, c)
            total[...] += jnp.dot(
                weights,
                kvq[pl.ds(pl.multiple_of(c * chunk, chunk), chunk), low : low + VP],
                preferred_element_type=jnp.float32,
            )
            return carry

        lax.fori_loop(0, steps, weigh, 0)
        mixed = total[...]
        mixed = (mixed * (1.0 / mixed[:, VD : VD + 1])).astype(jnp.bfloat16)
        mixed = jnp.dot(pool, mixed, preferred_element_type=jnp.float32).astype(jnp.bfloat16)
        if h == 0:
            size = own // POOL
            pair = jnp.dot(
                pooled[pl.ds(pl.multiple_of(order[n] * size, size), size)].astype(jnp.bfloat16),
                w_pair[...],
                preferred_element_type=jnp.float32,
            )
        pair = pair + jnp.dot(mixed, w_mix[h], preferred_element_type=jnp.float32)
        if h == heads - 1:
            out[n] = pair.astype(out.dtype)


def pair_kernel(variants, order, table, *refs):
    row_feats = refs[:variants]
    col_feats = refs[variants : 2 * variants]
    out, rows, cols, blocks, sems = refs[2 * variants :]
    side = cols.shape[1]
    count = rows.shape[1]
    for s in range(variants):
        rows[order[s]] = row_feats[s][...].astype(jnp.float32)
        cols[order[variants + s]] = col_feats[s][...]

    def write(block, slot, variant):
        into = out.at[variant, pl.ds(block * ROWS, ROWS)]
        return pltpu.make_async_copy(blocks.at[slot, variant], into, sems.at[slot, variant])

    def one_block(block, carry):
        slot = lax.rem(block, 2)
        for variant in range(variants):
            pl.when(block >= 2)(write(block, slot, variant).wait)
            for r in range(ROWS):
                back = count - 1 - (block * ROWS + r)
                low = pl.multiple_of((back // SHIFTS) * SHIFTS, SHIFTS)
                relative = table[(count - 1 - r) % SHIFTS, pl.ds(low, side), :]
                row = rows[variant, pl.ds(block * ROWS + r, 1), :]
                row = jnp.broadcast_to(row, (SHIFTS, C)).astype(jnp.bfloat16)
                found = (cols[variant] + relative).reshape(side // SHIFTS, SHIFTS, C) + row[None]
                blocks[slot, variant, r] = found.reshape(side, C)
            write(block, slot, variant).start()
        return carry

    total = count // ROWS
    lax.fori_loop(0, total, one_block, 0)
    for block in range(max(total - 2, 0), total):
        for variant in range(variants):
            write(block, block % 2, variant).wait()


def distance_table(dist_table, row_start, col_start, rows, cols):
    at = jnp.arange(SHIFTS, dtype=jnp.int32)[:, None] + jnp.arange(
        rows + cols, dtype=jnp.int32
    )
    distance = jnp.abs(row_start - col_start + rows - 1 - at)
    buckets = jnp.zeros(distance.shape, jnp.int32)
    for power_index in range(NB - 1):
        buckets = buckets + (distance >= 2**power_index).astype(jnp.int32)
    one_hot = (buckets[:, :, None] == jnp.arange(NB, dtype=jnp.int32)).astype(jnp.float32)
    return jnp.einsum("skb,bc->skc", one_hot, dist_table, precision=lax.Precision.HIGHEST).astype(
        jnp.bfloat16
    )


def whole(memory=pltpu.VMEM):
    return pl.BlockSpec(memory_space=memory)


def shifts(array, axis):
    size = lax.axis_size(axis)
    return [array] + [
        lax.ppermute(array, axis, [(k, (k + s) % size) for k in range(size)])
        for s in range(1, size)
    ]


def head_order(n_head):
    return [0, 1, 3, 2] if n_head == 4 else list(range(n_head))


def gather_rows(block, scalars, w_pair, n_ctx, n_var, n_head, core):
    if n_ctx == 4 and n_head == 4 and n_var == 2:
        shift = lambda array, s: lax.ppermute(array, "head", [(k, (k + s) % 4) for k in range(4)])
        over = lambda array, bit: lax.ppermute(array, "ctx", [(k, k ^ bit) for k in range(4)])
        crossing = lambda array: lax.ppermute(array, "var", [(0, 1), (1, 0)])
        step = block.shape[0] - TAP_ROWS
        first = shift(block, 1)
        near = jnp.stack([block, first, shift(block, 3)])
        near, scalars = lax.optimization_barrier((near, scalars))
        later, _ = lax.optimization_barrier((block, first))
        far = shift(later, 2)[None]
        taps = jnp.concatenate([near[:, step:], far[:, step:]])
        near, far = near[:, :step], far[:, :step]
        slab, over_x, over_y = (
            jnp.concatenate(pair)
            for pair in (
                (near, far), (over(near, 1), over(far, 1)), (over(near, 2), over(far, 2))
            )
        )
        late_pair, _ = lax.optimization_barrier((w_pair, slab))
        pair_parts = [w_pair, shift(late_pair, 1), None, shift(late_pair, 3)]
        own_crossed = crossing(slab)
        over_x, over_y, own_crossed, pair_parts[1], pair_parts[3] = lax.optimization_barrier(
            (over_x, over_y, own_crossed, pair_parts[1], pair_parts[3])
        )
        pairs = [(2 * k + c, 2 * (k ^ (c + 1)) + c) for k in range(4) for c in range(2)]
        corner = lax.ppermute(jnp.where(core == 0, over_y, over_x), ("ctx", "var"), pairs)
        pair_parts[2] = shift(late_pair, 2)
        crossed = [own_crossed, crossing(over_x), crossing(over_y)]
        return [slab, over_x, over_y, corner], crossed, taps, scalars, pair_parts
    slab = jnp.stack(shifts(block, "head"))
    taps = slab[:, -TAP_ROWS:]
    pieces = shifts(slab[:, :-TAP_ROWS], "ctx")
    crossed = [lax.ppermute(piece, "var", [(0, 1), (1, 0)]) for piece in pieces]
    return pieces, crossed, taps, scalars, shifts(w_pair, "head")


def local(sequence, deletions, conv_taps, conv_bias, w_proj, w_out, w_pair, dist_table):
    own, width = sequence.shape
    variants = deletions.shape[0]
    heads = w_out.shape[0] // VD
    n_ctx, n_head, n_var = (lax.axis_size(name) for name in ("ctx", "head", "var"))
    if n_ctx != n_head or n_var != 2 or n_ctx % variants:
        raise ValueError("mesh shape")
    step = own // n_var
    tokens = n_ctx * own
    pair_rows = own // POOL
    columns = heads * (2 * HD + VP)
    splits = n_ctx // variants
    mine, ours, core = (lax.axis_index(name) for name in ("ctx", "head", "var"))

    half = lax.dynamic_slice_in_dim(sequence, core * step, step, 0)
    taps = jnp.concatenate([conv_taps, conv_bias[None]], 0).astype(jnp.bfloat16)
    half = jnp.concatenate([half, jnp.pad(taps, ((0, TAP_ROWS - 4), (0, 0)))], 0)
    all_tiles = n_ctx * n_var
    quick = n_ctx == 4 and n_head == 4 and splits == 1
    if quick:
        blocks = [mine, mine ^ 1, mine ^ 2, mine ^ 3]
        order = jnp.array(
            [
                [0, 1, 2, 3, 4, 5, 6, 7],
                [0, 1, 2, 7, 3, 4, 5, 6],
                [0, 5, 6, 7, 1, 2, 3, 4],
                [4, 5, 6, 7, 0, 1, 2, 3],
            ],
            jnp.int32,
        )[mine]
    else:
        blocks = [(mine + n_ctx - s) % n_ctx for s in range(n_ctx)]
        order = jnp.arange(all_tiles, dtype=jnp.int32)
    scalars = jnp.concatenate(
        [
            jnp.stack([ours, core]).astype(jnp.int32),
            lax.dynamic_index_in_dim(deletions, mine // splits, 0, keepdims=False),
            jnp.stack(blocks).astype(jnp.int32),
            order,
        ]
    )
    pieces, crossed, taps, scalars, pair_parts = gather_rows(
        half, scalars, w_pair, n_ctx, n_var, n_head, core
    )
    store = [
        jax.ShapeDtypeStruct((n_head * width, columns), jnp.bfloat16),
        jax.ShapeDtypeStruct((n_head, tokens + 2 * step, width), jnp.bfloat16),
        jax.ShapeDtypeStruct((tokens, columns), jnp.bfloat16),
        jax.ShapeDtypeStruct((tokens // POOL, width), jnp.float32),
    ]

    def project(sources, first_piece, tiles, finish, given):
        n_given = len(given)
        return pl.pallas_call(
            functools.partial(
                project_kernel, heads, n_var, n_head, len(blocks), first_piece, tiles, finish
            ),
            out_shape=store[1:] if first_piece else store,
            in_specs=[whole(pltpu.SMEM), whole()]
            + [whole(pl.ANY)] * len(sources)
            + [whole(pltpu.VMEM if first_piece else pl.ANY)] * n_given,
            out_specs=[whole()] * (3 if first_piece else 4),
            scratch_shapes=([] if first_piece else [pltpu.VMEM(w_proj.shape, jnp.bfloat16)])
            + [
                pltpu.VMEM((2 * step, n_head * width), jnp.bfloat16),
                pltpu.VMEM((2 * step, n_head * width), jnp.bfloat16),
                pltpu.SemaphoreType.DMA((len(sources) + 1, n_head)),
            ],
            input_output_aliases=(
                {3 + len(sources) + k: k for k in range(3)} if first_piece else {}
            ),
            compiler_params=pltpu.CompilerParams(vmem_limit_bytes=(30 if quick else 52) * MIB),
            name="project",
        )(scalars, taps, *sources, *given)

    if quick:
        weights, *done = project(pieces[:3] + crossed, 0, 4, 0, [w_proj])
        corner, done, pair_parts = lax.optimization_barrier((pieces[3], done, pair_parts))
        corner_crossed = lax.ppermute(corner, "var", [(0, 1), (1, 0)])
        _, kvq, pooled = project([corner, corner_crossed], 3, 4, 1, [weights, *done])
    else:
        _, _, kvq, pooled = project(pieces + crossed, 0, all_tiles, 1, [w_proj])
    pair_parts, _ = lax.optimization_barrier((pair_parts, pooled))
    w_mix = jnp.zeros((heads * VD, 2 * C), jnp.float32)
    for s, part in enumerate(pair_parts):
        from_head = (ours + n_head - s) % n_head
        w_mix += jnp.dot(
            lax.dynamic_slice_in_dim(w_out, from_head * width, width, 1),
            part,
            preferred_element_type=jnp.float32,
        )
    w_mix = w_mix.astype(jnp.bfloat16).reshape(heads, VD, 2 * C)
    w_mix = jnp.pad(w_mix, ((0, 0), (0, VP - VD), (0, 0)))
    table = distance_table(dist_table, mine * pair_rows, ours * pair_rows, pair_rows, pair_rows)

    chunk = min(tokens, CHUNK)

    def attend(order, dtype):
        count = order.shape[0]
        return pl.pallas_call(
            functools.partial(attend_kernel, heads, own),
            out_shape=jax.ShapeDtypeStruct((count, pair_rows, 2 * C), dtype),
            in_specs=[whole(pltpu.SMEM)] + [whole()] * 4,
            out_specs=whole(),
            scratch_shapes=[
                pltpu.VMEM((tokens // chunk, own, chunk), jnp.float32),
                pltpu.VMEM((tokens // chunk, own, chunk), jnp.float32),
                pltpu.VMEM((own, 128), jnp.float32),
                pltpu.VMEM((own, 128), jnp.float32),
                pltpu.VMEM((own, VP), jnp.float32),
            ],
            compiler_params=pltpu.CompilerParams(vmem_limit_bytes=(20 if splits == 1 else 52) * MIB),
            cost_estimate=pl.CostEstimate(
                flops=2 * count * heads * own * tokens * (2 * HD + VP),
                bytes_accessed=2 * tokens * columns,
                transcendentals=count * heads * own * tokens,
            ),
            name="attend",
        )(order.astype(jnp.int32), kvq, pooled, w_mix, w_pair)

    if splits == 1:
        sent = attend((ours + jnp.arange(1, n_head)) % n_head, jnp.bfloat16)
        last_block, table = lax.optimization_barrier((ours[None], table))
        summed = attend(last_block, jnp.float32)[0]
        for s in range(1, n_head):
            pairs = [(k, (k + s) % n_head) for k in range(n_head)]
            summed += lax.ppermute(sent[s - 1], "head", pairs).astype(jnp.float32)
        turned = lax.ppermute(
            summed[:, :C].astype(jnp.bfloat16),
            ("ctx", "head"),
            [(i * n_head + h, h * n_head + i) for i in range(n_ctx) for h in range(n_head)],
        )
        row_feats = shifts(turned, "head")
        col_feats = shifts(summed[:, C:].astype(jnp.bfloat16), "ctx")
        order = [(at + n_ctx - s) % n_ctx for at in (ours, mine) for s in range(variants)]
    else:
        blocks_here = n_ctx // splits
        part = attend((mine % splits) * blocks_here + jnp.arange(blocks_here), jnp.bfloat16)
        feats = lax.all_gather(lax.psum(part, "head"), "ctx", axis=0, tiled=False)
        feats = feats.reshape(variants, n_ctx, pair_rows, 2 * C)
        row_feats = lax.dynamic_index_in_dim(feats, mine, 1, keepdims=False)[:, :, :C]
        col_feats = lax.dynamic_index_in_dim(feats, ours, 1, keepdims=False)[:, :, C:]
        row_feats, col_feats = list(row_feats), list(col_feats)
        order = list(range(variants)) * 2

    return pl.pallas_call(
        functools.partial(pair_kernel, variants),
        out_shape=jax.ShapeDtypeStruct((variants, pair_rows, pair_rows, C), jnp.bfloat16),
        in_specs=[whole(pltpu.SMEM)] + [whole()] * (1 + 2 * variants),
        out_specs=whole(pl.ANY),
        scratch_shapes=[
            pltpu.VMEM((variants, pair_rows, C), jnp.float32),
            pltpu.VMEM((variants, pair_rows, C), jnp.bfloat16),
            pltpu.VMEM((2, variants, ROWS, pair_rows, C), jnp.bfloat16),
            pltpu.SemaphoreType.DMA((2, variants)),
        ],
        compiler_params=pltpu.CompilerParams(vmem_limit_bytes=24 * MIB),
        name="pair_map",
    )(jnp.stack(order).astype(jnp.int32) if splits == 1 else jnp.array(order, jnp.int32),
      table, *row_feats, *col_feats)


def solution(mesh):
    in_specs = (
        P("ctx", "head"),
        P("var", None),
        P(None, "head"),
        P("head"),
        P(None, "head"),
        P("head", None),
        P("head", None),
        P(),
    )
    out_specs = P("var", "ctx", "head", None)
    return jax.shard_map(local, mesh=mesh, in_specs=in_specs, out_specs=out_specs, check_vma=False)
```

```python
import functools
import math

import jax
import jax.numpy as jnp
from jax import lax
from jax.experimental import pallas as pl
from jax.experimental.pallas import tpu as pltpu
from jax.sharding import PartitionSpec as P

HD = 128
VD = 192
VP = 256
C = 128
NB = 16
POOL = 4
WIN = 160
ALIGN = 32
CHUNK = 512
SHIFTS = 16
ROWS = 16
TAP_ROWS = 16
MIB = 1024 * 1024
QSCALE = math.log2(math.e) / math.sqrt(HD)
GELU_A = math.sqrt(2.0 / math.pi)
GELU_B = GELU_A * 0.044715


def trunk_of(taps, low, middle, high):
    convolved = taps[0:1] * low + taps[1:2] * middle + taps[2:3] * high + taps[3:4]
    half = 0.5 * convolved
    bent = jnp.tanh(convolved * (GELU_A + GELU_B * (convolved * convolved)))
    return middle + (half + half * bent)


def pool_matrix(count):
    wide = lax.broadcasted_iota(jnp.int32, (count // POOL, count), 1) // POOL
    tall = lax.broadcasted_iota(jnp.int32, (count // POOL, count), 0)
    return jnp.where(wide == tall, 1.0 / POOL, 0.0).astype(jnp.bfloat16)


def project_kernel(heads, n_var, n_head, blocks, spots, given, tiles, finish, scalars, *refs):
    count = len(spots)
    pieces, rest = refs[: 2 * count], refs[2 * count :]
    if given:
        weights, taps = rest[:2]
        rows, out, pooled_out, left, right, sems = rest[6:]
    else:
        w_proj, weights, taps, rows, out, pooled_out, token, plain, left, right, sems = rest
        token[...] = jnp.zeros(token.shape, jnp.float32)
    width = rows.shape[2]
    step = left.shape[0] // 2
    tokens = rows.shape[1] - 2 * step
    size = step // POOL
    ours, core, first, last = (scalars[k] for k in range(4))

    def chosen(index):
        return scalars[4 + blocks + (tiles if given else 0) + index]

    copies = []
    for index, piece in enumerate(pieces):
        block, spot = spots[index % count]
        half = core if index < count else 1 - core
        at = pl.multiple_of((scalars[4 + block] * n_var + half + 1) * step, step)
        for s in range(piece.shape[0]):
            copy = pltpu.make_async_copy(
                piece.at[s, pl.ds(0, step)],
                rows.at[spot + s, pl.ds(at, step)],
                sems.at[index, spot + s],
            )
            copy.start()
            copies.append(copy)
            if not given and block == 0 and index < count:
                copy = pltpu.make_async_copy(
                    piece.at[s, pl.ds(step, TAP_ROWS)], taps.at[spot + s], sems.at[2 * count, spot + s]
                )
                copy.start()
                copies.append(copy)
    if not given:
        plain_copy = pltpu.make_async_copy(w_proj, plain, sems.at[2 * count + 1, 0])
        plain_copy.start()
        rows[:, 0:step] = jnp.zeros((n_head, step, width), jnp.bfloat16)
        rows[:, tokens + step :] = jnp.zeros((n_head, step, width), jnp.bfloat16)
    columns = weights.shape[1]
    if not given:
        plain_copy.wait()
        for s, back in enumerate(head_order(n_head)):
            source = pl.ds(pl.multiple_of(lax.rem(ours + n_head - back, n_head) * width, ALIGN), width)
            into = slice(s * width, (s + 1) * width)
            for h in range(heads):
                low, key, value = h * (2 * HD + VD), h * HD, heads * HD + h * VP
                query = heads * (HD + VP) + h * HD
                weights[into, key : key + HD] = plain[source, low + HD : low + 2 * HD]
                weights[into, value : value + VD] = plain[source, low + 2 * HD : low + 2 * HD + VD]
                weights[into, value + VD : value + VP] = jnp.zeros((width, VP - VD), jnp.bfloat16)
                weights[into, query : query + HD] = plain[source, low : low + HD]
    at = lax.broadcasted_iota(jnp.int32, (1, columns), 1)
    ones = jnp.zeros((1, columns), jnp.float32)
    scale = jnp.where(at >= heads * (HD + VP), QSCALE, 1.0)
    for h in range(heads):
        ones = jnp.where(at == heads * HD + h * VP + VD, 1.0, ones)
    for copy in copies:
        copy.wait()
    low_taps = [taps[s, 0:4] for s in range(n_head)]

    def make(stage, into):
        for part in range(2):
            start = chosen(stage * 2 + part) * step
            for s in range(n_head):
                into[part * step : (part + 1) * step, s * width : (s + 1) * width] = trunk_of(
                    low_taps[s],
                    *(
                        rows[s, pl.ds(pl.multiple_of(start + shift, step), step), :]
                        for shift in (0, step, 2 * step)
                    ),
                )

    def product_of(block):
        product = jnp.dot(block, weights[...], preferred_element_type=jnp.float32)
        return (product * scale + ones).astype(jnp.bfloat16)

    def project(stage, block):
        product = product_of(block[...])
        for part in range(2):
            at = chosen(stage * 2 + part)
            rows_here = slice(part * step, (part + 1) * step)
            out[pl.ds(pl.multiple_of(at * step, step), step)] = product[rows_here]
            pooled_out[pl.ds(pl.multiple_of(at * size, size), size)] = jnp.dot(
                pool_matrix(step), block[rows_here, 0:width], preferred_element_type=jnp.float32
            )

    def window(index):
        start = (first // ALIGN) * ALIGN + (index - 1) * step
        return pl.multiple_of(jnp.clip(start, 0, tokens - WIN), ALIGN)

    def make_windows(into):
        for index in range(3):
            start = window(index)
            at = start + lax.broadcasted_iota(jnp.int32, (WIN, 1), 0)
            kept = [
                jnp.where(
                    jnp.logical_or(at + shift < first, at + shift >= last), 1.0, 0.0
                ).astype(jnp.bfloat16)
                for shift in (-step, 0, step)
            ]
            for s in range(n_head):
                into[index * WIN : (index + 1) * WIN, s * width : (s + 1) * width] = trunk_of(
                    low_taps[s],
                    *(
                        rows[s, pl.ds(pl.multiple_of(start + shift, ALIGN), WIN), :] * keep
                        for shift, keep in zip((0, step, 2 * step), kept)
                    ),
                )

    stages = tiles // 2
    make(0, left)

    def two_stages(n, carry):
        make(2 * n + 1, right)
        project(2 * n, left)
        make(2 * n + 2, left)
        project(2 * n + 1, right)
        return carry

    if stages > 2:
        lax.fori_loop(0, stages // 2 - 1, two_stages, 0)
    make(stages - 1, right)
    project(stages - 2, left)
    if finish:
        make_windows(left)
    project(stages - 1, right)
    if finish:
        product = product_of(left[0 : 3 * WIN])
        for index in range(3):
            rows_here = slice(index * WIN, (index + 1) * WIN)
            out[pl.ds(window(index), WIN)] = product[rows_here]
            small = pl.multiple_of(window(index) // POOL, ALIGN // POOL)
            pooled_out[pl.ds(small, WIN // POOL)] = jnp.dot(
                pool_matrix(WIN), left[rows_here, 0:width], preferred_element_type=jnp.float32
            )


def attend_kernel(
    heads, own, order, kvq, pooled, w_mix, w_pair,
    out, scores_a, scores_b, top_a, top_b, total,
):
    tokens = kvq.shape[0]
    chunk = scores_a.shape[2]
    steps = tokens // chunk
    key_cols, value_cols = heads * HD, heads * (HD + VP)
    pool = pool_matrix(own)
    scores, tops = (scores_a, scores_b), (top_a, top_b)
    chains = [(n, h) for n in range(out.shape[0]) for h in range(heads)]

    def score(index, c):
        n, h = chains[index]
        low = value_cols + h * HD
        found = lax.dot_general(
            kvq[pl.ds(pl.multiple_of(order[n] * own, own), own), low : low + HD],
            kvq[pl.ds(pl.multiple_of(c * chunk, chunk), chunk), h * HD : (h + 1) * HD],
            (((1,), (1,)), ((), ())),
            preferred_element_type=jnp.float32,
        )
        scores[index % 2][c] = found
        best = found[:, 0:128]
        for low in range(128, chunk, 128):
            best = jnp.maximum(best, found[:, low : low + 128])
        top = tops[index % 2]
        top[...] = jnp.maximum(top[...], best)

    def clear(index):
        tops[index % 2][...] = jnp.full(top_a.shape, -jnp.inf, jnp.float32)

    clear(0)

    def first_scores(c, carry):
        score(0, c)
        return carry

    lax.fori_loop(0, steps, first_scores, 0)
    for index, (n, h) in enumerate(chains):
        more = index + 1 < len(chains)
        if more:
            clear(index + 1)
        row_max = jnp.max(tops[index % 2][...], axis=1, keepdims=True)
        total[...] = jnp.zeros(total.shape, jnp.float32)
        low = key_cols + h * VP

        def weigh(c, carry):
            weights = jnp.exp2((scores[index % 2][c] - row_max).astype(jnp.bfloat16))
            if more:
                score(index + 1, c)
            total[...] += jnp.dot(
                weights,
                kvq[pl.ds(pl.multiple_of(c * chunk, chunk), chunk), low : low + VP],
                preferred_element_type=jnp.float32,
            )
            return carry

        lax.fori_loop(0, steps, weigh, 0)
        mixed = total[...]
        mixed = (mixed * (1.0 / mixed[:, VD : VD + 1])).astype(jnp.bfloat16)
        mixed = jnp.dot(pool, mixed, preferred_element_type=jnp.float32).astype(jnp.bfloat16)
        if h == 0:
            size = own // POOL
            pair = jnp.dot(
                pooled[pl.ds(pl.multiple_of(order[n] * size, size), size)].astype(jnp.bfloat16),
                w_pair[...],
                preferred_element_type=jnp.float32,
            )
        pair = pair + jnp.dot(mixed, w_mix[h], preferred_element_type=jnp.float32)
        if h == heads - 1:
            out[n] = pair.astype(out.dtype)


def pair_kernel(variants, order, table, *refs):
    row_feats = refs[:variants]
    col_feats = refs[variants : 2 * variants]
    out, rows, cols, blocks, sems = refs[2 * variants :]
    side = cols.shape[1]
    count = rows.shape[1]
    for s in range(variants):
        rows[order[s]] = row_feats[s][...].astype(jnp.float32)
        cols[order[variants + s]] = col_feats[s][...]

    def write(block, slot, variant):
        into = out.at[variant, pl.ds(block * ROWS, ROWS)]
        return pltpu.make_async_copy(blocks.at[slot, variant], into, sems.at[slot, variant])

    def one_block(block, carry):
        slot = lax.rem(block, 2)
        for variant in range(variants):
            pl.when(block >= 2)(write(block, slot, variant).wait)
            for r in range(ROWS):
                back = count - 1 - (block * ROWS + r)
                low = pl.multiple_of((back // SHIFTS) * SHIFTS, SHIFTS)
                relative = table[(count - 1 - r) % SHIFTS, pl.ds(low, side), :]
                row = rows[variant, pl.ds(block * ROWS + r, 1), :]
                row = jnp.broadcast_to(row, (SHIFTS, C)).astype(jnp.bfloat16)
                found = (cols[variant] + relative).reshape(side // SHIFTS, SHIFTS, C) + row[None]
                blocks[slot, variant, r] = found.reshape(side, C)
            write(block, slot, variant).start()
        return carry

    total = count // ROWS
    lax.fori_loop(0, total, one_block, 0)
    for block in range(max(total - 2, 0), total):
        for variant in range(variants):
            write(block, block % 2, variant).wait()


def distance_table(dist_table, row_start, col_start, rows, cols):
    at = jnp.arange(SHIFTS, dtype=jnp.int32)[:, None] + jnp.arange(
        rows + cols, dtype=jnp.int32
    )
    distance = jnp.abs(row_start - col_start + rows - 1 - at)
    buckets = jnp.zeros(distance.shape, jnp.int32)
    for power_index in range(NB - 1):
        buckets = buckets + (distance >= 2**power_index).astype(jnp.int32)
    one_hot = (buckets[:, :, None] == jnp.arange(NB, dtype=jnp.int32)).astype(jnp.float32)
    return jnp.einsum("skb,bc->skc", one_hot, dist_table, precision=lax.Precision.HIGHEST).astype(
        jnp.bfloat16
    )


def whole(memory=pltpu.VMEM):
    return pl.BlockSpec(memory_space=memory)


def shifts(array, axis):
    size = lax.axis_size(axis)
    return [array] + [
        lax.ppermute(array, axis, [(k, (k + s) % size) for k in range(size)])
        for s in range(1, size)
    ]


def head_order(n_head):
    return [0, 1, 3, 2] if n_head == 4 else list(range(n_head))


def gather_rows(block, w_pair, n_ctx, n_var, n_head, core):
    if n_ctx == 4 and n_head == 4 and n_var == 2:
        shift = lambda array, s: lax.ppermute(array, "head", [(k, (k + s) % 4) for k in range(4)])
        over = lambda array, bit: lax.ppermute(array, "ctx", [(k, k ^ bit) for k in range(4)])
        crossing = lambda array: lax.ppermute(array, "var", [(0, 1), (1, 0)])
        first = shift(block, 1)
        near = jnp.stack([block, first, shift(block, 3)])
        far, part = lax.optimization_barrier((shift(block, 2), w_pair))
        pair_part = shift(part, 2)
        near_x, near_y, far_x, far_y = over(near, 1), over(near, 2), over(far, 1), over(far, 2)
        early = [crossing(piece) for piece in (near, far, near_x, near_y)]
        far_x, far_y, early, pair_part = lax.optimization_barrier(
            (far_x, far_y, early, pair_part)
        )
        pieces = [near, far[None], near_x, far_x[None], near_y, far_y[None]]
        crossed = [
            early[0], early[1][None], early[2], crossing(far_x)[None], early[3], crossing(far_y)[None]
        ]
        pairs = [(2 * k + c, 2 * (k ^ (c + 1)) + c) for k in range(4) for c in range(2)]
        corner = lax.ppermute(
            jnp.where(
                core == 0,
                jnp.concatenate([near_y, far_y[None]]),
                jnp.concatenate([near_x, far_x[None]]),
            ),
            ("ctx", "var"),
            pairs,
        )
        spots = [(0, 0), (0, 3), (1, 0), (1, 3), (2, 0), (2, 3)]
        return pieces, spots, crossed, corner, [w_pair, None, pair_part, None]
    slab = jnp.stack(shifts(block, "head"))
    pieces = shifts(slab, "ctx")
    crossed = [lax.ppermute(piece, "var", [(0, 1), (1, 0)]) for piece in pieces]
    return pieces, [(s, 0) for s in range(n_ctx)], crossed, None, shifts(w_pair, "head")


def local(sequence, deletions, conv_taps, conv_bias, w_proj, w_out, w_pair, dist_table):
    own, width = sequence.shape
    variants = deletions.shape[0]
    heads = w_out.shape[0] // VD
    n_ctx, n_head, n_var = (lax.axis_size(name) for name in ("ctx", "head", "var"))
    if n_ctx != n_head or n_var != 2 or n_ctx % variants:
        raise ValueError("mesh shape")
    step = own // n_var
    tokens = n_ctx * own
    pair_rows = own // POOL
    columns = heads * (2 * HD + VP)
    splits = n_ctx // variants
    mine, ours, core = (lax.axis_index(name) for name in ("ctx", "head", "var"))

    half = lax.dynamic_slice_in_dim(sequence, core * step, step, 0)
    taps = jnp.pad(conv_taps, ((0, TAP_ROWS - 3), (0, 0))) + jnp.pad(
        conv_bias[None], ((3, TAP_ROWS - 4), (0, 0))
    )
    half = jnp.concatenate([half, taps.astype(jnp.bfloat16)], 0)
    all_tiles = n_ctx * n_var
    quick = n_ctx == 4 and n_head == 4 and splits == 1
    if quick:
        blocks = [mine, mine ^ 1, mine ^ 2, mine ^ 3]
        order = jnp.array(
            [
                [0, 1, 2, 3, 4, 5, 6, 7],
                [0, 1, 2, 7, 3, 4, 5, 6],
                [0, 5, 6, 7, 1, 2, 3, 4],
                [4, 5, 6, 7, 0, 1, 2, 3],
            ],
            jnp.int32,
        )[mine]
    else:
        blocks = [(mine + n_ctx - s) % n_ctx for s in range(n_ctx)]
        order = jnp.arange(all_tiles, dtype=jnp.int32)
    scalars = jnp.concatenate(
        [
            jnp.stack([ours, core]).astype(jnp.int32),
            lax.dynamic_index_in_dim(deletions, mine // splits, 0, keepdims=False),
            jnp.stack(blocks).astype(jnp.int32),
            order,
        ]
    )
    pieces, spots, crossed, corner, pair_parts = gather_rows(
        half, w_pair, n_ctx, n_var, n_head, core
    )
    store = [
        jax.ShapeDtypeStruct((n_head * width, columns), jnp.bfloat16),
        jax.ShapeDtypeStruct((n_head, TAP_ROWS, width), jnp.bfloat16),
        jax.ShapeDtypeStruct((n_head, tokens + 2 * step, width), jnp.bfloat16),
        jax.ShapeDtypeStruct((tokens, columns), jnp.bfloat16),
        jax.ShapeDtypeStruct((tokens // POOL, width), jnp.float32),
        jax.ShapeDtypeStruct((8, 128), jnp.float32),
    ]

    def project(sources, spots, tiles, finish, given):
        kept = store[2:5] if given else store
        return pl.pallas_call(
            functools.partial(
                project_kernel, heads, n_var, n_head, len(blocks), spots, bool(given), tiles, finish
            ),
            out_shape=kept,
            in_specs=[whole(pltpu.SMEM)]
            + [whole(pl.ANY)] * len(sources)
            + ([whole()] * len(given) if given else [whole(pl.ANY)]),
            out_specs=[whole()] * len(kept),
            scratch_shapes=([] if given else [pltpu.VMEM(w_proj.shape, jnp.bfloat16)])
            + [
                pltpu.VMEM((2 * step, n_head * width), jnp.bfloat16),
                pltpu.VMEM((2 * step, n_head * width), jnp.bfloat16),
                pltpu.SemaphoreType.DMA((len(sources) + 2, n_head)),
            ],
            input_output_aliases=(
                {3 + len(sources) + k: k for k in range(3)} if given else {}
            ),
            compiler_params=pltpu.CompilerParams(vmem_limit_bytes=(30 if quick else 52) * MIB),
            name="project",
        )(scalars, *sources, *(given or [w_proj]))

    if quick:
        *done, token = project(pieces + crossed, spots, 4, 0, None)
        corner, token, part = lax.optimization_barrier((corner, token, w_pair))
        for s in (1, 3):
            pair_parts[s] = lax.ppermute(part, "head", [(k, (k + s) % 4) for k in range(4)])
        corner_crossed = lax.ppermute(corner, "var", [(0, 1), (1, 0)])
        _, kvq, pooled = project([corner, corner_crossed], [(3, 0)], 4, 1, [*done, token])
    else:
        _, _, _, kvq, pooled, _ = project(pieces + crossed, spots, all_tiles, 1, None)
    w_mix = jnp.zeros((heads * VD, 2 * C), jnp.float32)
    for s, part in enumerate(pair_parts):
        from_head = (ours + n_head - s) % n_head
        w_mix += jnp.dot(
            lax.dynamic_slice_in_dim(w_out, from_head * width, width, 1),
            part,
            preferred_element_type=jnp.float32,
        )
    w_mix = w_mix.astype(jnp.bfloat16).reshape(heads, VD, 2 * C)
    w_mix = jnp.pad(w_mix, ((0, 0), (0, VP - VD), (0, 0)))
    table = distance_table(dist_table, mine * pair_rows, ours * pair_rows, pair_rows, pair_rows)

    chunk = min(tokens, CHUNK)

    def attend(order, dtype):
        count = order.shape[0]
        return pl.pallas_call(
            functools.partial(attend_kernel, heads, own),
            out_shape=jax.ShapeDtypeStruct((count, pair_rows, 2 * C), dtype),
            in_specs=[whole(pltpu.SMEM)] + [whole()] * 4,
            out_specs=whole(),
            scratch_shapes=[
                pltpu.VMEM((tokens // chunk, own, chunk), jnp.float32),
                pltpu.VMEM((tokens // chunk, own, chunk), jnp.float32),
                pltpu.VMEM((own, 128), jnp.float32),
                pltpu.VMEM((own, 128), jnp.float32),
                pltpu.VMEM((own, VP), jnp.float32),
            ],
            compiler_params=pltpu.CompilerParams(vmem_limit_bytes=(20 if splits == 1 else 52) * MIB),
            cost_estimate=pl.CostEstimate(
                flops=2 * count * heads * own * tokens * (2 * HD + VP),
                bytes_accessed=2 * tokens * columns,
                transcendentals=count * heads * own * tokens,
            ),
            name="attend",
        )(order.astype(jnp.int32), kvq, pooled, w_mix, w_pair)

    if splits == 1:
        sent = attend((ours + jnp.arange(1, n_head)) % n_head, jnp.bfloat16)
        last_block, table = lax.optimization_barrier((ours[None], table))
        summed = attend(last_block, jnp.float32)[0]
        for s in range(1, n_head):
            pairs = [(k, (k + s) % n_head) for k in range(n_head)]
            summed += lax.ppermute(sent[s - 1], "head", pairs).astype(jnp.float32)
        turned = lax.ppermute(
            summed[:, :C].astype(jnp.bfloat16),
            ("ctx", "head"),
            [(i * n_head + h, h * n_head + i) for i in range(n_ctx) for h in range(n_head)],
        )
        row_feats = shifts(turned, "head")
        col_feats = shifts(summed[:, C:].astype(jnp.bfloat16), "ctx")
        order = [(at + n_ctx - s) % n_ctx for at in (ours, mine) for s in range(variants)]
    else:
        blocks_here = n_ctx // splits
        part = attend((mine % splits) * blocks_here + jnp.arange(blocks_here), jnp.bfloat16)
        feats = lax.all_gather(lax.psum(part, "head"), "ctx", axis=0, tiled=False)
        feats = feats.reshape(variants, n_ctx, pair_rows, 2 * C)
        row_feats = lax.dynamic_index_in_dim(feats, mine, 1, keepdims=False)[:, :, :C]
        col_feats = lax.dynamic_index_in_dim(feats, ours, 1, keepdims=False)[:, :, C:]
        row_feats, col_feats = list(row_feats), list(col_feats)
        order = list(range(variants)) * 2

    return pl.pallas_call(
        functools.partial(pair_kernel, variants),
        out_shape=jax.ShapeDtypeStruct((variants, pair_rows, pair_rows, C), jnp.bfloat16),
        in_specs=[whole(pltpu.SMEM)] + [whole()] * (1 + 2 * variants),
        out_specs=whole(pl.ANY),
        scratch_shapes=[
            pltpu.VMEM((variants, pair_rows, C), jnp.float32),
            pltpu.VMEM((variants, pair_rows, C), jnp.bfloat16),
            pltpu.VMEM((2, variants, ROWS, pair_rows, C), jnp.bfloat16),
            pltpu.SemaphoreType.DMA((2, variants)),
        ],
        compiler_params=pltpu.CompilerParams(vmem_limit_bytes=24 * MIB),
        name="pair_map",
    )(jnp.stack(order).astype(jnp.int32) if splits == 1 else jnp.array(order, jnp.int32),
      table, *row_feats, *col_feats)


def solution(mesh):
    in_specs = (
        P("ctx", "head"),
        P("var", None),
        P(None, "head"),
        P("head"),
        P(None, "head"),
        P("head", None),
        P("head", None),
        P(),
    )
    out_specs = P("var", "ctx", "head", None)
    return jax.shard_map(local, mesh=mesh, in_specs=in_specs, out_specs=out_specs, check_vma=False)
```

```python
import functools
import math

import jax
import jax.numpy as jnp
from jax import lax
from jax.experimental import pallas as pl
from jax.experimental.pallas import tpu as pltpu
from jax.sharding import PartitionSpec as P

HD = 128
VD = 192
VP = 256
C = 128
NB = 16
POOL = 4
WIN = 160
ALIGN = 32
CHUNK = 512
SHIFTS = 16
ROWS = 16
MIB = 1024 * 1024
QSCALE = math.log2(math.e) / math.sqrt(HD)
GELU_A = math.sqrt(2.0 / math.pi)
GELU_B = GELU_A * 0.044715


def trunk_of(taps, low, middle, high):
    convolved = taps[0:1] * low + taps[1:2] * middle + taps[2:3] * high + taps[3:4]
    half = 0.5 * convolved
    bent = jnp.tanh(convolved * (GELU_A + GELU_B * (convolved * convolved)))
    return middle + (half + half * bent)


def pool_matrix(count):
    wide = lax.broadcasted_iota(jnp.int32, (count // POOL, count), 1) // POOL
    tall = lax.broadcasted_iota(jnp.int32, (count // POOL, count), 0)
    return jnp.where(wide == tall, 1.0 / POOL, 0.0).astype(jnp.bfloat16)


def project_kernel(heads, n_var, n_head, count, scalars, w_proj, *refs):
    taps, pieces = refs[:n_head], refs[n_head : n_head + 2 * count]
    out, pooled_out, given, weights, rows, left, right, sems = refs[n_head + 2 * count :]
    step, width = pieces[0].shape[1:]
    tokens = rows.shape[1] - 2 * step
    size = step // POOL
    ours, core, first, last = (scalars[k] for k in range(4))

    given_copy = pltpu.make_async_copy(w_proj, given, sems.at[2 * count, 0])
    given_copy.start()
    copies = []
    for index, piece in enumerate(pieces):
        half = core if index < count else 1 - core
        at = pl.multiple_of((scalars[4 + index % count] * n_var + half + 1) * step, step)
        for s in range(n_head):
            copy = pltpu.make_async_copy(
                piece.at[s], rows.at[s, pl.ds(at, step)], sems.at[index, s]
            )
            copy.start()
            copies.append(copy)
    rows[:, 0:step] = jnp.zeros((n_head, step, width), jnp.bfloat16)
    rows[:, tokens + step :] = jnp.zeros((n_head, step, width), jnp.bfloat16)
    columns = weights.shape[1]
    given_copy.wait()
    for s, back in enumerate(head_order(n_head)):
        source = pl.ds(pl.multiple_of(lax.rem(ours + n_head - back, n_head) * width, ALIGN), width)
        into = slice(s * width, (s + 1) * width)
        for h in range(heads):
            low, key, value = h * (2 * HD + VD), h * HD, heads * HD + h * VP
            query = heads * (HD + VP) + h * HD
            weights[into, key : key + HD] = given[source, low + HD : low + 2 * HD]
            weights[into, value : value + VD] = given[source, low + 2 * HD : low + 2 * HD + VD]
            weights[into, value + VD : value + VP] = jnp.zeros((width, VP - VD), jnp.bfloat16)
            weights[into, query : query + HD] = given[source, low : low + HD]
    at = lax.broadcasted_iota(jnp.int32, (1, columns), 1)
    ones = jnp.zeros((1, columns), jnp.float32)
    scale = jnp.where(at >= heads * (HD + VP), QSCALE, 1.0)
    for h in range(heads):
        ones = jnp.where(at == heads * HD + h * VP + VD, 1.0, ones)
    low_taps = [tap[...].astype(jnp.bfloat16) for tap in taps]
    for copy in copies:
        copy.wait()

    def make(stage, into):
        for part in range(2):
            start = (stage * 2 + part) * step
            for s in range(n_head):
                into[part * step : (part + 1) * step, s * width : (s + 1) * width] = trunk_of(
                    low_taps[s],
                    *(
                        rows[s, pl.ds(pl.multiple_of(start + shift, step), step), :]
                        for shift in (0, step, 2 * step)
                    ),
                )

    def product_of(block):
        product = jnp.dot(block, weights[...], preferred_element_type=jnp.float32)
        return (product * scale + ones).astype(jnp.bfloat16)

    def project(stage, block):
        product = product_of(block[...])
        for part in range(2):
            at = stage * 2 + part
            rows_here = slice(part * step, (part + 1) * step)
            out[pl.ds(pl.multiple_of(at * step, step), step)] = product[rows_here]
            pooled_out[pl.ds(pl.multiple_of(at * size, size), size)] = jnp.dot(
                pool_matrix(step), block[rows_here, 0:width], preferred_element_type=jnp.float32
            )

    def window(index):
        start = (first // ALIGN) * ALIGN + (index - 1) * step
        return pl.multiple_of(jnp.clip(start, 0, tokens - WIN), ALIGN)

    def make_windows(into):
        for index in range(3):
            start = window(index)
            at = start + lax.broadcasted_iota(jnp.int32, (WIN, 1), 0)
            kept = [
                jnp.where(
                    jnp.logical_or(at + shift < first, at + shift >= last), 1.0, 0.0
                ).astype(jnp.bfloat16)
                for shift in (-step, 0, step)
            ]
            for s in range(n_head):
                into[index * WIN : (index + 1) * WIN, s * width : (s + 1) * width] = trunk_of(
                    low_taps[s],
                    *(
                        rows[s, pl.ds(pl.multiple_of(start + shift, ALIGN), WIN), :] * keep
                        for shift, keep in zip((0, step, 2 * step), kept)
                    ),
                )

    stages = tokens // (2 * step)
    make(0, left)

    def two_stages(n, carry):
        make(2 * n + 1, right)
        project(2 * n, left)
        make(2 * n + 2, left)
        project(2 * n + 1, right)
        return carry

    if stages > 2:
        lax.fori_loop(0, stages // 2 - 1, two_stages, 0)
    make(stages - 1, right)
    project(stages - 2, left)
    make_windows(left)
    project(stages - 1, right)
    product = product_of(left[0 : 3 * WIN])
    for index in range(3):
        rows_here = slice(index * WIN, (index + 1) * WIN)
        out[pl.ds(window(index), WIN)] = product[rows_here]
        small = pl.multiple_of(window(index) // POOL, ALIGN // POOL)
        pooled_out[pl.ds(small, WIN // POOL)] = jnp.dot(
            pool_matrix(WIN), left[rows_here, 0:width], preferred_element_type=jnp.float32
        )


def attend_kernel(
    heads, own, order, kvq, pooled, w_mix, w_pair,
    out, scores_a, scores_b, top_a, top_b, total,
):
    tokens = kvq.shape[0]
    chunk = scores_a.shape[2]
    steps = tokens // chunk
    key_cols, value_cols = heads * HD, heads * (HD + VP)
    pool = pool_matrix(own)
    scores, tops = (scores_a, scores_b), (top_a, top_b)
    chains = [(n, h) for n in range(out.shape[0]) for h in range(heads)]

    def score(index, c):
        n, h = chains[index]
        low = value_cols + h * HD
        found = lax.dot_general(
            kvq[pl.ds(pl.multiple_of(order[n] * own, own), own), low : low + HD],
            kvq[pl.ds(pl.multiple_of(c * chunk, chunk), chunk), h * HD : (h + 1) * HD],
            (((1,), (1,)), ((), ())),
            preferred_element_type=jnp.float32,
        )
        scores[index % 2][c] = found
        best = found[:, 0:128]
        for low in range(128, chunk, 128):
            best = jnp.maximum(best, found[:, low : low + 128])
        top = tops[index % 2]
        top[...] = jnp.maximum(top[...], best)

    def clear(index):
        tops[index % 2][...] = jnp.full(top_a.shape, -jnp.inf, jnp.float32)

    clear(0)

    def first_scores(c, carry):
        score(0, c)
        return carry

    lax.fori_loop(0, steps, first_scores, 0)
    for index, (n, h) in enumerate(chains):
        more = index + 1 < len(chains)
        if more:
            clear(index + 1)
        row_max = jnp.max(tops[index % 2][...], axis=1, keepdims=True)
        total[...] = jnp.zeros(total.shape, jnp.float32)
        low = key_cols + h * VP

        def weigh(c, carry):
            weights = jnp.exp2((scores[index % 2][c] - row_max).astype(jnp.bfloat16))
            if more:
                score(index + 1, c)
            total[...] += jnp.dot(
                weights,
                kvq[pl.ds(pl.multiple_of(c * chunk, chunk), chunk), low : low + VP],
                preferred_element_type=jnp.float32,
            )
            return carry

        lax.fori_loop(0, steps, weigh, 0)
        mixed = total[...]
        mixed = (mixed * (1.0 / mixed[:, VD : VD + 1])).astype(jnp.bfloat16)
        mixed = jnp.dot(pool, mixed, preferred_element_type=jnp.float32).astype(jnp.bfloat16)
        if h == 0:
            size = own // POOL
            pair = jnp.dot(
                pooled[pl.ds(pl.multiple_of(order[n] * size, size), size)].astype(jnp.bfloat16),
                w_pair[...],
                preferred_element_type=jnp.float32,
            )
        pair = pair + jnp.dot(mixed, w_mix[h], preferred_element_type=jnp.float32)
        if h == heads - 1:
            out[n] = pair.astype(out.dtype)


def pair_kernel(variants, order, table, *refs):
    row_feats = refs[:variants]
    col_feats = refs[variants : 2 * variants]
    out, rows, cols, blocks, sems = refs[2 * variants :]
    side = cols.shape[1]
    count = rows.shape[1]
    for s in range(variants):
        rows[order[s]] = row_feats[s][...].astype(jnp.float32)
        cols[order[variants + s]] = col_feats[s][...]

    def write(block, slot, variant):
        into = out.at[variant, pl.ds(block * ROWS, ROWS)]
        return pltpu.make_async_copy(blocks.at[slot, variant], into, sems.at[slot, variant])

    def one_block(block, carry):
        slot = lax.rem(block, 2)
        for variant in range(variants):
            pl.when(block >= 2)(write(block, slot, variant).wait)
            for r in range(ROWS):
                back = count - 1 - (block * ROWS + r)
                low = pl.multiple_of((back // SHIFTS) * SHIFTS, SHIFTS)
                relative = table[(count - 1 - r) % SHIFTS, pl.ds(low, side), :]
                row = rows[variant, pl.ds(block * ROWS + r, 1), :]
                row = jnp.broadcast_to(row, (SHIFTS, C)).astype(jnp.bfloat16)
                found = (cols[variant] + relative).reshape(side // SHIFTS, SHIFTS, C) + row[None]
                blocks[slot, variant, r] = found.reshape(side, C)
            write(block, slot, variant).start()
        return carry

    total = count // ROWS
    lax.fori_loop(0, total, one_block, 0)
    for block in range(max(total - 2, 0), total):
        for variant in range(variants):
            write(block, block % 2, variant).wait()


def distance_table(dist_table, row_start, col_start, rows, cols):
    at = jnp.arange(SHIFTS, dtype=jnp.int32)[:, None] + jnp.arange(
        rows + cols, dtype=jnp.int32
    )
    distance = jnp.abs(row_start - col_start + rows - 1 - at)
    buckets = jnp.zeros(distance.shape, jnp.int32)
    for power_index in range(NB - 1):
        buckets = buckets + (distance >= 2**power_index).astype(jnp.int32)
    one_hot = (buckets[:, :, None] == jnp.arange(NB, dtype=jnp.int32)).astype(jnp.float32)
    return jnp.einsum("skb,bc->skc", one_hot, dist_table, precision=lax.Precision.HIGHEST).astype(
        jnp.bfloat16
    )


def whole(memory=pltpu.VMEM):
    return pl.BlockSpec(memory_space=memory)


def shifts(array, axis):
    size = lax.axis_size(axis)
    return [array] + [
        lax.ppermute(array, axis, [(k, (k + s) % size) for k in range(size)])
        for s in range(1, size)
    ]


def head_order(n_head):
    return [0, 1, 3, 2] if n_head == 4 else list(range(n_head))


def gather_rows(block, taps, n_ctx, n_var, n_head, core):
    crossing = lambda array: lax.ppermute(array, "var", [(0, 1), (1, 0)])
    if n_ctx == 4 and n_head == 4 and n_var == 2:
        shift = lambda array, s: lax.ppermute(array, "head", [(k, (k + s) % 4) for k in range(4)])
        over = lambda array, bit: lax.ppermute(array, "ctx", [(k, k ^ bit) for k in range(4)])
        near = jnp.stack([block, shift(block, 1), shift(block, 3)])
        far = shift(block, 2)[None]
        slab, over_x, over_y = (
            jnp.concatenate(pair)
            for pair in (
                (near, far), (over(near, 1), over(far, 1)), (over(near, 2), over(far, 2))
            )
        )
        pairs = [(2 * k + c, 2 * (k ^ (c + 1)) + c) for k in range(4) for c in range(2)]
        corner = lax.ppermute(jnp.where(core == 0, over_y, over_x), ("ctx", "var"), pairs)
        pieces = [slab, over_x, over_y]
        corner, crossed, taps = lax.optimization_barrier(
            (corner, [crossing(piece) for piece in pieces], shifts(taps, "head"))
        )
        return pieces + [corner], crossed + [crossing(corner)], taps
    pieces = shifts(jnp.stack(shifts(block, "head")), "ctx")
    crossed = [crossing(piece) for piece in pieces]
    return pieces, crossed, shifts(taps, "head")


def local(sequence, deletions, conv_taps, conv_bias, w_proj, w_out, w_pair, dist_table):
    own, width = sequence.shape
    variants = deletions.shape[0]
    heads = w_out.shape[0] // VD
    n_ctx, n_head, n_var = (lax.axis_size(name) for name in ("ctx", "head", "var"))
    if n_ctx != n_head or n_var != 2 or n_ctx % variants:
        raise ValueError("mesh shape")
    step = own // n_var
    tokens = n_ctx * own
    pair_rows = own // POOL
    columns = heads * (2 * HD + VP)
    splits = n_ctx // variants
    mine, ours, core = (lax.axis_index(name) for name in ("ctx", "head", "var"))

    half = lax.dynamic_slice_in_dim(sequence, core * step, step, 0)
    taps = jnp.concatenate([conv_taps, conv_bias[None]], 0)
    pieces, crossed, taps = gather_rows(half, taps, n_ctx, n_var, n_head, core)
    if n_ctx == 4 and n_head == 4:
        blocks = [mine, mine ^ 1, mine ^ 2, mine ^ 3]
    else:
        blocks = [(mine + n_ctx - s) % n_ctx for s in range(n_ctx)]
    scalars = jnp.concatenate(
        [
            jnp.stack([ours, core]).astype(jnp.int32),
            lax.dynamic_index_in_dim(deletions, mine // splits, 0, keepdims=False),
            jnp.stack(blocks).astype(jnp.int32),
        ]
    )
    kvq, pooled = pl.pallas_call(
        functools.partial(project_kernel, heads, n_var, n_head, len(pieces)),
        out_shape=(
            jax.ShapeDtypeStruct((tokens, columns), jnp.bfloat16),
            jax.ShapeDtypeStruct((tokens // POOL, width), jnp.float32),
        ),
        in_specs=[whole(pltpu.SMEM), whole(pltpu.HBM)]
        + [whole()] * n_head
        + [whole(pltpu.HBM)] * (2 * len(pieces)),
        out_specs=(whole(), whole()),
        scratch_shapes=[
            pltpu.VMEM(w_proj.shape, jnp.bfloat16),
            pltpu.VMEM((n_head * width, columns), jnp.bfloat16),
            pltpu.VMEM((n_head, tokens + 2 * step, width), jnp.bfloat16),
            pltpu.VMEM((2 * step, n_head * width), jnp.bfloat16),
            pltpu.VMEM((2 * step, n_head * width), jnp.bfloat16),
            pltpu.SemaphoreType.DMA((2 * len(pieces) + 1, n_head)),
        ],
        compiler_params=pltpu.CompilerParams(vmem_limit_bytes=(34 if splits == 1 else 52) * MIB),
        cost_estimate=pl.CostEstimate(
            flops=2 * (tokens + 3 * WIN) * n_head * width * columns,
            bytes_accessed=4 * tokens * n_head * width,
            transcendentals=tokens * n_head * width,
        ),
        name="project",
    )(
        scalars, w_proj, *(taps[s] for s in head_order(n_head)), *pieces, *crossed
    )
    pair_parts, pooled = lax.optimization_barrier((shifts(w_pair, "head"), pooled))
    w_mix = jnp.zeros((heads * VD, 2 * C), jnp.float32)
    for s, part in enumerate(pair_parts):
        from_head = (ours + n_head - s) % n_head
        w_mix += jnp.dot(
            lax.dynamic_slice_in_dim(w_out, from_head * width, width, 1),
            part,
            preferred_element_type=jnp.float32,
        )
    w_mix = w_mix.astype(jnp.bfloat16).reshape(heads, VD, 2 * C)
    w_mix = jnp.pad(w_mix, ((0, 0), (0, VP - VD), (0, 0)))
    table = distance_table(dist_table, mine * pair_rows, ours * pair_rows, pair_rows, pair_rows)

    chunk = min(tokens, CHUNK)

    def attend(order, dtype):
        count = order.shape[0]
        return pl.pallas_call(
            functools.partial(attend_kernel, heads, own),
            out_shape=jax.ShapeDtypeStruct((count, pair_rows, 2 * C), dtype),
            in_specs=[whole(pltpu.SMEM)] + [whole()] * 4,
            out_specs=whole(),
            scratch_shapes=[
                pltpu.VMEM((tokens // chunk, own, chunk), jnp.float32),
                pltpu.VMEM((tokens // chunk, own, chunk), jnp.float32),
                pltpu.VMEM((own, 128), jnp.float32),
                pltpu.VMEM((own, 128), jnp.float32),
                pltpu.VMEM((own, VP), jnp.float32),
            ],
            compiler_params=pltpu.CompilerParams(vmem_limit_bytes=(20 if splits == 1 else 52) * MIB),
            cost_estimate=pl.CostEstimate(
                flops=2 * count * heads * own * tokens * (2 * HD + VP),
                bytes_accessed=2 * tokens * columns,
                transcendentals=count * heads * own * tokens,
            ),
            name="attend",
        )(order.astype(jnp.int32), kvq, pooled, w_mix, w_pair)

    if splits == 1:
        sent = attend((ours + jnp.arange(1, n_head)) % n_head, jnp.bfloat16)
        last_block, table = lax.optimization_barrier((ours[None], table))
        summed = attend(last_block, jnp.float32)[0]
        for s in range(1, n_head):
            pairs = [(k, (k + s) % n_head) for k in range(n_head)]
            summed += lax.ppermute(sent[s - 1], "head", pairs).astype(jnp.float32)
        turned = lax.ppermute(
            summed[:, :C].astype(jnp.bfloat16),
            ("ctx", "head"),
            [(i * n_head + h, h * n_head + i) for i in range(n_ctx) for h in range(n_head)],
        )
        row_feats = shifts(turned, "head")
        col_feats = shifts(summed[:, C:].astype(jnp.bfloat16), "ctx")
        order = [(at + n_ctx - s) % n_ctx for at in (ours, mine) for s in range(variants)]
    else:
        blocks_here = n_ctx // splits
        part = attend((mine % splits) * blocks_here + jnp.arange(blocks_here), jnp.bfloat16)
        feats = lax.all_gather(lax.psum(part, "head"), "ctx", axis=0, tiled=False)
        feats = feats.reshape(variants, n_ctx, pair_rows, 2 * C)
        row_feats = lax.dynamic_index_in_dim(feats, mine, 1, keepdims=False)[:, :, :C]
        col_feats = lax.dynamic_index_in_dim(feats, ours, 1, keepdims=False)[:, :, C:]
        row_feats, col_feats = list(row_feats), list(col_feats)
        order = list(range(variants)) * 2

    return pl.pallas_call(
        functools.partial(pair_kernel, variants),
        out_shape=jax.ShapeDtypeStruct((variants, pair_rows, pair_rows, C), jnp.bfloat16),
        in_specs=[whole(pltpu.SMEM)] + [whole()] * (1 + 2 * variants),
        out_specs=whole(pl.ANY),
        scratch_shapes=[
            pltpu.VMEM((variants, pair_rows, C), jnp.float32),
            pltpu.VMEM((variants, pair_rows, C), jnp.bfloat16),
            pltpu.VMEM((2, variants, ROWS, pair_rows, C), jnp.bfloat16),
            pltpu.SemaphoreType.DMA((2, variants)),
        ],
        compiler_params=pltpu.CompilerParams(vmem_limit_bytes=24 * MIB),
        name="pair_map",
    )(jnp.stack(order).astype(jnp.int32) if splits == 1 else jnp.array(order, jnp.int32),
      table, *row_feats, *col_feats)


def solution(mesh):
    in_specs = (
        P("ctx", "head"),
        P("var", None),
        P(None, "head"),
        P("head"),
        P(None, "head"),
        P("head", None),
        P("head", None),
        P(),
    )
    out_specs = P("var", "ctx", "head", None)
    return jax.shard_map(local, mesh=mesh, in_specs=in_specs, out_specs=out_specs, check_vma=False)
```

```python
import functools
import math

import jax
import jax.numpy as jnp
from jax import lax
from jax.experimental import pallas as pl
from jax.experimental.pallas import tpu as pltpu
from jax.sharding import PartitionSpec as P

HD = 128
VD = 192
VP = 256
C = 128
NB = 16
POOL = 4
WIN = 160
ALIGN = 32
CHUNK = 512
SHIFTS = 16
ROWS = 16
MIB = 1024 * 1024
QSCALE = math.log2(math.e) / math.sqrt(HD)
GELU_A = math.sqrt(2.0 / math.pi)
GELU_B = GELU_A * 0.044715


def trunk_of(taps, low, middle, high):
    convolved = taps[0:1] * low + taps[1:2] * middle + taps[2:3] * high + taps[3:4]
    half = 0.5 * convolved
    bent = jnp.tanh(convolved * (GELU_A + GELU_B * (convolved * convolved)))
    return middle + (half + half * bent)


def pool_matrix(count):
    wide = lax.broadcasted_iota(jnp.int32, (count // POOL, count), 1) // POOL
    tall = lax.broadcasted_iota(jnp.int32, (count // POOL, count), 0)
    return jnp.where(wide == tall, 1.0 / POOL, 0.0).astype(jnp.bfloat16)


def project_kernel(heads, n_var, n_head, count, scalars, w_proj, *refs):
    taps, pieces = refs[:n_head], refs[n_head : n_head + 2 * count]
    out, pooled_out, given, weights, rows, left, right, sems = refs[n_head + 2 * count :]
    step, width = pieces[0].shape[1:]
    tokens = rows.shape[1] - 2 * step
    size = step // POOL
    ours, core, first, last = (scalars[k] for k in range(4))

    given_copy = pltpu.make_async_copy(w_proj, given, sems.at[2 * count, 0])
    given_copy.start()
    copies = []
    for index, piece in enumerate(pieces):
        half = core if index < count else 1 - core
        at = pl.multiple_of((scalars[4 + index % count] * n_var + half + 1) * step, step)
        for s in range(n_head):
            copy = pltpu.make_async_copy(
                piece.at[s], rows.at[s, pl.ds(at, step)], sems.at[index, s]
            )
            copy.start()
            copies.append(copy)
    rows[:, 0:step] = jnp.zeros((n_head, step, width), jnp.bfloat16)
    rows[:, tokens + step :] = jnp.zeros((n_head, step, width), jnp.bfloat16)
    columns = weights.shape[1]
    given_copy.wait()
    for s, back in enumerate(head_order(n_head)):
        source = pl.ds(pl.multiple_of(lax.rem(ours + n_head - back, n_head) * width, ALIGN), width)
        into = slice(s * width, (s + 1) * width)
        for h in range(heads):
            low, key, value = h * (2 * HD + VD), h * HD, heads * HD + h * VP
            query = heads * (HD + VP) + h * HD
            weights[into, key : key + HD] = given[source, low + HD : low + 2 * HD]
            weights[into, value : value + VD] = given[source, low + 2 * HD : low + 2 * HD + VD]
            weights[into, value + VD : value + VP] = jnp.zeros((width, VP - VD), jnp.bfloat16)
            weights[into, query : query + HD] = given[source, low : low + HD]
    at = lax.broadcasted_iota(jnp.int32, (1, columns), 1)
    ones = jnp.zeros((1, columns), jnp.float32)
    scale = jnp.where(at >= heads * (HD + VP), QSCALE, 1.0)
    for h in range(heads):
        ones = jnp.where(at == heads * HD + h * VP + VD, 1.0, ones)
    low_taps = [tap[...].astype(jnp.bfloat16) for tap in taps]
    for copy in copies:
        copy.wait()

    def make(stage, into):
        for part in range(2):
            start = (stage * 2 + part) * step
            for s in range(n_head):
                into[part * step : (part + 1) * step, s * width : (s + 1) * width] = trunk_of(
                    low_taps[s],
                    *(
                        rows[s, pl.ds(pl.multiple_of(start + shift, step), step), :]
                        for shift in (0, step, 2 * step)
                    ),
                )

    def product_of(block):
        product = jnp.dot(block, weights[...], preferred_element_type=jnp.float32)
        return (product * scale + ones).astype(jnp.bfloat16)

    def project(stage, block):
        product = product_of(block[...])
        for part in range(2):
            at = stage * 2 + part
            rows_here = slice(part * step, (part + 1) * step)
            out[pl.ds(pl.multiple_of(at * step, step), step)] = product[rows_here]
            pooled_out[pl.ds(pl.multiple_of(at * size, size), size)] = jnp.dot(
                pool_matrix(step), block[rows_here, 0:width], preferred_element_type=jnp.float32
            )

    def window(index):
        start = (first // ALIGN) * ALIGN + (index - 1) * step
        return pl.multiple_of(jnp.clip(start, 0, tokens - WIN), ALIGN)

    def make_windows(into):
        for index in range(3):
            start = window(index)
            at = start + lax.broadcasted_iota(jnp.int32, (WIN, 1), 0)
            kept = [
                jnp.where(
                    jnp.logical_or(at + shift < first, at + shift >= last), 1.0, 0.0
                ).astype(jnp.bfloat16)
                for shift in (-step, 0, step)
            ]
            for s in range(n_head):
                into[index * WIN : (index + 1) * WIN, s * width : (s + 1) * width] = trunk_of(
                    low_taps[s],
                    *(
                        rows[s, pl.ds(pl.multiple_of(start + shift, ALIGN), WIN), :] * keep
                        for shift, keep in zip((0, step, 2 * step), kept)
                    ),
                )

    stages = tokens // (2 * step)
    make(0, left)

    def two_stages(n, carry):
        make(2 * n + 1, right)
        project(2 * n, left)
        make(2 * n + 2, left)
        project(2 * n + 1, right)
        return carry

    if stages > 2:
        lax.fori_loop(0, stages // 2 - 1, two_stages, 0)
    make(stages - 1, right)
    project(stages - 2, left)
    make_windows(left)
    project(stages - 1, right)
    product = product_of(left[0 : 3 * WIN])
    for index in range(3):
        rows_here = slice(index * WIN, (index + 1) * WIN)
        out[pl.ds(window(index), WIN)] = product[rows_here]
        small = pl.multiple_of(window(index) // POOL, ALIGN // POOL)
        pooled_out[pl.ds(small, WIN // POOL)] = jnp.dot(
            pool_matrix(WIN), left[rows_here, 0:width], preferred_element_type=jnp.float32
        )


def attend_kernel(heads, own, given, order, kvq, pooled, *refs):
    mixing, out = refs[:given], refs[given]
    *mix_out, scores_a, scores_b, top_a, top_b, total, parts = refs[given + 1 :]
    if mix_out:
        w_out, w_pair = mixing[:2]
        (w_mix,) = mix_out
        width = w_pair.shape[0]
        for s in range(given - 1):
            parts[order[out.shape[0] + s]] = mixing[1 + s][...]
        for h in range(heads):
            mix = jnp.zeros((VD, w_pair.shape[1]), jnp.float32)
            for k in range(given - 1):
                mix += jnp.dot(
                    w_out[h * VD : (h + 1) * VD, k * width : (k + 1) * width],
                    parts[k],
                    preferred_element_type=jnp.float32,
                )
            w_mix[h, 0:VD] = mix.astype(jnp.bfloat16)
            w_mix[h, VD:] = jnp.zeros((VP - VD, w_pair.shape[1]), jnp.bfloat16)
    else:
        w_mix, w_pair = mixing
    tokens = kvq.shape[0]
    chunk = scores_a.shape[2]
    steps = tokens // chunk
    key_cols, value_cols = heads * HD, heads * (HD + VP)
    pool = pool_matrix(own)
    scores, tops = (scores_a, scores_b), (top_a, top_b)
    chains = [(n, h) for n in range(out.shape[0]) for h in range(heads)]

    def score(index, c):
        n, h = chains[index]
        low = value_cols + h * HD
        found = lax.dot_general(
            kvq[pl.ds(pl.multiple_of(order[n] * own, own), own), low : low + HD],
            kvq[pl.ds(pl.multiple_of(c * chunk, chunk), chunk), h * HD : (h + 1) * HD],
            (((1,), (1,)), ((), ())),
            preferred_element_type=jnp.float32,
        )
        scores[index % 2][c] = found
        best = found[:, 0:128]
        for low in range(128, chunk, 128):
            best = jnp.maximum(best, found[:, low : low + 128])
        top = tops[index % 2]
        top[...] = jnp.maximum(top[...], best)

    def clear(index):
        tops[index % 2][...] = jnp.full(top_a.shape, -jnp.inf, jnp.float32)

    clear(0)

    def first_scores(c, carry):
        score(0, c)
        return carry

    lax.fori_loop(0, steps, first_scores, 0)
    for index, (n, h) in enumerate(chains):
        more = index + 1 < len(chains)
        if more:
            clear(index + 1)
        row_max = jnp.max(tops[index % 2][...], axis=1, keepdims=True)
        total[...] = jnp.zeros(total.shape, jnp.float32)
        low = key_cols + h * VP

        def weigh(c, carry):
            weights = jnp.exp2((scores[index % 2][c] - row_max).astype(jnp.bfloat16))
            if more:
                score(index + 1, c)
            total[...] += jnp.dot(
                weights,
                kvq[pl.ds(pl.multiple_of(c * chunk, chunk), chunk), low : low + VP],
                preferred_element_type=jnp.float32,
            )
            return carry

        lax.fori_loop(0, steps, weigh, 0)
        mixed = total[...]
        mixed = (mixed * (1.0 / mixed[:, VD : VD + 1])).astype(jnp.bfloat16)
        mixed = jnp.dot(pool, mixed, preferred_element_type=jnp.float32).astype(jnp.bfloat16)
        if h == 0:
            size = own // POOL
            pair = jnp.dot(
                pooled[pl.ds(pl.multiple_of(order[n] * size, size), size)].astype(jnp.bfloat16),
                w_pair[...],
                preferred_element_type=jnp.float32,
            )
        pair = pair + jnp.dot(mixed, w_mix[h], preferred_element_type=jnp.float32)
        if h == heads - 1:
            out[n] = pair.astype(out.dtype)


def pair_kernel(variants, order, table, *refs):
    row_feats = refs[:variants]
    col_feats = refs[variants : 2 * variants]
    out, rows, cols, blocks, sems = refs[2 * variants :]
    side = cols.shape[1]
    count = rows.shape[1]
    for s in range(variants):
        rows[order[s]] = row_feats[s][...].astype(jnp.float32)
        cols[order[variants + s]] = col_feats[s][...]

    def write(block, slot, variant):
        into = out.at[variant, pl.ds(block * ROWS, ROWS)]
        return pltpu.make_async_copy(blocks.at[slot, variant], into, sems.at[slot, variant])

    def one_block(block, carry):
        slot = lax.rem(block, 2)
        for variant in range(variants):
            pl.when(block >= 2)(write(block, slot, variant).wait)
            for r in range(ROWS):
                back = count - 1 - (block * ROWS + r)
                low = pl.multiple_of((back // SHIFTS) * SHIFTS, SHIFTS)
                relative = table[(count - 1 - r) % SHIFTS, pl.ds(low, side), :]
                row = rows[variant, pl.ds(block * ROWS + r, 1), :]
                row = jnp.broadcast_to(row, (SHIFTS, C)).astype(jnp.bfloat16)
                found = (cols[variant] + relative).reshape(side // SHIFTS, SHIFTS, C) + row[None]
                blocks[slot, variant, r] = found.reshape(side, C)
            write(block, slot, variant).start()
        return carry

    total = count // ROWS
    lax.fori_loop(0, total, one_block, 0)
    for block in range(max(total - 2, 0), total):
        for variant in range(variants):
            write(block, block % 2, variant).wait()


def distance_table(dist_table, row_start, col_start, rows, cols):
    at = jnp.arange(SHIFTS, dtype=jnp.int32)[:, None] + jnp.arange(
        rows + cols, dtype=jnp.int32
    )
    distance = jnp.abs(row_start - col_start + rows - 1 - at)
    buckets = jnp.zeros(distance.shape, jnp.int32)
    for power_index in range(NB - 1):
        buckets = buckets + (distance >= 2**power_index).astype(jnp.int32)
    one_hot = (buckets[:, :, None] == jnp.arange(NB, dtype=jnp.int32)).astype(jnp.float32)
    return jnp.einsum("skb,bc->skc", one_hot, dist_table, precision=lax.Precision.HIGHEST).astype(
        jnp.bfloat16
    )


def in_hbm(array):
    return pltpu.with_memory_space_constraint(array, pltpu.HBM)


def whole(memory=pltpu.VMEM):
    return pl.BlockSpec(memory_space=memory)


def shifts(array, axis):
    size = lax.axis_size(axis)
    return [array] + [
        lax.ppermute(array, axis, [(k, (k + s) % size) for k in range(size)])
        for s in range(1, size)
    ]


def head_order(n_head):
    return [0, 1, 3, 2] if n_head == 4 else list(range(n_head))


def gather_rows(block, taps, n_ctx, n_var, n_head, core):
    crossing = lambda array: lax.ppermute(array, "var", [(0, 1), (1, 0)])
    if n_ctx == 4 and n_head == 4 and n_var == 2:
        shift = lambda array, s: lax.ppermute(array, "head", [(k, (k + s) % 4) for k in range(4)])
        over = lambda array, bit: lax.ppermute(array, "ctx", [(k, k ^ bit) for k in range(4)])
        near = jnp.stack([block, shift(block, 1), shift(block, 3)])
        far = shift(block, 2)[None]
        slab, over_x, over_y = (
            jnp.concatenate(pair)
            for pair in (
                (near, far), (over(near, 1), over(far, 1)), (over(near, 2), over(far, 2))
            )
        )
        pairs = [(2 * k + c, 2 * (k ^ (c + 1)) + c) for k in range(4) for c in range(2)]
        corner = lax.ppermute(jnp.where(core == 0, over_y, over_x), ("ctx", "var"), pairs)
        pieces = [slab, over_x, over_y]
        corner, crossed, taps = lax.optimization_barrier(
            (corner, [crossing(piece) for piece in pieces], shifts(taps, "head"))
        )
        return pieces + [corner], crossed + [crossing(corner)], taps
    pieces = shifts(jnp.stack(shifts(block, "head")), "ctx")
    crossed = [crossing(piece) for piece in pieces]
    return pieces, crossed, shifts(taps, "head")


def local(sequence, deletions, conv_taps, conv_bias, w_proj, w_out, w_pair, dist_table):
    own, width = sequence.shape
    variants = deletions.shape[0]
    heads = w_out.shape[0] // VD
    n_ctx, n_head, n_var = (lax.axis_size(name) for name in ("ctx", "head", "var"))
    if n_ctx != n_head or n_var != 2 or n_ctx % variants:
        raise ValueError("mesh shape")
    step = own // n_var
    tokens = n_ctx * own
    pair_rows = own // POOL
    columns = heads * (2 * HD + VP)
    splits = n_ctx // variants
    mine, ours, core = (lax.axis_index(name) for name in ("ctx", "head", "var"))

    half = lax.dynamic_slice_in_dim(sequence, core * step, step, 0)
    taps = jnp.concatenate([conv_taps, conv_bias[None]], 0)
    pieces, crossed, taps = gather_rows(half, taps, n_ctx, n_var, n_head, core)
    if n_ctx == 4 and n_head == 4:
        blocks = [mine, mine ^ 1, mine ^ 2, mine ^ 3]
    else:
        blocks = [(mine + n_ctx - s) % n_ctx for s in range(n_ctx)]
    scalars = jnp.concatenate(
        [
            jnp.stack([ours, core]).astype(jnp.int32),
            lax.dynamic_index_in_dim(deletions, mine // splits, 0, keepdims=False),
            jnp.stack(blocks).astype(jnp.int32),
        ]
    )
    kvq, pooled = pl.pallas_call(
        functools.partial(project_kernel, heads, n_var, n_head, len(pieces)),
        out_shape=(
            jax.ShapeDtypeStruct((tokens, columns), jnp.bfloat16),
            jax.ShapeDtypeStruct((tokens // POOL, width), jnp.float32),
        ),
        in_specs=[whole(pltpu.SMEM), whole(pltpu.HBM)]
        + [whole()] * n_head
        + [whole(pltpu.HBM)] * (2 * len(pieces)),
        out_specs=(whole(), whole()),
        scratch_shapes=[
            pltpu.VMEM(w_proj.shape, jnp.bfloat16),
            pltpu.VMEM((n_head * width, columns), jnp.bfloat16),
            pltpu.VMEM((n_head, tokens + 2 * step, width), jnp.bfloat16),
            pltpu.VMEM((2 * step, n_head * width), jnp.bfloat16),
            pltpu.VMEM((2 * step, n_head * width), jnp.bfloat16),
            pltpu.SemaphoreType.DMA((2 * len(pieces) + 1, n_head)),
        ],
        compiler_params=pltpu.CompilerParams(vmem_limit_bytes=(34 if splits == 1 else 52) * MIB),
        cost_estimate=pl.CostEstimate(
            flops=2 * (tokens + 3 * WIN) * n_head * width * columns,
            bytes_accessed=4 * tokens * n_head * width,
            transcendentals=tokens * n_head * width,
        ),
        name="project",
    )(
        scalars,
        in_hbm(w_proj),
        *(taps[s] for s in head_order(n_head)),
        *(in_hbm(piece) for piece in pieces + crossed),
    )
    table = distance_table(dist_table, mine * pair_rows, ours * pair_rows, pair_rows, pair_rows)

    chunk = min(tokens, CHUNK)

    pair_parts = shifts(w_pair, "head")
    order_of_parts = [(ours + n_head - s) % n_head for s in range(n_head)]

    def attend(order, dtype, w_mix):
        count = order.shape[0]
        mix_shape = jax.ShapeDtypeStruct((heads, VP, 2 * C), jnp.bfloat16)
        out_shape = [jax.ShapeDtypeStruct((count, pair_rows, 2 * C), dtype)]
        if w_mix is None:
            mixing, out_shape = [w_out, *pair_parts], out_shape + [mix_shape]
            order = jnp.concatenate([order, jnp.stack(order_of_parts)])
        else:
            mixing = [w_mix, w_pair]
        return pl.pallas_call(
            functools.partial(attend_kernel, heads, own, len(mixing)),
            out_shape=out_shape,
            in_specs=[whole(pltpu.SMEM)] + [whole()] * (2 + len(mixing)),
            out_specs=[whole()] * len(out_shape),
            scratch_shapes=[
                pltpu.VMEM((tokens // chunk, own, chunk), jnp.float32),
                pltpu.VMEM((tokens // chunk, own, chunk), jnp.float32),
                pltpu.VMEM((own, 128), jnp.float32),
                pltpu.VMEM((own, 128), jnp.float32),
                pltpu.VMEM((own, VP), jnp.float32),
                pltpu.VMEM((n_head, width, 2 * C), jnp.bfloat16),
            ],
            compiler_params=pltpu.CompilerParams(
                vmem_limit_bytes=(22 if splits == 1 else 52) * MIB
            ),
            cost_estimate=pl.CostEstimate(
                flops=2 * count * heads * own * tokens * (2 * HD + VP),
                bytes_accessed=2 * tokens * columns,
                transcendentals=count * heads * own * tokens,
            ),
            name="attend",
        )(order.astype(jnp.int32), kvq, pooled, *mixing)

    if splits == 1:
        sent, w_mix = attend((ours + jnp.arange(1, n_head)) % n_head, jnp.bfloat16, None)
        summed = attend(ours[None], jnp.float32, w_mix)[0][0]
        for s in range(1, n_head):
            pairs = [(k, (k + s) % n_head) for k in range(n_head)]
            summed += lax.ppermute(sent[s - 1], "head", pairs).astype(jnp.float32)
        turned = lax.ppermute(
            summed[:, :C].astype(jnp.bfloat16),
            ("ctx", "head"),
            [(i * n_head + h, h * n_head + i) for i in range(n_ctx) for h in range(n_head)],
        )
        row_feats = shifts(turned, "head")
        col_feats = shifts(summed[:, C:].astype(jnp.bfloat16), "ctx")
        order = [(at + n_ctx - s) % n_ctx for at in (ours, mine) for s in range(variants)]
    else:
        blocks_here = n_ctx // splits
        here = (mine % splits) * blocks_here + jnp.arange(blocks_here)
        part = attend(here, jnp.bfloat16, None)[0]
        feats = lax.all_gather(lax.psum(part, "head"), "ctx", axis=0, tiled=False)
        feats = feats.reshape(variants, n_ctx, pair_rows, 2 * C)
        row_feats = lax.dynamic_index_in_dim(feats, mine, 1, keepdims=False)[:, :, :C]
        col_feats = lax.dynamic_index_in_dim(feats, ours, 1, keepdims=False)[:, :, C:]
        row_feats, col_feats = list(row_feats), list(col_feats)
        order = list(range(variants)) * 2

    return pl.pallas_call(
        functools.partial(pair_kernel, variants),
        out_shape=jax.ShapeDtypeStruct((variants, pair_rows, pair_rows, C), jnp.bfloat16),
        in_specs=[whole(pltpu.SMEM)] + [whole()] * (1 + 2 * variants),
        out_specs=whole(pl.ANY),
        scratch_shapes=[
            pltpu.VMEM((variants, pair_rows, C), jnp.float32),
            pltpu.VMEM((variants, pair_rows, C), jnp.bfloat16),
            pltpu.VMEM((2, variants, ROWS, pair_rows, C), jnp.bfloat16),
            pltpu.SemaphoreType.DMA((2, variants)),
        ],
        compiler_params=pltpu.CompilerParams(vmem_limit_bytes=24 * MIB),
        name="pair_map",
    )(jnp.stack(order).astype(jnp.int32) if splits == 1 else jnp.array(order, jnp.int32),
      table, *row_feats, *col_feats)


def solution(mesh):
    in_specs = (
        P("ctx", "head"),
        P("var", None),
        P(None, "head"),
        P("head"),
        P(None, "head"),
        P("head", None),
        P("head", None),
        P(),
    )
    out_specs = P("var", "ctx", "head", None)
    return jax.shard_map(local, mesh=mesh, in_specs=in_specs, out_specs=out_specs, check_vma=False)
```

```python
import functools
import math

import jax
import jax.numpy as jnp
from jax import lax
from jax.experimental import pallas as pl
from jax.experimental.pallas import tpu as pltpu
from jax.sharding import PartitionSpec as P

HD = 128
VD = 192
VP = 256
C = 128
NB = 16
POOL = 4
WIN = 160
ALIGN = 32
CHUNK = 1024
SHIFTS = 16
ROWS = 16
MIB = 1024 * 1024
QSCALE = math.log2(math.e) / math.sqrt(HD)
GELU_A = math.sqrt(2.0 / math.pi)
GELU_B = GELU_A * 0.044715


def trunk_of(taps, low, middle, high):
    convolved = taps[0:1] * low + taps[1:2] * middle + taps[2:3] * high + taps[3:4]
    half = 0.5 * convolved
    bent = jnp.tanh(convolved * (GELU_A + GELU_B * (convolved * convolved)))
    return middle + (half + half * bent)


def pool_matrix(count):
    wide = lax.broadcasted_iota(jnp.int32, (count // POOL, count), 1) // POOL
    tall = lax.broadcasted_iota(jnp.int32, (count // POOL, count), 0)
    return jnp.where(wide == tall, 1.0 / POOL, 0.0).astype(jnp.bfloat16)


def project_kernel(heads, n_var, n_head, count, scalars, w_proj, *refs):
    taps, pieces = refs[:n_head], refs[n_head : n_head + 2 * count]
    out, pooled_out, given, weights, rows, left, right, sems = refs[n_head + 2 * count :]
    step, width = pieces[0].shape[1:]
    tokens = rows.shape[1] - 2 * step
    size = step // POOL
    ours, core, first, last = (scalars[k] for k in range(4))

    given_copy = pltpu.make_async_copy(w_proj, given, sems.at[2 * count, 0])
    given_copy.start()
    copies = []
    for index, piece in enumerate(pieces):
        half = core if index < count else 1 - core
        at = pl.multiple_of((scalars[4 + index % count] * n_var + half + 1) * step, step)
        for s in range(n_head):
            copy = pltpu.make_async_copy(
                piece.at[s], rows.at[s, pl.ds(at, step)], sems.at[index, s]
            )
            copy.start()
            copies.append(copy)
    rows[:, 0:step] = jnp.zeros((n_head, step, width), jnp.bfloat16)
    rows[:, tokens + step :] = jnp.zeros((n_head, step, width), jnp.bfloat16)
    columns = weights.shape[1]
    given_copy.wait()
    for s, back in enumerate(head_order(n_head)):
        source = pl.ds(pl.multiple_of(lax.rem(ours + n_head - back, n_head) * width, ALIGN), width)
        into = slice(s * width, (s + 1) * width)
        for h in range(heads):
            low, key, value = h * (2 * HD + VD), h * HD, heads * HD + h * VP
            query = heads * (HD + VP) + h * HD
            weights[into, key : key + HD] = given[source, low + HD : low + 2 * HD]
            weights[into, value : value + VD] = given[source, low + 2 * HD : low + 2 * HD + VD]
            weights[into, value + VD : value + VP] = jnp.zeros((width, VP - VD), jnp.bfloat16)
            weights[into, query : query + HD] = given[source, low : low + HD]
    at = lax.broadcasted_iota(jnp.int32, (1, columns), 1)
    ones = jnp.zeros((1, columns), jnp.float32)
    scale = jnp.where(at >= heads * (HD + VP), QSCALE, 1.0)
    for h in range(heads):
        ones = jnp.where(at == heads * HD + h * VP + VD, 1.0, ones)
    low_taps = [tap[...].astype(jnp.bfloat16) for tap in taps]
    for copy in copies:
        copy.wait()

    def make(stage, into):
        for part in range(2):
            start = (stage * 2 + part) * step
            for s in range(n_head):
                into[part * step : (part + 1) * step, s * width : (s + 1) * width] = trunk_of(
                    low_taps[s],
                    *(
                        rows[s, pl.ds(pl.multiple_of(start + shift, step), step), :]
                        for shift in (0, step, 2 * step)
                    ),
                )

    def product_of(block):
        product = jnp.dot(block, weights[...], preferred_element_type=jnp.float32)
        return (product * scale + ones).astype(jnp.bfloat16)

    def project(stage, block):
        product = product_of(block[...])
        for part in range(2):
            at = stage * 2 + part
            rows_here = slice(part * step, (part + 1) * step)
            out[pl.ds(pl.multiple_of(at * step, step), step)] = product[rows_here]
            pooled_out[pl.ds(pl.multiple_of(at * size, size), size)] = jnp.dot(
                pool_matrix(step), block[rows_here, 0:width], preferred_element_type=jnp.float32
            )

    def window(index):
        start = (first // ALIGN) * ALIGN + (index - 1) * step
        return pl.multiple_of(jnp.clip(start, 0, tokens - WIN), ALIGN)

    def make_windows(into):
        for index in range(3):
            start = window(index)
            at = start + lax.broadcasted_iota(jnp.int32, (WIN, 1), 0)
            kept = [
                jnp.where(
                    jnp.logical_or(at + shift < first, at + shift >= last), 1.0, 0.0
                ).astype(jnp.bfloat16)
                for shift in (-step, 0, step)
            ]
            for s in range(n_head):
                into[index * WIN : (index + 1) * WIN, s * width : (s + 1) * width] = trunk_of(
                    low_taps[s],
                    *(
                        rows[s, pl.ds(pl.multiple_of(start + shift, ALIGN), WIN), :] * keep
                        for shift, keep in zip((0, step, 2 * step), kept)
                    ),
                )

    stages = tokens // (2 * step)
    make(0, left)

    def two_stages(n, carry):
        make(2 * n + 1, right)
        project(2 * n, left)
        make(2 * n + 2, left)
        project(2 * n + 1, right)
        return carry

    if stages > 2:
        lax.fori_loop(0, stages // 2 - 1, two_stages, 0)
    make(stages - 1, right)
    project(stages - 2, left)
    make_windows(left)
    project(stages - 1, right)
    product = product_of(left[0 : 3 * WIN])
    for index in range(3):
        rows_here = slice(index * WIN, (index + 1) * WIN)
        out[pl.ds(window(index), WIN)] = product[rows_here]
        small = pl.multiple_of(window(index) // POOL, ALIGN // POOL)
        pooled_out[pl.ds(small, WIN // POOL)] = jnp.dot(
            pool_matrix(WIN), left[rows_here, 0:width], preferred_element_type=jnp.float32
        )


def attend_kernel(heads, own, given, order, kvq, pooled, *refs):
    mixing, out = refs[:given], refs[given]
    *mix_out, scores_a, scores_b, top_a, top_b, total, parts = refs[given + 1 :]
    if mix_out:
        w_out, w_pair = mixing[:2]
        (w_mix,) = mix_out
        width = w_pair.shape[0]
        for s in range(given - 1):
            parts[order[out.shape[0] + s]] = mixing[1 + s][...]
        for h in range(heads):
            mix = jnp.zeros((VD, w_pair.shape[1]), jnp.float32)
            for k in range(given - 1):
                mix += jnp.dot(
                    w_out[h * VD : (h + 1) * VD, k * width : (k + 1) * width],
                    parts[k],
                    preferred_element_type=jnp.float32,
                )
            w_mix[h, 0:VD] = mix.astype(jnp.bfloat16)
            w_mix[h, VD:] = jnp.zeros((VP - VD, w_pair.shape[1]), jnp.bfloat16)
    else:
        w_mix, w_pair = mixing
    tokens = kvq.shape[0]
    chunk = scores_a.shape[2]
    steps = tokens // chunk
    key_cols, value_cols = heads * HD, heads * (HD + VP)
    pool = pool_matrix(own)
    scores, tops = (scores_a, scores_b), (top_a, top_b)
    chains = [(n, h) for n in range(out.shape[0]) for h in range(heads)]

    def score(index, c):
        n, h = chains[index]
        low = value_cols + h * HD
        found = lax.dot_general(
            kvq[pl.ds(pl.multiple_of(order[n] * own, own), own), low : low + HD],
            kvq[pl.ds(pl.multiple_of(c * chunk, chunk), chunk), h * HD : (h + 1) * HD],
            (((1,), (1,)), ((), ())),
            preferred_element_type=jnp.float32,
        )
        scores[index % 2][c] = found
        best = found[:, 0:128]
        for low in range(128, chunk, 128):
            best = jnp.maximum(best, found[:, low : low + 128])
        top = tops[index % 2]
        top[...] = jnp.maximum(top[...], best)

    def clear(index):
        tops[index % 2][...] = jnp.full(top_a.shape, -jnp.inf, jnp.float32)

    clear(0)

    def first_scores(c, carry):
        score(0, c)
        return carry

    lax.fori_loop(0, steps, first_scores, 0)
    for index, (n, h) in enumerate(chains):
        more = index + 1 < len(chains)
        if more:
            clear(index + 1)
        row_max = jnp.max(tops[index % 2][...], axis=1, keepdims=True)
        total[...] = jnp.zeros(total.shape, jnp.float32)
        low = key_cols + h * VP

        def weigh(c, carry):
            weights = jnp.exp2((scores[index % 2][c] - row_max).astype(jnp.bfloat16))
            if more:
                score(index + 1, c)
            total[...] += jnp.dot(
                weights,
                kvq[pl.ds(pl.multiple_of(c * chunk, chunk), chunk), low : low + VP],
                preferred_element_type=jnp.float32,
            )
            return carry

        lax.fori_loop(0, steps, weigh, 0)
        mixed = total[...]
        mixed = (mixed * (1.0 / mixed[:, VD : VD + 1])).astype(jnp.bfloat16)
        mixed = jnp.dot(pool, mixed, preferred_element_type=jnp.float32).astype(jnp.bfloat16)
        if h == 0:
            size = own // POOL
            pair = jnp.dot(
                pooled[pl.ds(pl.multiple_of(order[n] * size, size), size)].astype(jnp.bfloat16),
                w_pair[...],
                preferred_element_type=jnp.float32,
            )
        pair = pair + jnp.dot(mixed, w_mix[h], preferred_element_type=jnp.float32)
        if h == heads - 1:
            out[n] = pair.astype(out.dtype)


def pair_kernel(variants, order, table, *refs):
    row_feats = refs[:variants]
    col_feats = refs[variants : 2 * variants]
    out, rows, cols, blocks, sems = refs[2 * variants :]
    side = cols.shape[1]
    count = rows.shape[1]
    for s in range(variants):
        rows[order[s]] = row_feats[s][...].astype(jnp.float32)
        cols[order[variants + s]] = col_feats[s][...]

    def write(block, slot, variant):
        into = out.at[variant, pl.ds(block * ROWS, ROWS)]
        return pltpu.make_async_copy(blocks.at[slot, variant], into, sems.at[slot, variant])

    def one_block(block, carry):
        slot = lax.rem(block, 2)
        for variant in range(variants):
            pl.when(block >= 2)(write(block, slot, variant).wait)
            row_block = rows[variant, pl.ds(pl.multiple_of(block * ROWS, ROWS), ROWS), :]
            for r in range(ROWS):
                back = count - 1 - (block * ROWS + r)
                low = pl.multiple_of((back // SHIFTS) * SHIFTS, SHIFTS)
                relative = table[(count - 1 - r) % SHIFTS, pl.ds(low, side), :]
                row = jnp.broadcast_to(row_block[r : r + 1], (SHIFTS, C)).astype(jnp.bfloat16)
                found = (cols[variant] + relative).reshape(side // SHIFTS, SHIFTS, C) + row[None]
                blocks[slot, variant, r] = found.reshape(side, C)
            write(block, slot, variant).start()
        return carry

    total = count // ROWS
    lax.fori_loop(0, total, one_block, 0)
    for block in range(max(total - 2, 0), total):
        for variant in range(variants):
            write(block, block % 2, variant).wait()


def distance_table(dist_table, row_start, col_start, rows, cols):
    at = jnp.arange(SHIFTS, dtype=jnp.int32)[:, None] + jnp.arange(
        rows + cols, dtype=jnp.int32
    )
    distance = jnp.abs(row_start - col_start + rows - 1 - at)
    buckets = jnp.zeros(distance.shape, jnp.int32)
    for power_index in range(NB - 1):
        buckets = buckets + (distance >= 2**power_index).astype(jnp.int32)
    one_hot = (buckets[:, :, None] == jnp.arange(NB, dtype=jnp.int32)).astype(jnp.float32)
    return jnp.einsum("skb,bc->skc", one_hot, dist_table, precision=lax.Precision.HIGHEST).astype(
        jnp.bfloat16
    )


def in_hbm(array):
    return pltpu.with_memory_space_constraint(array, pltpu.HBM)


def whole(memory=pltpu.VMEM):
    return pl.BlockSpec(memory_space=memory)


def shifts(array, axis):
    size = lax.axis_size(axis)
    return [array] + [
        lax.ppermute(array, axis, [(k, (k + s) % size) for k in range(size)])
        for s in range(1, size)
    ]


def head_order(n_head):
    return [0, 1, 3, 2] if n_head == 4 else list(range(n_head))


def gather_rows(block, taps, table, n_ctx, n_var, n_head, core):
    crossing = lambda array: lax.ppermute(array, "var", [(0, 1), (1, 0)])
    if n_ctx == 4 and n_head == 4 and n_var == 2:
        shift = lambda array, s: lax.ppermute(array, "head", [(k, (k + s) % 4) for k in range(4)])
        over = lambda array, bit: lax.ppermute(array, "ctx", [(k, k ^ bit) for k in range(4)])
        near = jnp.stack([block, shift(block, 1), shift(block, 3)])
        far = shift(block, 2)[None]
        near_x, near_y, far_x, far_y = over(near, 1), over(near, 2), over(far, 1), over(far, 2)
        far_x, table = lax.optimization_barrier((far_x, table))
        slab, over_x, over_y = (
            jnp.concatenate(pair) for pair in ((near, far), (near_x, far_x), (near_y, far_y))
        )
        pairs = [(2 * k + c, 2 * (k ^ (c + 1)) + c) for k in range(4) for c in range(2)]
        corner = lax.ppermute(jnp.where(core == 0, over_y, over_x), ("ctx", "var"), pairs)
        pieces = [slab, over_x, over_y]
        corner, crossed, taps = lax.optimization_barrier(
            (corner, [crossing(piece) for piece in pieces], shifts(taps, "head"))
        )
        return pieces + [corner], crossed + [crossing(corner)], taps, table
    pieces = shifts(jnp.stack(shifts(block, "head")), "ctx")
    crossed = [crossing(piece) for piece in pieces]
    return pieces, crossed, shifts(taps, "head"), table


def local(sequence, deletions, conv_taps, conv_bias, w_proj, w_out, w_pair, dist_table):
    own, width = sequence.shape
    variants = deletions.shape[0]
    heads = w_out.shape[0] // VD
    n_ctx, n_head, n_var = (lax.axis_size(name) for name in ("ctx", "head", "var"))
    if n_ctx != n_head or n_var != 2 or n_ctx % variants:
        raise ValueError("mesh shape")
    step = own // n_var
    tokens = n_ctx * own
    pair_rows = own // POOL
    columns = heads * (2 * HD + VP)
    splits = n_ctx // variants
    mine, ours, core = (lax.axis_index(name) for name in ("ctx", "head", "var"))

    half = lax.dynamic_slice_in_dim(sequence, core * step, step, 0)
    taps = jnp.concatenate([conv_taps, conv_bias[None]], 0)
    table = distance_table(dist_table, mine * pair_rows, ours * pair_rows, pair_rows, pair_rows)
    pieces, crossed, taps, table = gather_rows(half, taps, table, n_ctx, n_var, n_head, core)
    if n_ctx == 4 and n_head == 4:
        blocks = [mine, mine ^ 1, mine ^ 2, mine ^ 3]
    else:
        blocks = [(mine + n_ctx - s) % n_ctx for s in range(n_ctx)]
    scalars = jnp.concatenate(
        [
            jnp.stack([ours, core]).astype(jnp.int32),
            lax.dynamic_index_in_dim(deletions, mine // splits, 0, keepdims=False),
            jnp.stack(blocks).astype(jnp.int32),
        ]
    )
    kvq, pooled = pl.pallas_call(
        functools.partial(project_kernel, heads, n_var, n_head, len(pieces)),
        out_shape=(
            jax.ShapeDtypeStruct((tokens, columns), jnp.bfloat16),
            jax.ShapeDtypeStruct((tokens // POOL, width), jnp.float32),
        ),
        in_specs=[whole(pltpu.SMEM), whole(pltpu.HBM)]
        + [whole()] * n_head
        + [whole(pltpu.HBM)] * (2 * len(pieces)),
        out_specs=(whole(), whole()),
        scratch_shapes=[
            pltpu.VMEM(w_proj.shape, jnp.bfloat16),
            pltpu.VMEM((n_head * width, columns), jnp.bfloat16),
            pltpu.VMEM((n_head, tokens + 2 * step, width), jnp.bfloat16),
            pltpu.VMEM((2 * step, n_head * width), jnp.bfloat16),
            pltpu.VMEM((2 * step, n_head * width), jnp.bfloat16),
            pltpu.SemaphoreType.DMA((2 * len(pieces) + 1, n_head)),
        ],
        compiler_params=pltpu.CompilerParams(vmem_limit_bytes=(34 if splits == 1 else 52) * MIB),
        cost_estimate=pl.CostEstimate(
            flops=2 * (tokens + 3 * WIN) * n_head * width * columns,
            bytes_accessed=4 * tokens * n_head * width,
            transcendentals=tokens * n_head * width,
        ),
        name="project",
    )(
        scalars,
        in_hbm(w_proj),
        *(taps[s] for s in head_order(n_head)),
        *(in_hbm(piece) for piece in pieces + crossed),
    )

    chunk = min(tokens, CHUNK)

    pair_parts = shifts(w_pair, "head")
    order_of_parts = [(ours + n_head - s) % n_head for s in range(n_head)]

    def attend(order, dtype, w_mix):
        count = order.shape[0]
        mix_shape = jax.ShapeDtypeStruct((heads, VP, 2 * C), jnp.bfloat16)
        out_shape = [jax.ShapeDtypeStruct((count, pair_rows, 2 * C), dtype)]
        if w_mix is None:
            mixing, out_shape = [w_out, *pair_parts], out_shape + [mix_shape]
            order = jnp.concatenate([order, jnp.stack(order_of_parts)])
        else:
            mixing = [w_mix, w_pair]
        return pl.pallas_call(
            functools.partial(attend_kernel, heads, own, len(mixing)),
            out_shape=out_shape,
            in_specs=[whole(pltpu.SMEM)] + [whole()] * (2 + len(mixing)),
            out_specs=[whole()] * len(out_shape),
            scratch_shapes=[
                pltpu.VMEM((tokens // chunk, own, chunk), jnp.float32),
                pltpu.VMEM((tokens // chunk, own, chunk), jnp.float32),
                pltpu.VMEM((own, 128), jnp.float32),
                pltpu.VMEM((own, 128), jnp.float32),
                pltpu.VMEM((own, VP), jnp.float32),
                pltpu.VMEM((n_head, width, 2 * C), jnp.bfloat16),
            ],
            compiler_params=pltpu.CompilerParams(
                vmem_limit_bytes=(22 if splits == 1 else 52) * MIB
            ),
            cost_estimate=pl.CostEstimate(
                flops=2 * count * heads * own * tokens * (2 * HD + VP),
                bytes_accessed=2 * tokens * columns,
                transcendentals=count * heads * own * tokens,
            ),
            name="attend",
        )(order.astype(jnp.int32), kvq, pooled, *mixing)

    if splits == 1:
        sent, w_mix = attend((ours + jnp.arange(1, n_head)) % n_head, jnp.bfloat16, None)
        summed = attend(ours[None], jnp.float32, w_mix)[0][0]
        for s in range(1, n_head):
            pairs = [(k, (k + s) % n_head) for k in range(n_head)]
            summed += lax.ppermute(sent[s - 1], "head", pairs).astype(jnp.float32)
        turned = lax.ppermute(
            summed[:, :C].astype(jnp.bfloat16),
            ("ctx", "head"),
            [(i * n_head + h, h * n_head + i) for i in range(n_ctx) for h in range(n_head)],
        )
        row_feats = shifts(turned, "head")
        col_feats = shifts(summed[:, C:].astype(jnp.bfloat16), "ctx")
        order = [(at + n_ctx - s) % n_ctx for at in (ours, mine) for s in range(variants)]
    else:
        blocks_here = n_ctx // splits
        here = (mine % splits) * blocks_here + jnp.arange(blocks_here)
        part = attend(here, jnp.bfloat16, None)[0]
        feats = lax.all_gather(lax.psum(part, "head"), "ctx", axis=0, tiled=False)
        feats = feats.reshape(variants, n_ctx, pair_rows, 2 * C)
        row_feats = lax.dynamic_index_in_dim(feats, mine, 1, keepdims=False)[:, :, :C]
        col_feats = lax.dynamic_index_in_dim(feats, ours, 1, keepdims=False)[:, :, C:]
        row_feats, col_feats = list(row_feats), list(col_feats)
        order = list(range(variants)) * 2

    return pl.pallas_call(
        functools.partial(pair_kernel, variants),
        out_shape=jax.ShapeDtypeStruct((variants, pair_rows, pair_rows, C), jnp.bfloat16),
        in_specs=[whole(pltpu.SMEM)] + [whole()] * (1 + 2 * variants),
        out_specs=whole(pl.ANY),
        scratch_shapes=[
            pltpu.VMEM((variants, pair_rows, C), jnp.float32),
            pltpu.VMEM((variants, pair_rows, C), jnp.bfloat16),
            pltpu.VMEM((2, variants, ROWS, pair_rows, C), jnp.bfloat16),
            pltpu.SemaphoreType.DMA((2, variants)),
        ],
        compiler_params=pltpu.CompilerParams(vmem_limit_bytes=24 * MIB),
        name="pair_map",
    )(jnp.stack(order).astype(jnp.int32) if splits == 1 else jnp.array(order, jnp.int32),
      table, *row_feats, *col_feats)


def solution(mesh):
    in_specs = (
        P("ctx", "head"),
        P("var", None),
        P(None, "head"),
        P("head"),
        P(None, "head"),
        P("head", None),
        P("head", None),
        P(),
    )
    out_specs = P("var", "ctx", "head", None)
    return jax.shard_map(local, mesh=mesh, in_specs=in_specs, out_specs=out_specs, check_vma=False)
```

```python
import functools
import math

import jax
import jax.numpy as jnp
from jax import lax
from jax.experimental import pallas as pl
from jax.experimental.pallas import tpu as pltpu
from jax.sharding import PartitionSpec as P

HD = 128
VD = 192
VP = 256
C = 128
NB = 16
POOL = 4
WIN = 160
ALIGN = 32
CHUNK = 2048
SHIFTS = 16
ROWS = 16
MIB = 1024 * 1024
QSCALE = math.log2(math.e) / math.sqrt(HD)
GELU_A = math.sqrt(2.0 / math.pi)
GELU_B = GELU_A * 0.044715


def trunk_of(taps, low, middle, high):
    convolved = taps[0:1] * low + taps[1:2] * middle + taps[2:3] * high + taps[3:4]
    half = 0.5 * convolved
    bent = jnp.tanh(convolved * (GELU_A + GELU_B * (convolved * convolved)))
    return middle + (half + half * bent)


def pool_matrix(count):
    wide = lax.broadcasted_iota(jnp.int32, (count // POOL, count), 1) // POOL
    tall = lax.broadcasted_iota(jnp.int32, (count // POOL, count), 0)
    return jnp.where(wide == tall, 1.0 / POOL, 0.0).astype(jnp.bfloat16)


def project_kernel(heads, n_var, n_head, count, scalars, w_proj, *refs):
    taps, pieces = refs[:n_head], refs[n_head : n_head + 2 * count]
    out, pooled_out, given, weights, rows, left, right, sems = refs[n_head + 2 * count :]
    step, width = pieces[0].shape[1:]
    tokens = rows.shape[1] - 2 * step
    size = step // POOL
    ours, core, first, last = (scalars[k] for k in range(4))

    given_copy = pltpu.make_async_copy(w_proj, given, sems.at[2 * count, 0])
    given_copy.start()
    copies = []
    for index, piece in enumerate(pieces):
        half = core if index < count else 1 - core
        at = pl.multiple_of((scalars[4 + index % count] * n_var + half + 1) * step, step)
        for s in range(n_head):
            copy = pltpu.make_async_copy(
                piece.at[s], rows.at[s, pl.ds(at, step)], sems.at[index, s]
            )
            copy.start()
            copies.append(copy)
    rows[:, 0:step] = jnp.zeros((n_head, step, width), jnp.bfloat16)
    rows[:, tokens + step :] = jnp.zeros((n_head, step, width), jnp.bfloat16)
    columns = weights.shape[1]
    given_copy.wait()
    for s, back in enumerate(head_order(n_head)):
        source = pl.ds(pl.multiple_of(lax.rem(ours + n_head - back, n_head) * width, ALIGN), width)
        into = slice(s * width, (s + 1) * width)
        for h in range(heads):
            low, key, value = h * (2 * HD + VD), h * HD, heads * HD + h * VP
            query = heads * (HD + VP) + h * HD
            weights[into, key : key + HD] = given[source, low + HD : low + 2 * HD]
            weights[into, value : value + VD] = given[source, low + 2 * HD : low + 2 * HD + VD]
            weights[into, value + VD : value + VP] = jnp.zeros((width, VP - VD), jnp.bfloat16)
            weights[into, query : query + HD] = given[source, low : low + HD]
    at = lax.broadcasted_iota(jnp.int32, (1, columns), 1)
    ones = jnp.zeros((1, columns), jnp.float32)
    scale = jnp.where(at >= heads * (HD + VP), QSCALE, 1.0)
    for h in range(heads):
        ones = jnp.where(at == heads * HD + h * VP + VD, 1.0, ones)
    low_taps = [tap[...].astype(jnp.bfloat16) for tap in taps]
    for copy in copies:
        copy.wait()

    def make(stage, into):
        for part in range(2):
            start = (stage * 2 + part) * step
            for s in range(n_head):
                into[part * step : (part + 1) * step, s * width : (s + 1) * width] = trunk_of(
                    low_taps[s],
                    *(
                        rows[s, pl.ds(pl.multiple_of(start + shift, step), step), :]
                        for shift in (0, step, 2 * step)
                    ),
                )

    def product_of(block):
        product = jnp.dot(block, weights[...], preferred_element_type=jnp.float32)
        return (product * scale + ones).astype(jnp.bfloat16)

    def project(stage, block):
        product = product_of(block[...])
        for part in range(2):
            at = stage * 2 + part
            rows_here = slice(part * step, (part + 1) * step)
            out[pl.ds(pl.multiple_of(at * step, step), step)] = product[rows_here]
            pooled_out[pl.ds(pl.multiple_of(at * size, size), size)] = jnp.dot(
                pool_matrix(step), block[rows_here, 0:width], preferred_element_type=jnp.float32
            )

    def window(index):
        start = (first // ALIGN) * ALIGN + (index - 1) * step
        return pl.multiple_of(jnp.clip(start, 0, tokens - WIN), ALIGN)

    def make_windows(into):
        for index in range(3):
            start = window(index)
            at = start + lax.broadcasted_iota(jnp.int32, (WIN, 1), 0)
            kept = [
                jnp.where(
                    jnp.logical_or(at + shift < first, at + shift >= last), 1.0, 0.0
                ).astype(jnp.bfloat16)
                for shift in (-step, 0, step)
            ]
            for s in range(n_head):
                into[index * WIN : (index + 1) * WIN, s * width : (s + 1) * width] = trunk_of(
                    low_taps[s],
                    *(
                        rows[s, pl.ds(pl.multiple_of(start + shift, ALIGN), WIN), :] * keep
                        for shift, keep in zip((0, step, 2 * step), kept)
                    ),
                )

    stages = tokens // (2 * step)
    make(0, left)

    def two_stages(n, carry):
        make(2 * n + 1, right)
        project(2 * n, left)
        make(2 * n + 2, left)
        project(2 * n + 1, right)
        return carry

    if stages > 2:
        lax.fori_loop(0, stages // 2 - 1, two_stages, 0)
    make(stages - 1, right)
    project(stages - 2, left)
    make_windows(left)
    project(stages - 1, right)
    product = product_of(left[0 : 3 * WIN])
    for index in range(3):
        rows_here = slice(index * WIN, (index + 1) * WIN)
        out[pl.ds(window(index), WIN)] = product[rows_here]
        small = pl.multiple_of(window(index) // POOL, ALIGN // POOL)
        pooled_out[pl.ds(small, WIN // POOL)] = jnp.dot(
            pool_matrix(WIN), left[rows_here, 0:width], preferred_element_type=jnp.float32
        )


def attend_kernel(heads, own, given, order, kvq, pooled, *refs):
    mixing, out = refs[:given], refs[given]
    *mix_out, scores_a, scores_b, top_a, top_b, total, parts = refs[given + 1 :]
    if mix_out:
        w_out, w_pair = mixing[:2]
        (w_mix,) = mix_out
        width = w_pair.shape[0]
        for s in range(given - 1):
            parts[order[out.shape[0] + s]] = mixing[1 + s][...]
        for h in range(heads):
            mix = jnp.zeros((VD, w_pair.shape[1]), jnp.float32)
            for k in range(given - 1):
                mix += jnp.dot(
                    w_out[h * VD : (h + 1) * VD, k * width : (k + 1) * width],
                    parts[k],
                    preferred_element_type=jnp.float32,
                )
            w_mix[h, 0:VD] = mix.astype(jnp.bfloat16)
            w_mix[h, VD:] = jnp.zeros((VP - VD, w_pair.shape[1]), jnp.bfloat16)
    else:
        w_mix, w_pair = mixing
    tokens = kvq.shape[0]
    chunk = scores_a.shape[2]
    steps = tokens // chunk
    key_cols, value_cols = heads * HD, heads * (HD + VP)
    pool = pool_matrix(own)
    scores, tops = (scores_a, scores_b), (top_a, top_b)
    chains = [(n, h) for n in range(out.shape[0]) for h in range(heads)]

    def score(index, c):
        n, h = chains[index]
        low = value_cols + h * HD
        found = lax.dot_general(
            kvq[pl.ds(pl.multiple_of(order[n] * own, own), own), low : low + HD],
            kvq[pl.ds(pl.multiple_of(c * chunk, chunk), chunk), h * HD : (h + 1) * HD],
            (((1,), (1,)), ((), ())),
            preferred_element_type=jnp.float32,
        )
        scores[index % 2][c] = found
        best = found[:, 0:128]
        for low in range(128, chunk, 128):
            best = jnp.maximum(best, found[:, low : low + 128])
        top = tops[index % 2]
        top[...] = jnp.maximum(top[...], best)

    def clear(index):
        tops[index % 2][...] = jnp.full(top_a.shape, -jnp.inf, jnp.float32)

    clear(0)

    def first_scores(c, carry):
        score(0, c)
        return carry

    lax.fori_loop(0, steps, first_scores, 0)
    for index, (n, h) in enumerate(chains):
        more = index + 1 < len(chains)
        if more:
            clear(index + 1)
        row_max = jnp.max(tops[index % 2][...], axis=1, keepdims=True)
        total[...] = jnp.zeros(total.shape, jnp.float32)
        low = key_cols + h * VP

        def weigh(c, carry):
            weights = jnp.exp2((scores[index % 2][c] - row_max).astype(jnp.bfloat16))
            if more:
                score(index + 1, c)
            total[...] += jnp.dot(
                weights,
                kvq[pl.ds(pl.multiple_of(c * chunk, chunk), chunk), low : low + VP],
                preferred_element_type=jnp.float32,
            )
            return carry

        lax.fori_loop(0, steps, weigh, 0)
        mixed = total[...]
        mixed = (mixed * (1.0 / mixed[:, VD : VD + 1])).astype(jnp.bfloat16)
        mixed = jnp.dot(pool, mixed, preferred_element_type=jnp.float32).astype(jnp.bfloat16)
        if h == 0:
            size = own // POOL
            pair = jnp.dot(
                pooled[pl.ds(pl.multiple_of(order[n] * size, size), size)].astype(jnp.bfloat16),
                w_pair[...],
                preferred_element_type=jnp.float32,
            )
        pair = pair + jnp.dot(mixed, w_mix[h], preferred_element_type=jnp.float32)
        if h == heads - 1:
            out[n] = pair.astype(out.dtype)


def pair_kernel(variants, order, dist_table, *refs):
    row_feats = refs[:variants]
    col_feats = refs[variants : 2 * variants]
    out, rows, cols, table, span, blocks, sems = refs[2 * variants :]
    side = cols.shape[1]
    count = rows.shape[1]
    for s in range(variants):
        rows[order[s]] = row_feats[s][...].astype(jnp.float32)
        cols[order[variants + s]] = col_feats[s][...]

    offset = order[2 * variants] + count - 1
    bucket = lax.broadcasted_iota(jnp.int32, (count + side, NB), 1)
    distance = jnp.abs(offset - lax.broadcasted_iota(jnp.int32, (count + side, NB), 0))
    above = distance >= jnp.where(bucket == 0, 0, jnp.left_shift(1, jnp.maximum(bucket - 1, 0)))
    below = jnp.logical_or(bucket == NB - 1, distance < jnp.left_shift(1, bucket))
    one_hot = jnp.where(jnp.logical_and(above, below), 1.0, 0.0).astype(jnp.bfloat16)
    span[...] = jnp.dot(
        one_hot, dist_table[...].astype(jnp.bfloat16), preferred_element_type=jnp.float32
    )
    for s in range(SHIFTS):
        table[s] = span[s : s + count + side - SHIFTS].astype(jnp.bfloat16)

    def write(block, slot, variant):
        into = out.at[variant, pl.ds(block * ROWS, ROWS)]
        return pltpu.make_async_copy(blocks.at[slot, variant], into, sems.at[slot, variant])

    def one_block(block, carry):
        slot = lax.rem(block, 2)
        for variant in range(variants):
            pl.when(block >= 2)(write(block, slot, variant).wait)
            row_block = rows[variant, pl.ds(pl.multiple_of(block * ROWS, ROWS), ROWS), :]
            for r in range(ROWS):
                back = count - 1 - (block * ROWS + r)
                low = pl.multiple_of((back // SHIFTS) * SHIFTS, SHIFTS)
                relative = table[(count - 1 - r) % SHIFTS, pl.ds(low, side), :]
                row = jnp.broadcast_to(row_block[r : r + 1], (SHIFTS, C)).astype(jnp.bfloat16)
                found = (cols[variant] + relative).reshape(side // SHIFTS, SHIFTS, C) + row[None]
                blocks[slot, variant, r] = found.reshape(side, C)
            write(block, slot, variant).start()
        return carry

    total = count // ROWS
    lax.fori_loop(0, total, one_block, 0)
    for block in range(max(total - 2, 0), total):
        for variant in range(variants):
            write(block, block % 2, variant).wait()


def in_hbm(array):
    return pltpu.with_memory_space_constraint(array, pltpu.HBM)


def whole(memory=pltpu.VMEM):
    return pl.BlockSpec(memory_space=memory)


def shifts(array, axis):
    size = lax.axis_size(axis)
    return [array] + [
        lax.ppermute(array, axis, [(k, (k + s) % size) for k in range(size)])
        for s in range(1, size)
    ]


def head_order(n_head):
    return [0, 1, 3, 2] if n_head == 4 else list(range(n_head))


def gather_rows(block, taps, n_ctx, n_var, n_head, core):
    crossing = lambda array: lax.ppermute(array, "var", [(0, 1), (1, 0)])
    if n_ctx == 4 and n_head == 4 and n_var == 2:
        shift = lambda array, s: lax.ppermute(array, "head", [(k, (k + s) % 4) for k in range(4)])
        over = lambda array, bit: lax.ppermute(array, "ctx", [(k, k ^ bit) for k in range(4)])
        near = jnp.stack([block, shift(block, 1), shift(block, 3)])
        far = shift(block, 2)[None]
        slab, over_x, over_y = (
            jnp.concatenate(pair)
            for pair in (
                (near, far), (over(near, 1), over(far, 1)), (over(near, 2), over(far, 2))
            )
        )
        pairs = [(2 * k + c, 2 * (k ^ (c + 1)) + c) for k in range(4) for c in range(2)]
        corner = lax.ppermute(jnp.where(core == 0, over_y, over_x), ("ctx", "var"), pairs)
        pieces = [slab, over_x, over_y]
        corner, crossed, taps = lax.optimization_barrier(
            (corner, [crossing(piece) for piece in pieces], shifts(taps, "head"))
        )
        return pieces + [corner], crossed + [crossing(corner)], taps
    pieces = shifts(jnp.stack(shifts(block, "head")), "ctx")
    crossed = [crossing(piece) for piece in pieces]
    return pieces, crossed, shifts(taps, "head")


def local(sequence, deletions, conv_taps, conv_bias, w_proj, w_out, w_pair, dist_table):
    own, width = sequence.shape
    variants = deletions.shape[0]
    heads = w_out.shape[0] // VD
    n_ctx, n_head, n_var = (lax.axis_size(name) for name in ("ctx", "head", "var"))
    if n_ctx != n_head or n_var != 2 or n_ctx % variants:
        raise ValueError("mesh shape")
    step = own // n_var
    tokens = n_ctx * own
    pair_rows = own // POOL
    columns = heads * (2 * HD + VP)
    splits = n_ctx // variants
    mine, ours, core = (lax.axis_index(name) for name in ("ctx", "head", "var"))

    half = lax.dynamic_slice_in_dim(sequence, core * step, step, 0)
    taps = jnp.concatenate([conv_taps, conv_bias[None]], 0)
    pieces, crossed, taps = gather_rows(half, taps, n_ctx, n_var, n_head, core)
    if n_ctx == 4 and n_head == 4:
        blocks = [mine, mine ^ 1, mine ^ 2, mine ^ 3]
    else:
        blocks = [(mine + n_ctx - s) % n_ctx for s in range(n_ctx)]
    scalars = jnp.concatenate(
        [
            jnp.stack([ours, core]).astype(jnp.int32),
            lax.dynamic_index_in_dim(deletions, mine // splits, 0, keepdims=False),
            jnp.stack(blocks).astype(jnp.int32),
        ]
    )
    kvq, pooled = pl.pallas_call(
        functools.partial(project_kernel, heads, n_var, n_head, len(pieces)),
        out_shape=(
            jax.ShapeDtypeStruct((tokens, columns), jnp.bfloat16),
            jax.ShapeDtypeStruct((tokens // POOL, width), jnp.float32),
        ),
        in_specs=[whole(pltpu.SMEM), whole(pltpu.HBM)]
        + [whole()] * n_head
        + [whole(pltpu.HBM)] * (2 * len(pieces)),
        out_specs=(whole(), whole()),
        scratch_shapes=[
            pltpu.VMEM(w_proj.shape, jnp.bfloat16),
            pltpu.VMEM((n_head * width, columns), jnp.bfloat16),
            pltpu.VMEM((n_head, tokens + 2 * step, width), jnp.bfloat16),
            pltpu.VMEM((2 * step, n_head * width), jnp.bfloat16),
            pltpu.VMEM((2 * step, n_head * width), jnp.bfloat16),
            pltpu.SemaphoreType.DMA((2 * len(pieces) + 1, n_head)),
        ],
        compiler_params=pltpu.CompilerParams(vmem_limit_bytes=(34 if splits == 1 else 52) * MIB),
        cost_estimate=pl.CostEstimate(
            flops=2 * (tokens + 3 * WIN) * n_head * width * columns,
            bytes_accessed=4 * tokens * n_head * width,
            transcendentals=tokens * n_head * width,
        ),
        name="project",
    )(
        scalars,
        in_hbm(w_proj),
        *(taps[s] for s in head_order(n_head)),
        *(in_hbm(piece) for piece in pieces + crossed),
    )

    chunk = min(tokens, CHUNK)

    pair_parts = shifts(w_pair, "head")
    order_of_parts = [(ours + n_head - s) % n_head for s in range(n_head)]

    def attend(order, dtype, w_mix):
        count = order.shape[0]
        mix_shape = jax.ShapeDtypeStruct((heads, VP, 2 * C), jnp.bfloat16)
        out_shape = [jax.ShapeDtypeStruct((count, pair_rows, 2 * C), dtype)]
        if w_mix is None:
            mixing, out_shape = [w_out, *pair_parts], out_shape + [mix_shape]
            order = jnp.concatenate([order, jnp.stack(order_of_parts)])
        else:
            mixing = [w_mix, w_pair]
        return pl.pallas_call(
            functools.partial(attend_kernel, heads, own, len(mixing)),
            out_shape=out_shape,
            in_specs=[whole(pltpu.SMEM)] + [whole()] * (2 + len(mixing)),
            out_specs=[whole()] * len(out_shape),
            scratch_shapes=[
                pltpu.VMEM((tokens // chunk, own, chunk), jnp.float32),
                pltpu.VMEM((tokens // chunk, own, chunk), jnp.float32),
                pltpu.VMEM((own, 128), jnp.float32),
                pltpu.VMEM((own, 128), jnp.float32),
                pltpu.VMEM((own, VP), jnp.float32),
                pltpu.VMEM((n_head, width, 2 * C), jnp.bfloat16),
            ],
            compiler_params=pltpu.CompilerParams(
                vmem_limit_bytes=(22 if splits == 1 else 52) * MIB
            ),
            cost_estimate=pl.CostEstimate(
                flops=2 * count * heads * own * tokens * (2 * HD + VP),
                bytes_accessed=2 * tokens * columns,
                transcendentals=count * heads * own * tokens,
            ),
            name="attend",
        )(order.astype(jnp.int32), kvq, pooled, *mixing)

    if splits == 1:
        sent, w_mix = attend((ours + jnp.arange(1, n_head)) % n_head, jnp.bfloat16, None)
        summed = attend(ours[None], jnp.float32, w_mix)[0][0]
        for s in range(1, n_head):
            pairs = [(k, (k + s) % n_head) for k in range(n_head)]
            summed += lax.ppermute(sent[s - 1], "head", pairs).astype(jnp.float32)
        turned = lax.ppermute(
            summed[:, :C].astype(jnp.bfloat16),
            ("ctx", "head"),
            [(i * n_head + h, h * n_head + i) for i in range(n_ctx) for h in range(n_head)],
        )
        row_feats = shifts(turned, "head")
        col_feats = shifts(summed[:, C:].astype(jnp.bfloat16), "ctx")
        order = [(at + n_ctx - s) % n_ctx for at in (ours, mine) for s in range(variants)]
    else:
        blocks_here = n_ctx // splits
        here = (mine % splits) * blocks_here + jnp.arange(blocks_here)
        part = attend(here, jnp.bfloat16, None)[0]
        feats = lax.all_gather(lax.psum(part, "head"), "ctx", axis=0, tiled=False)
        feats = feats.reshape(variants, n_ctx, pair_rows, 2 * C)
        row_feats = lax.dynamic_index_in_dim(feats, mine, 1, keepdims=False)[:, :, :C]
        col_feats = lax.dynamic_index_in_dim(feats, ours, 1, keepdims=False)[:, :, C:]
        row_feats, col_feats = list(row_feats), list(col_feats)
        order = list(range(variants)) * 2

    return pl.pallas_call(
        functools.partial(pair_kernel, variants),
        out_shape=jax.ShapeDtypeStruct((variants, pair_rows, pair_rows, C), jnp.bfloat16),
        in_specs=[whole(pltpu.SMEM)] + [whole()] * (1 + 2 * variants),
        out_specs=whole(pl.ANY),
        scratch_shapes=[
            pltpu.VMEM((variants, pair_rows, C), jnp.float32),
            pltpu.VMEM((variants, pair_rows, C), jnp.bfloat16),
            pltpu.VMEM((SHIFTS, 2 * pair_rows - SHIFTS, C), jnp.bfloat16),
            pltpu.VMEM((2 * pair_rows, C), jnp.float32),
            pltpu.VMEM((2, variants, ROWS, pair_rows, C), jnp.bfloat16),
            pltpu.SemaphoreType.DMA((2, variants)),
        ],
        compiler_params=pltpu.CompilerParams(vmem_limit_bytes=24 * MIB),
        name="pair_map",
    )(
        jnp.stack([*order, (mine - ours) * pair_rows]).astype(jnp.int32),
        dist_table,
        *row_feats,
        *col_feats,
    )


def solution(mesh):
    in_specs = (
        P("ctx", "head"),
        P("var", None),
        P(None, "head"),
        P("head"),
        P(None, "head"),
        P("head", None),
        P("head", None),
        P(),
    )
    out_specs = P("var", "ctx", "head", None)
    return jax.shard_map(local, mesh=mesh, in_specs=in_specs, out_specs=out_specs, check_vma=False)
```

```python
import functools
import math

import jax
import jax.numpy as jnp
from jax import lax
from jax.experimental import pallas as pl
from jax.experimental.pallas import tpu as pltpu
from jax.sharding import PartitionSpec as P

HD = 128
VD = 192
VP = 256
C = 128
NB = 16
POOL = 4
WIN = 160
ALIGN = 32
CHUNK = 2048
SHIFTS = 16
ROWS = 16
MIB = 1024 * 1024
QSCALE = math.log2(math.e) / math.sqrt(HD)
GELU_A = math.sqrt(2.0 / math.pi)
GELU_B = GELU_A * 0.044715


def trunk_of(taps, low, middle, high):
    convolved = taps[0:1] * low + taps[1:2] * middle + taps[2:3] * high + taps[3:4]
    half = 0.5 * convolved
    bent = jnp.tanh(convolved * (GELU_A + GELU_B * (convolved * convolved)))
    return middle + (half + half * bent)


def pool_matrix(count):
    wide = lax.broadcasted_iota(jnp.int32, (count // POOL, count), 1) // POOL
    tall = lax.broadcasted_iota(jnp.int32, (count // POOL, count), 0)
    return jnp.where(wide == tall, 1.0 / POOL, 0.0).astype(jnp.bfloat16)


def project_kernel(heads, n_var, n_head, count, scalars, w_proj, *refs):
    taps, pieces = refs[0], refs[1 : 1 + 2 * count]
    out, pooled_out, given, weights, rows, left, right, sems = refs[1 + 2 * count :]
    step, width = pieces[0].shape[1:]
    tokens = rows.shape[1] - 2 * step
    size = step // POOL
    ours, core, first, last = (scalars[k] for k in range(4))

    given_copy = pltpu.make_async_copy(w_proj, given, sems.at[2 * count, 0])
    given_copy.start()
    copies = []
    for index, piece in enumerate(pieces):
        half = core if index < count else 1 - core
        at = pl.multiple_of((scalars[4 + index % count] * n_var + half + 1) * step, step)
        for s in range(n_head):
            copy = pltpu.make_async_copy(
                piece.at[s], rows.at[s, pl.ds(at, step)], sems.at[index, s]
            )
            copy.start()
            copies.append(copy)
    rows[:, 0:step] = jnp.zeros((n_head, step, width), jnp.bfloat16)
    rows[:, tokens + step :] = jnp.zeros((n_head, step, width), jnp.bfloat16)
    columns = weights.shape[1]
    given_copy.wait()
    for s, back in enumerate(head_order(n_head)):
        source = pl.ds(pl.multiple_of(lax.rem(ours + n_head - back, n_head) * width, ALIGN), width)
        into = slice(s * width, (s + 1) * width)
        for h in range(heads):
            low, key, value = h * (2 * HD + VD), h * HD, heads * HD + h * VP
            query = heads * (HD + VP) + h * HD
            weights[into, key : key + HD] = given[source, low + HD : low + 2 * HD]
            weights[into, value : value + VD] = given[source, low + 2 * HD : low + 2 * HD + VD]
            weights[into, value + VD : value + VP] = jnp.zeros((width, VP - VD), jnp.bfloat16)
            weights[into, query : query + HD] = given[source, low : low + HD]
    at = lax.broadcasted_iota(jnp.int32, (1, columns), 1)
    ones = jnp.zeros((1, columns), jnp.float32)
    scale = jnp.where(at >= heads * (HD + VP), QSCALE, 1.0)
    for h in range(heads):
        ones = jnp.where(at == heads * HD + h * VP + VD, 1.0, ones)
    low_taps = []
    for s, back in enumerate(head_order(n_head)):
        place = jnp.bitwise_xor(ours, lax.rem(ours + n_head - back, n_head)) if n_head == 4 else s
        low_taps.append(taps[place].astype(jnp.bfloat16))
    for copy in copies:
        copy.wait()

    def make(stage, into):
        for part in range(2):
            start = (stage * 2 + part) * step
            for s in range(n_head):
                into[part * step : (part + 1) * step, s * width : (s + 1) * width] = trunk_of(
                    low_taps[s],
                    *(
                        rows[s, pl.ds(pl.multiple_of(start + shift, step), step), :]
                        for shift in (0, step, 2 * step)
                    ),
                )

    def product_of(block):
        product = jnp.dot(block, weights[...], preferred_element_type=jnp.float32)
        return (product * scale + ones).astype(jnp.bfloat16)

    def project(stage, block):
        product = product_of(block[...])
        for part in range(2):
            at = stage * 2 + part
            rows_here = slice(part * step, (part + 1) * step)
            out[pl.ds(pl.multiple_of(at * step, step), step)] = product[rows_here]
            pooled_out[pl.ds(pl.multiple_of(at * size, size), size)] = jnp.dot(
                pool_matrix(step), block[rows_here, 0:width], preferred_element_type=jnp.float32
            )

    def window(index):
        start = (first // ALIGN) * ALIGN + (index - 1) * step
        return pl.multiple_of(jnp.clip(start, 0, tokens - WIN), ALIGN)

    def make_windows(into):
        for index in range(3):
            start = window(index)
            at = start + lax.broadcasted_iota(jnp.int32, (WIN, 1), 0)
            kept = [
                jnp.where(
                    jnp.logical_or(at + shift < first, at + shift >= last), 1.0, 0.0
                ).astype(jnp.bfloat16)
                for shift in (-step, 0, step)
            ]
            for s in range(n_head):
                into[index * WIN : (index + 1) * WIN, s * width : (s + 1) * width] = trunk_of(
                    low_taps[s],
                    *(
                        rows[s, pl.ds(pl.multiple_of(start + shift, ALIGN), WIN), :] * keep
                        for shift, keep in zip((0, step, 2 * step), kept)
                    ),
                )

    stages = tokens // (2 * step)
    make(0, left)

    def two_stages(n, carry):
        make(2 * n + 1, right)
        project(2 * n, left)
        make(2 * n + 2, left)
        project(2 * n + 1, right)
        return carry

    if stages > 2:
        lax.fori_loop(0, stages // 2 - 1, two_stages, 0)
    make(stages - 1, right)
    project(stages - 2, left)
    make_windows(left)
    project(stages - 1, right)
    product = product_of(left[0 : 3 * WIN])
    for index in range(3):
        rows_here = slice(index * WIN, (index + 1) * WIN)
        out[pl.ds(window(index), WIN)] = product[rows_here]
        small = pl.multiple_of(window(index) // POOL, ALIGN // POOL)
        pooled_out[pl.ds(small, WIN // POOL)] = jnp.dot(
            pool_matrix(WIN), left[rows_here, 0:width], preferred_element_type=jnp.float32
        )


def attend_kernel(heads, own, given, order, kvq, pooled, *refs):
    mixing, out = refs[:given], refs[given]
    *mix_out, scores_a, scores_b, top_a, top_b, total, parts = refs[given + 1 :]
    if mix_out:
        w_out, w_pair = mixing[:2]
        (w_mix,) = mix_out
        width = w_pair.shape[0]
        for s in range(given - 1):
            parts[order[out.shape[0] + s]] = mixing[1 + s][...]
        for h in range(heads):
            mix = jnp.zeros((VD, w_pair.shape[1]), jnp.float32)
            for k in range(given - 1):
                mix += jnp.dot(
                    w_out[h * VD : (h + 1) * VD, k * width : (k + 1) * width],
                    parts[k],
                    preferred_element_type=jnp.float32,
                )
            w_mix[h, 0:VD] = mix.astype(jnp.bfloat16)
            w_mix[h, VD:] = jnp.zeros((VP - VD, w_pair.shape[1]), jnp.bfloat16)
    else:
        w_mix, w_pair = mixing
    tokens = kvq.shape[0]
    chunk = scores_a.shape[2]
    steps = tokens // chunk
    key_cols, value_cols = heads * HD, heads * (HD + VP)
    pool = pool_matrix(own)
    scores, tops = (scores_a, scores_b), (top_a, top_b)
    chains = [(n, h) for n in range(out.shape[0]) for h in range(heads)]

    def score(index, c):
        n, h = chains[index]
        low = value_cols + h * HD
        found = lax.dot_general(
            kvq[pl.ds(pl.multiple_of(order[n] * own, own), own), low : low + HD],
            kvq[pl.ds(pl.multiple_of(c * chunk, chunk), chunk), h * HD : (h + 1) * HD],
            (((1,), (1,)), ((), ())),
            preferred_element_type=jnp.float32,
        )
        scores[index % 2][c] = found
        best = found[:, 0:128]
        for low in range(128, chunk, 128):
            best = jnp.maximum(best, found[:, low : low + 128])
        top = tops[index % 2]
        top[...] = jnp.maximum(top[...], best)

    def clear(index):
        tops[index % 2][...] = jnp.full(top_a.shape, -jnp.inf, jnp.float32)

    clear(0)

    def first_scores(c, carry):
        score(0, c)
        return carry

    lax.fori_loop(0, steps, first_scores, 0)
    for index, (n, h) in enumerate(chains):
        more = index + 1 < len(chains)
        if more:
            clear(index + 1)
        row_max = jnp.max(tops[index % 2][...], axis=1, keepdims=True)
        total[...] = jnp.zeros(total.shape, jnp.float32)
        low = key_cols + h * VP

        def weigh(c, carry):
            weights = jnp.exp2((scores[index % 2][c] - row_max).astype(jnp.bfloat16))
            if more:
                score(index + 1, c)
            total[...] += jnp.dot(
                weights,
                kvq[pl.ds(pl.multiple_of(c * chunk, chunk), chunk), low : low + VP],
                preferred_element_type=jnp.float32,
            )
            return carry

        lax.fori_loop(0, steps, weigh, 0)
        mixed = total[...]
        mixed = (mixed * (1.0 / mixed[:, VD : VD + 1])).astype(jnp.bfloat16)
        mixed = jnp.dot(pool, mixed, preferred_element_type=jnp.float32).astype(jnp.bfloat16)
        if h == 0:
            size = own // POOL
            pair = jnp.dot(
                pooled[pl.ds(pl.multiple_of(order[n] * size, size), size)].astype(jnp.bfloat16),
                w_pair[...],
                preferred_element_type=jnp.float32,
            )
        pair = pair + jnp.dot(mixed, w_mix[h], preferred_element_type=jnp.float32)
        if h == heads - 1:
            out[n] = pair.astype(out.dtype)


def pair_kernel(variants, order, dist_table, *refs):
    row_feats = refs[:variants]
    col_feats = refs[variants : 2 * variants]
    out, rows, cols, table, span, blocks, sems = refs[2 * variants :]
    side = cols.shape[1]
    count = rows.shape[1]
    for s in range(variants):
        rows[order[s]] = row_feats[s][...].astype(jnp.float32)
        cols[order[variants + s]] = col_feats[s][...]

    offset = order[2 * variants] + count - 1
    bucket = lax.broadcasted_iota(jnp.int32, (count + side, NB), 1)
    distance = jnp.abs(offset - lax.broadcasted_iota(jnp.int32, (count + side, NB), 0))
    above = distance >= jnp.where(bucket == 0, 0, jnp.left_shift(1, jnp.maximum(bucket - 1, 0)))
    below = jnp.logical_or(bucket == NB - 1, distance < jnp.left_shift(1, bucket))
    one_hot = jnp.where(jnp.logical_and(above, below), 1.0, 0.0).astype(jnp.bfloat16)
    span[...] = jnp.dot(
        one_hot, dist_table[...].astype(jnp.bfloat16), preferred_element_type=jnp.float32
    )
    for s in range(SHIFTS):
        table[s] = span[s : s + count + side - SHIFTS].astype(jnp.bfloat16)

    def write(block, slot, variant):
        into = out.at[variant, pl.ds(block * ROWS, ROWS)]
        return pltpu.make_async_copy(blocks.at[slot, variant], into, sems.at[slot, variant])

    def one_block(block, carry):
        slot = lax.rem(block, 2)
        for variant in range(variants):
            pl.when(block >= 2)(write(block, slot, variant).wait)
            row_block = rows[variant, pl.ds(pl.multiple_of(block * ROWS, ROWS), ROWS), :]
            for r in range(ROWS):
                back = count - 1 - (block * ROWS + r)
                low = pl.multiple_of((back // SHIFTS) * SHIFTS, SHIFTS)
                relative = table[(count - 1 - r) % SHIFTS, pl.ds(low, side), :]
                row = jnp.broadcast_to(row_block[r : r + 1], (SHIFTS, C)).astype(jnp.bfloat16)
                found = (cols[variant] + relative).reshape(side // SHIFTS, SHIFTS, C) + row[None]
                blocks[slot, variant, r] = found.reshape(side, C)
            write(block, slot, variant).start()
        return carry

    total = count // ROWS
    lax.fori_loop(0, total, one_block, 0)
    for block in range(max(total - 2, 0), total):
        for variant in range(variants):
            write(block, block % 2, variant).wait()


def in_hbm(array):
    return pltpu.with_memory_space_constraint(array, pltpu.HBM)


def whole(memory=pltpu.VMEM):
    return pl.BlockSpec(memory_space=memory)


def shifts(array, axis):
    size = lax.axis_size(axis)
    return [array] + [
        lax.ppermute(array, axis, [(k, (k + s) % size) for k in range(size)])
        for s in range(1, size)
    ]


def head_order(n_head):
    return [0, 1, 3, 2] if n_head == 4 else list(range(n_head))


def gather_rows(block, taps, n_ctx, n_var, n_head, core):
    crossing = lambda array: lax.ppermute(array, "var", [(0, 1), (1, 0)])
    if n_head == 4:
        shift = lambda array, s: lax.ppermute(array, "head", [(k, (k + s) % 4) for k in range(4)])
        over = lambda array, bit: lax.ppermute(array, "ctx", [(k, k ^ bit) for k in range(4)])
        near = jnp.stack([block, shift(block, 1), shift(block, 3)])
        far = shift(block, 2)[None]
        slab, over_x, over_y = (
            jnp.concatenate(pair)
            for pair in (
                (near, far), (over(near, 1), over(far, 1)), (over(near, 2), over(far, 2))
            )
        )
        pairs = [(2 * k + c, 2 * (k ^ (c + 1)) + c) for k in range(4) for c in range(2)]
        corner = lax.ppermute(jnp.where(core == 0, over_y, over_x), ("ctx", "var"), pairs)
        pieces = [slab, over_x, over_y]
        for bit in (1, 2):
            moved = lax.ppermute(taps, "head", [(k, k ^ bit) for k in range(4)])
            taps = jnp.concatenate([taps, moved])
        corner, crossed, taps = lax.optimization_barrier(
            (corner, [crossing(piece) for piece in pieces], taps)
        )
        return pieces + [corner], crossed + [crossing(corner)], taps
    pieces = shifts(jnp.stack(shifts(block, "head")), "ctx")
    crossed = [crossing(piece) for piece in pieces]
    return pieces, crossed, jnp.concatenate(shifts(taps, "head"))


def local(sequence, deletions, conv_taps, conv_bias, w_proj, w_out, w_pair, dist_table):
    own, width = sequence.shape
    variants = deletions.shape[0]
    heads = w_out.shape[0] // VD
    n_ctx, n_head, n_var = (lax.axis_size(name) for name in ("ctx", "head", "var"))
    if n_ctx != n_head or n_var != 2 or n_ctx % variants:
        raise ValueError("mesh shape")
    step = own // n_var
    tokens = n_ctx * own
    pair_rows = own // POOL
    columns = heads * (2 * HD + VP)
    splits = n_ctx // variants
    mine, ours, core = (lax.axis_index(name) for name in ("ctx", "head", "var"))

    half = lax.dynamic_slice_in_dim(sequence, core * step, step, 0)
    taps = jnp.concatenate([conv_taps, conv_bias[None]], 0)
    pieces, crossed, taps = gather_rows(half, taps, n_ctx, n_var, n_head, core)
    if n_ctx == 4 and n_head == 4:
        blocks = [mine, mine ^ 1, mine ^ 2, mine ^ 3]
    else:
        blocks = [(mine + n_ctx - s) % n_ctx for s in range(n_ctx)]
    scalars = jnp.concatenate(
        [
            jnp.stack([ours, core]).astype(jnp.int32),
            lax.dynamic_index_in_dim(deletions, mine // splits, 0, keepdims=False),
            jnp.stack(blocks).astype(jnp.int32),
        ]
    )
    kvq, pooled = pl.pallas_call(
        functools.partial(project_kernel, heads, n_var, n_head, len(pieces)),
        out_shape=(
            jax.ShapeDtypeStruct((tokens, columns), jnp.bfloat16),
            jax.ShapeDtypeStruct((tokens // POOL, width), jnp.float32),
        ),
        in_specs=[whole(pltpu.SMEM), whole(pltpu.HBM)]
        + [whole()]
        + [whole(pltpu.HBM)] * (2 * len(pieces)),
        out_specs=(whole(), whole()),
        scratch_shapes=[
            pltpu.VMEM(w_proj.shape, jnp.bfloat16),
            pltpu.VMEM((n_head * width, columns), jnp.bfloat16),
            pltpu.VMEM((n_head, tokens + 2 * step, width), jnp.bfloat16),
            pltpu.VMEM((2 * step, n_head * width), jnp.bfloat16),
            pltpu.VMEM((2 * step, n_head * width), jnp.bfloat16),
            pltpu.SemaphoreType.DMA((2 * len(pieces) + 1, n_head)),
        ],
        compiler_params=pltpu.CompilerParams(vmem_limit_bytes=(34 if splits == 1 else 52) * MIB),
        cost_estimate=pl.CostEstimate(
            flops=2 * (tokens + 3 * WIN) * n_head * width * columns,
            bytes_accessed=4 * tokens * n_head * width,
            transcendentals=tokens * n_head * width,
        ),
        name="project",
    )(
        scalars,
        in_hbm(w_proj),
        taps.reshape(n_head, 4, width),
        *(in_hbm(piece) for piece in pieces + crossed),
    )

    chunk = min(tokens, CHUNK)

    pair_parts = shifts(w_pair, "head")
    order_of_parts = [(ours + n_head - s) % n_head for s in range(n_head)]

    def attend(order, dtype, w_mix):
        count = order.shape[0]
        mix_shape = jax.ShapeDtypeStruct((heads, VP, 2 * C), jnp.bfloat16)
        out_shape = [jax.ShapeDtypeStruct((count, pair_rows, 2 * C), dtype)]
        if w_mix is None:
            mixing, out_shape = [w_out, *pair_parts], out_shape + [mix_shape]
            order = jnp.concatenate([order, jnp.stack(order_of_parts)])
        else:
            mixing = [w_mix, w_pair]
        return pl.pallas_call(
            functools.partial(attend_kernel, heads, own, len(mixing)),
            out_shape=out_shape,
            in_specs=[whole(pltpu.SMEM)] + [whole()] * (2 + len(mixing)),
            out_specs=[whole()] * len(out_shape),
            scratch_shapes=[
                pltpu.VMEM((tokens // chunk, own, chunk), jnp.float32),
                pltpu.VMEM((tokens // chunk, own, chunk), jnp.float32),
                pltpu.VMEM((own, 128), jnp.float32),
                pltpu.VMEM((own, 128), jnp.float32),
                pltpu.VMEM((own, VP), jnp.float32),
                pltpu.VMEM((n_head, width, 2 * C), jnp.bfloat16),
            ],
            compiler_params=pltpu.CompilerParams(
                vmem_limit_bytes=(22 if splits == 1 else 52) * MIB
            ),
            cost_estimate=pl.CostEstimate(
                flops=2 * count * heads * own * tokens * (2 * HD + VP),
                bytes_accessed=2 * tokens * columns,
                transcendentals=count * heads * own * tokens,
            ),
            name="attend",
        )(order.astype(jnp.int32), kvq, pooled, *mixing)

    if splits == 1:
        sent, w_mix = attend((ours + jnp.arange(1, n_head)) % n_head, jnp.bfloat16, None)
        summed = attend(ours[None], jnp.float32, w_mix)[0][0]
        for s in range(1, n_head):
            pairs = [(k, (k + s) % n_head) for k in range(n_head)]
            summed += lax.ppermute(sent[s - 1], "head", pairs).astype(jnp.float32)
        turned = lax.ppermute(
            summed[:, :C].astype(jnp.bfloat16),
            ("ctx", "head"),
            [(i * n_head + h, h * n_head + i) for i in range(n_ctx) for h in range(n_head)],
        )
        row_feats = shifts(turned, "head")
        col_feats = shifts(summed[:, C:].astype(jnp.bfloat16), "ctx")
        order = [(at + n_ctx - s) % n_ctx for at in (ours, mine) for s in range(variants)]
    else:
        blocks_here = n_ctx // splits
        here = (mine % splits) * blocks_here + jnp.arange(blocks_here)
        part = attend(here, jnp.bfloat16, None)[0]
        feats = lax.all_gather(lax.psum(part, "head"), "ctx", axis=0, tiled=False)
        feats = feats.reshape(variants, n_ctx, pair_rows, 2 * C)
        row_feats = lax.dynamic_index_in_dim(feats, mine, 1, keepdims=False)[:, :, :C]
        col_feats = lax.dynamic_index_in_dim(feats, ours, 1, keepdims=False)[:, :, C:]
        row_feats, col_feats = list(row_feats), list(col_feats)
        order = list(range(variants)) * 2

    return pl.pallas_call(
        functools.partial(pair_kernel, variants),
        out_shape=jax.ShapeDtypeStruct((variants, pair_rows, pair_rows, C), jnp.bfloat16),
        in_specs=[whole(pltpu.SMEM)] + [whole()] * (1 + 2 * variants),
        out_specs=whole(pl.ANY),
        scratch_shapes=[
            pltpu.VMEM((variants, pair_rows, C), jnp.float32),
            pltpu.VMEM((variants, pair_rows, C), jnp.bfloat16),
            pltpu.VMEM((SHIFTS, 2 * pair_rows - SHIFTS, C), jnp.bfloat16),
            pltpu.VMEM((2 * pair_rows, C), jnp.float32),
            pltpu.VMEM((2, variants, ROWS, pair_rows, C), jnp.bfloat16),
            pltpu.SemaphoreType.DMA((2, variants)),
        ],
        compiler_params=pltpu.CompilerParams(vmem_limit_bytes=24 * MIB),
        name="pair_map",
    )(
        jnp.stack([*order, (mine - ours) * pair_rows]).astype(jnp.int32),
        dist_table,
        *row_feats,
        *col_feats,
    )


def solution(mesh):
    in_specs = (
        P("ctx", "head"),
        P("var", None),
        P(None, "head"),
        P("head"),
        P(None, "head"),
        P("head", None),
        P("head", None),
        P(),
    )
    out_specs = P("var", "ctx", "head", None)
    return jax.shard_map(local, mesh=mesh, in_specs=in_specs, out_specs=out_specs, check_vma=False)
```

```python
import functools
import math

import jax
import jax.numpy as jnp
from jax import lax
from jax.experimental import pallas as pl
from jax.experimental.pallas import tpu as pltpu
from jax.sharding import PartitionSpec as P

HD = 128
VD = 192
VP = 256
C = 128
NB = 16
POOL = 4
WIN = 160
ALIGN = 32
CHUNK = 2048
SHIFTS = 16
ROWS = 16
MIB = 1024 * 1024
QSCALE = math.log2(math.e) / math.sqrt(HD)
GELU_A = math.sqrt(2.0 / math.pi)
GELU_B = GELU_A * 0.044715


def trunk_of(taps, low, middle, high):
    convolved = taps[0:1] * low + taps[1:2] * middle + taps[2:3] * high + taps[3:4]
    half = 0.5 * convolved
    bent = jnp.tanh(convolved * (GELU_A + GELU_B * (convolved * convolved)))
    return middle + (half + half * bent)


def pool_matrix(count):
    wide = lax.broadcasted_iota(jnp.int32, (count // POOL, count), 1) // POOL
    tall = lax.broadcasted_iota(jnp.int32, (count // POOL, count), 0)
    return jnp.where(wide == tall, 1.0 / POOL, 0.0).astype(jnp.bfloat16)


def project_kernel(heads, n_var, n_head, count, scalars, w_proj, *refs):
    taps, pieces = refs[0], refs[1 : 1 + 2 * count]
    out, pooled_out, given, weights, rows, left, right, sems = refs[1 + 2 * count :]
    step, width = pieces[0].shape[1:]
    tokens = rows.shape[1] - 2 * step
    size = step // POOL
    ours, core, first, last = (scalars[k] for k in range(4))

    given_copy = pltpu.make_async_copy(w_proj, given, sems.at[2 * count, 0])
    given_copy.start()
    copies = []
    for index, piece in enumerate(pieces):
        half = core if index < count else 1 - core
        at = pl.multiple_of((scalars[4 + index % count] * n_var + half + 1) * step, step)
        for s in range(n_head):
            copy = pltpu.make_async_copy(
                piece.at[s], rows.at[s, pl.ds(at, step)], sems.at[index, s]
            )
            copy.start()
            copies.append(copy)
    rows[:, 0:step] = jnp.zeros((n_head, step, width), jnp.bfloat16)
    rows[:, tokens + step :] = jnp.zeros((n_head, step, width), jnp.bfloat16)
    columns = weights.shape[1]
    given_copy.wait()
    for s, back in enumerate(head_order(n_head)):
        source = pl.ds(pl.multiple_of(lax.rem(ours + n_head - back, n_head) * width, ALIGN), width)
        into = slice(s * width, (s + 1) * width)
        for h in range(heads):
            low, key, value = h * (2 * HD + VD), h * HD, heads * HD + h * VP
            query = heads * (HD + VP) + h * HD
            weights[into, key : key + HD] = given[source, low + HD : low + 2 * HD]
            weights[into, value : value + VD] = given[source, low + 2 * HD : low + 2 * HD + VD]
            weights[into, value + VD : value + VP] = jnp.zeros((width, VP - VD), jnp.bfloat16)
            weights[into, query : query + HD] = given[source, low : low + HD]
    at = lax.broadcasted_iota(jnp.int32, (1, columns), 1)
    ones = jnp.zeros((1, columns), jnp.float32)
    scale = jnp.where(at >= heads * (HD + VP), QSCALE, 1.0)
    for h in range(heads):
        ones = jnp.where(at == heads * HD + h * VP + VD, 1.0, ones)
    low_taps = []
    for s, back in enumerate(head_order(n_head)):
        place = jnp.bitwise_xor(ours, lax.rem(ours + n_head - back, n_head)) if n_head == 4 else s
        low_taps.append(taps[place].astype(jnp.bfloat16))
    for copy in copies:
        copy.wait()

    def make(stage, into):
        for part in range(2):
            start = (stage * 2 + part) * step
            for s in range(n_head):
                into[part * step : (part + 1) * step, s * width : (s + 1) * width] = trunk_of(
                    low_taps[s],
                    *(
                        rows[s, pl.ds(pl.multiple_of(start + shift, step), step), :]
                        for shift in (0, step, 2 * step)
                    ),
                )

    def product_of(block):
        product = jnp.dot(block, weights[...], preferred_element_type=jnp.float32)
        return (product * scale + ones).astype(jnp.bfloat16)

    def project(stage, block):
        product = product_of(block[...])
        for part in range(2):
            at = stage * 2 + part
            rows_here = slice(part * step, (part + 1) * step)
            out[pl.ds(pl.multiple_of(at * step, step), step)] = product[rows_here]
            pooled_out[pl.ds(pl.multiple_of(at * size, size), size)] = jnp.dot(
                pool_matrix(step), block[rows_here, 0:width], preferred_element_type=jnp.float32
            )

    def window(index):
        start = (first // ALIGN) * ALIGN + (index - 1) * step
        return pl.multiple_of(jnp.clip(start, 0, tokens - WIN), ALIGN)

    def make_windows(into):
        for index in range(3):
            start = window(index)
            at = start + lax.broadcasted_iota(jnp.int32, (WIN, 1), 0)
            kept = [
                jnp.where(
                    jnp.logical_or(at + shift < first, at + shift >= last), 1.0, 0.0
                ).astype(jnp.bfloat16)
                for shift in (-step, 0, step)
            ]
            for s in range(n_head):
                into[index * WIN : (index + 1) * WIN, s * width : (s + 1) * width] = trunk_of(
                    low_taps[s],
                    *(
                        rows[s, pl.ds(pl.multiple_of(start + shift, ALIGN), WIN), :] * keep
                        for shift, keep in zip((0, step, 2 * step), kept)
                    ),
                )

    stages = tokens // (2 * step)
    make(0, left)

    def two_stages(n, carry):
        make(2 * n + 1, right)
        project(2 * n, left)
        make(2 * n + 2, left)
        project(2 * n + 1, right)
        return carry

    if stages > 2:
        lax.fori_loop(0, stages // 2 - 1, two_stages, 0)
    make(stages - 1, right)
    project(stages - 2, left)
    make_windows(left)
    project(stages - 1, right)
    product = product_of(left[0 : 3 * WIN])
    for index in range(3):
        rows_here = slice(index * WIN, (index + 1) * WIN)
        out[pl.ds(window(index), WIN)] = product[rows_here]
        small = pl.multiple_of(window(index) // POOL, ALIGN // POOL)
        pooled_out[pl.ds(small, WIN // POOL)] = jnp.dot(
            pool_matrix(WIN), left[rows_here, 0:width], preferred_element_type=jnp.float32
        )


def attend_kernel(heads, own, given, order, kvq, pooled, *refs):
    mixing, out = refs[:given], refs[given]
    *mix_out, scores_a, scores_b, top_a, top_b, total, parts = refs[given + 1 :]
    if mix_out:
        w_out, w_pair = mixing[:2]
        (w_mix,) = mix_out
        width = w_pair.shape[0]
        for s in range(given - 1):
            parts[order[out.shape[0] + s]] = mixing[1 + s][...]
        for h in range(heads):
            mix = jnp.zeros((VD, w_pair.shape[1]), jnp.float32)
            for k in range(given - 1):
                mix += jnp.dot(
                    w_out[h * VD : (h + 1) * VD, k * width : (k + 1) * width],
                    parts[k],
                    preferred_element_type=jnp.float32,
                )
            w_mix[h, 0:VD] = mix.astype(jnp.bfloat16)
            w_mix[h, VD:] = jnp.zeros((VP - VD, w_pair.shape[1]), jnp.bfloat16)
    else:
        w_mix, w_pair = mixing
    tokens = kvq.shape[0]
    chunk = scores_a.shape[2]
    steps = tokens // chunk
    key_cols, value_cols = heads * HD, heads * (HD + VP)
    pool = pool_matrix(own)
    scores, tops = (scores_a, scores_b), (top_a, top_b)
    chains = [(n, h) for n in range(out.shape[0]) for h in range(heads)]

    def score(index, c):
        n, h = chains[index]
        low = value_cols + h * HD
        found = lax.dot_general(
            kvq[pl.ds(pl.multiple_of(order[n] * own, own), own), low : low + HD],
            kvq[pl.ds(pl.multiple_of(c * chunk, chunk), chunk), h * HD : (h + 1) * HD],
            (((1,), (1,)), ((), ())),
            preferred_element_type=jnp.float32,
        )
        scores[index % 2][c] = found
        best = found[:, 0:128]
        for low in range(128, chunk, 128):
            best = jnp.maximum(best, found[:, low : low + 128])
        top = tops[index % 2]
        top[...] = jnp.maximum(top[...], best)

    def clear(index):
        tops[index % 2][...] = jnp.full(top_a.shape, -jnp.inf, jnp.float32)

    clear(0)

    def first_scores(c, carry):
        score(0, c)
        return carry

    lax.fori_loop(0, steps, first_scores, 0)
    for index, (n, h) in enumerate(chains):
        more = index + 1 < len(chains)
        if more:
            clear(index + 1)
        row_max = jnp.max(tops[index % 2][...], axis=1, keepdims=True)
        total[...] = jnp.zeros(total.shape, jnp.float32)
        low = key_cols + h * VP

        def weigh(c, carry):
            weights = jnp.exp2((scores[index % 2][c] - row_max).astype(jnp.bfloat16))
            if more:
                score(index + 1, c)
            total[...] += jnp.dot(
                weights,
                kvq[pl.ds(pl.multiple_of(c * chunk, chunk), chunk), low : low + VP],
                preferred_element_type=jnp.float32,
            )
            return carry

        lax.fori_loop(0, steps, weigh, 0)
        mixed = total[...]
        mixed = (mixed * (1.0 / mixed[:, VD : VD + 1])).astype(jnp.bfloat16)
        mixed = jnp.dot(pool, mixed, preferred_element_type=jnp.float32).astype(jnp.bfloat16)
        if h == 0:
            size = own // POOL
            pair = jnp.dot(
                pooled[pl.ds(pl.multiple_of(order[n] * size, size), size)].astype(jnp.bfloat16),
                w_pair[...],
                preferred_element_type=jnp.float32,
            )
        pair = pair + jnp.dot(mixed, w_mix[h], preferred_element_type=jnp.float32)
        if h == heads - 1:
            out[n] = pair.astype(out.dtype)


def pair_kernel(
    variants, order, dist_table, row_feats, col_feats,
    out, rows, cols, table, span, blocks, sems,
):
    side = cols.shape[1]
    count = rows.shape[1]
    for s in range(variants):
        rows[order[s]] = row_feats[s].astype(jnp.float32)
        cols[order[variants + s]] = col_feats[s]

    offset = order[2 * variants] + count - 1
    bucket = lax.broadcasted_iota(jnp.int32, (count + side, NB), 1)
    distance = jnp.abs(offset - lax.broadcasted_iota(jnp.int32, (count + side, NB), 0))
    above = distance >= jnp.where(bucket == 0, 0, jnp.left_shift(1, jnp.maximum(bucket - 1, 0)))
    below = jnp.logical_or(bucket == NB - 1, distance < jnp.left_shift(1, bucket))
    one_hot = jnp.where(jnp.logical_and(above, below), 1.0, 0.0).astype(jnp.bfloat16)
    span[...] = jnp.dot(
        one_hot, dist_table[...].astype(jnp.bfloat16), preferred_element_type=jnp.float32
    )
    for s in range(SHIFTS):
        table[s] = span[s : s + count + side - SHIFTS].astype(jnp.bfloat16)

    def write(block, slot, variant):
        into = out.at[variant, pl.ds(block * ROWS, ROWS)]
        return pltpu.make_async_copy(blocks.at[slot, variant], into, sems.at[slot, variant])

    def one_block(block, carry):
        slot = lax.rem(block, 2)
        for variant in range(variants):
            pl.when(block >= 2)(write(block, slot, variant).wait)
            row_block = rows[variant, pl.ds(pl.multiple_of(block * ROWS, ROWS), ROWS), :]
            for r in range(ROWS):
                back = count - 1 - (block * ROWS + r)
                low = pl.multiple_of((back // SHIFTS) * SHIFTS, SHIFTS)
                relative = table[(count - 1 - r) % SHIFTS, pl.ds(low, side), :]
                row = jnp.broadcast_to(row_block[r : r + 1], (SHIFTS, C)).astype(jnp.bfloat16)
                found = (cols[variant] + relative).reshape(side // SHIFTS, SHIFTS, C) + row[None]
                blocks[slot, variant, r] = found.reshape(side, C)
            write(block, slot, variant).start()
        return carry

    total = count // ROWS
    lax.fori_loop(0, total, one_block, 0)
    for block in range(max(total - 2, 0), total):
        for variant in range(variants):
            write(block, block % 2, variant).wait()


def in_hbm(array):
    return pltpu.with_memory_space_constraint(array, pltpu.HBM)


def whole(memory=pltpu.VMEM):
    return pl.BlockSpec(memory_space=memory)


def shifts(array, axis):
    size = lax.axis_size(axis)
    return [array] + [
        lax.ppermute(array, axis, [(k, (k + s) % size) for k in range(size)])
        for s in range(1, size)
    ]


def doubled(array, axis):
    size, found, bit = lax.axis_size(axis), array[None], 1
    while bit < size:
        moved = lax.ppermute(found, axis, [(k, k ^ bit) for k in range(size)])
        found, bit = jnp.concatenate([found, moved]), 2 * bit
    return found


def head_order(n_head):
    return [0, 1, 3, 2] if n_head == 4 else list(range(n_head))


def gather_rows(block, taps, n_ctx, n_var, n_head, core):
    crossing = lambda array: lax.ppermute(array, "var", [(0, 1), (1, 0)])
    if n_head == 4:
        shift = lambda array, s: lax.ppermute(array, "head", [(k, (k + s) % 4) for k in range(4)])
        over = lambda array, bit: lax.ppermute(array, "ctx", [(k, k ^ bit) for k in range(4)])
        near = jnp.stack([block, shift(block, 1), shift(block, 3)])
        far = shift(block, 2)[None]
        slab, over_x, over_y = (
            jnp.concatenate(pair)
            for pair in (
                (near, far), (over(near, 1), over(far, 1)), (over(near, 2), over(far, 2))
            )
        )
        pairs = [(2 * k + c, 2 * (k ^ (c + 1)) + c) for k in range(4) for c in range(2)]
        corner = lax.ppermute(jnp.where(core == 0, over_y, over_x), ("ctx", "var"), pairs)
        pieces = [slab, over_x, over_y]
        for bit in (1, 2):
            moved = lax.ppermute(taps, "head", [(k, k ^ bit) for k in range(4)])
            taps = jnp.concatenate([taps, moved])
        corner, crossed, taps = lax.optimization_barrier(
            (corner, [crossing(piece) for piece in pieces], taps)
        )
        return pieces + [corner], crossed + [crossing(corner)], taps
    pieces = shifts(jnp.stack(shifts(block, "head")), "ctx")
    crossed = [crossing(piece) for piece in pieces]
    return pieces, crossed, jnp.concatenate(shifts(taps, "head"))


def local(sequence, deletions, conv_taps, conv_bias, w_proj, w_out, w_pair, dist_table):
    own, width = sequence.shape
    variants = deletions.shape[0]
    heads = w_out.shape[0] // VD
    n_ctx, n_head, n_var = (lax.axis_size(name) for name in ("ctx", "head", "var"))
    if n_ctx != n_head or n_var != 2 or n_ctx % variants:
        raise ValueError("mesh shape")
    step = own // n_var
    tokens = n_ctx * own
    pair_rows = own // POOL
    columns = heads * (2 * HD + VP)
    splits = n_ctx // variants
    mine, ours, core = (lax.axis_index(name) for name in ("ctx", "head", "var"))

    half = lax.dynamic_slice_in_dim(sequence, core * step, step, 0)
    taps = jnp.concatenate([conv_taps, conv_bias[None]], 0)
    pieces, crossed, taps = gather_rows(half, taps, n_ctx, n_var, n_head, core)
    if n_ctx == 4 and n_head == 4:
        blocks = [mine, mine ^ 1, mine ^ 2, mine ^ 3]
    else:
        blocks = [(mine + n_ctx - s) % n_ctx for s in range(n_ctx)]
    scalars = jnp.concatenate(
        [
            jnp.stack([ours, core]).astype(jnp.int32),
            lax.dynamic_index_in_dim(deletions, mine // splits, 0, keepdims=False),
            jnp.stack(blocks).astype(jnp.int32),
        ]
    )
    kvq, pooled = pl.pallas_call(
        functools.partial(project_kernel, heads, n_var, n_head, len(pieces)),
        out_shape=(
            jax.ShapeDtypeStruct((tokens, columns), jnp.bfloat16),
            jax.ShapeDtypeStruct((tokens // POOL, width), jnp.float32),
        ),
        in_specs=[whole(pltpu.SMEM), whole(pltpu.HBM)]
        + [whole()]
        + [whole(pltpu.HBM)] * (2 * len(pieces)),
        out_specs=(whole(), whole()),
        scratch_shapes=[
            pltpu.VMEM(w_proj.shape, jnp.bfloat16),
            pltpu.VMEM((n_head * width, columns), jnp.bfloat16),
            pltpu.VMEM((n_head, tokens + 2 * step, width), jnp.bfloat16),
            pltpu.VMEM((2 * step, n_head * width), jnp.bfloat16),
            pltpu.VMEM((2 * step, n_head * width), jnp.bfloat16),
            pltpu.SemaphoreType.DMA((2 * len(pieces) + 1, n_head)),
        ],
        compiler_params=pltpu.CompilerParams(vmem_limit_bytes=(34 if splits == 1 else 52) * MIB),
        cost_estimate=pl.CostEstimate(
            flops=2 * (tokens + 3 * WIN) * n_head * width * columns,
            bytes_accessed=4 * tokens * n_head * width,
            transcendentals=tokens * n_head * width,
        ),
        name="project",
    )(
        scalars,
        in_hbm(w_proj),
        taps.reshape(n_head, 4, width),
        *(in_hbm(piece) for piece in pieces + crossed),
    )

    chunk = min(tokens, CHUNK)

    pair_parts = shifts(w_pair, "head")
    order_of_parts = [(ours + n_head - s) % n_head for s in range(n_head)]

    def attend(order, dtype, w_mix):
        count = order.shape[0]
        mix_shape = jax.ShapeDtypeStruct((heads, VP, 2 * C), jnp.bfloat16)
        out_shape = [jax.ShapeDtypeStruct((count, pair_rows, 2 * C), dtype)]
        if w_mix is None:
            mixing, out_shape = [w_out, *pair_parts], out_shape + [mix_shape]
            order = jnp.concatenate([order, jnp.stack(order_of_parts)])
        else:
            mixing = [w_mix, w_pair]
        return pl.pallas_call(
            functools.partial(attend_kernel, heads, own, len(mixing)),
            out_shape=out_shape,
            in_specs=[whole(pltpu.SMEM)] + [whole()] * (2 + len(mixing)),
            out_specs=[whole()] * len(out_shape),
            scratch_shapes=[
                pltpu.VMEM((tokens // chunk, own, chunk), jnp.float32),
                pltpu.VMEM((tokens // chunk, own, chunk), jnp.float32),
                pltpu.VMEM((own, 128), jnp.float32),
                pltpu.VMEM((own, 128), jnp.float32),
                pltpu.VMEM((own, VP), jnp.float32),
                pltpu.VMEM((n_head, width, 2 * C), jnp.bfloat16),
            ],
            compiler_params=pltpu.CompilerParams(
                vmem_limit_bytes=(22 if splits == 1 else 52) * MIB
            ),
            cost_estimate=pl.CostEstimate(
                flops=2 * count * heads * own * tokens * (2 * HD + VP),
                bytes_accessed=2 * tokens * columns,
                transcendentals=count * heads * own * tokens,
            ),
            name="attend",
        )(order.astype(jnp.int32), kvq, pooled, *mixing)

    if splits == 1:
        sent, w_mix = attend((ours + jnp.arange(1, n_head)) % n_head, jnp.bfloat16, None)
        summed = attend(ours[None], jnp.float32, w_mix)[0][0]
        for s in range(1, n_head):
            pairs = [(k, (k + s) % n_head) for k in range(n_head)]
            summed += lax.ppermute(sent[s - 1], "head", pairs).astype(jnp.float32)
        turned = lax.ppermute(
            summed[:, :C].astype(jnp.bfloat16),
            ("ctx", "head"),
            [(i * n_head + h, h * n_head + i) for i in range(n_ctx) for h in range(n_head)],
        )
        row_feats = doubled(turned, "head")
        col_feats = doubled(summed[:, C:].astype(jnp.bfloat16), "ctx")
        order = [at ^ s for at in (ours, mine) for s in range(variants)]
    else:
        blocks_here = n_ctx // splits
        here = (mine % splits) * blocks_here + jnp.arange(blocks_here)
        part = attend(here, jnp.bfloat16, None)[0]
        feats = lax.all_gather(lax.psum(part, "head"), "ctx", axis=0, tiled=False)
        feats = feats.reshape(variants, n_ctx, pair_rows, 2 * C)
        row_feats = lax.dynamic_index_in_dim(feats, mine, 1, keepdims=False)[:, :, :C]
        col_feats = lax.dynamic_index_in_dim(feats, ours, 1, keepdims=False)[:, :, C:]
        order = list(range(variants)) * 2

    return pl.pallas_call(
        functools.partial(pair_kernel, variants),
        out_shape=jax.ShapeDtypeStruct((variants, pair_rows, pair_rows, C), jnp.bfloat16),
        in_specs=[whole(pltpu.SMEM)] + [whole()] * 3,
        out_specs=whole(pl.ANY),
        scratch_shapes=[
            pltpu.VMEM((variants, pair_rows, C), jnp.float32),
            pltpu.VMEM((variants, pair_rows, C), jnp.bfloat16),
            pltpu.VMEM((SHIFTS, 2 * pair_rows - SHIFTS, C), jnp.bfloat16),
            pltpu.VMEM((2 * pair_rows, C), jnp.float32),
            pltpu.VMEM((2, variants, ROWS, pair_rows, C), jnp.bfloat16),
            pltpu.SemaphoreType.DMA((2, variants)),
        ],
        compiler_params=pltpu.CompilerParams(vmem_limit_bytes=24 * MIB),
        name="pair_map",
    )(
        jnp.stack([*order, (mine - ours) * pair_rows]).astype(jnp.int32),
        dist_table,
        row_feats,
        col_feats,
    )


def solution(mesh):
    in_specs = (
        P("ctx", "head"),
        P("var", None),
        P(None, "head"),
        P("head"),
        P(None, "head"),
        P("head", None),
        P("head", None),
        P(),
    )
    out_specs = P("var", "ctx", "head", None)
    return jax.shard_map(local, mesh=mesh, in_specs=in_specs, out_specs=out_specs, check_vma=False)
```

```python
import functools
import math

import jax
import jax.numpy as jnp
from jax import lax
from jax.experimental import pallas as pl
from jax.experimental.pallas import tpu as pltpu
from jax.sharding import PartitionSpec as P

HD = 128
VD = 192
VP = 256
C = 128
NB = 16
POOL = 4
WIN = 160
ALIGN = 32
CHUNK = 2048
SHIFTS = 16
ROWS = 16
MIB = 1024 * 1024
QSCALE = math.log2(math.e) / math.sqrt(HD)
GELU_A = math.sqrt(2.0 / math.pi)
GELU_B = GELU_A * 0.044715


def trunk_of(taps, low, middle, high):
    convolved = taps[0:1] * low + taps[1:2] * middle + taps[2:3] * high + taps[3:4]
    half = 0.5 * convolved
    bent = jnp.tanh(convolved * (GELU_A + GELU_B * (convolved * convolved)))
    return middle + (half + half * bent)


def pool_matrix(count):
    wide = lax.broadcasted_iota(jnp.int32, (count // POOL, count), 1) // POOL
    tall = lax.broadcasted_iota(jnp.int32, (count // POOL, count), 0)
    return jnp.where(wide == tall, 1.0 / POOL, 0.0).astype(jnp.bfloat16)


def project_kernel(heads, n_var, n_head, count, scalars, w_proj, *refs):
    taps, pieces = refs[0], refs[1 : 1 + 2 * count]
    out, pooled_out, given, weights, rows, left, right, sems = refs[1 + 2 * count :]
    step, width = pieces[0].shape[1:]
    tokens = rows.shape[1] - 2 * step
    size = step // POOL
    ours, core, first, last = (scalars[k] for k in range(4))

    given_copy = pltpu.make_async_copy(w_proj, given, sems.at[2 * count, 0])
    given_copy.start()
    copies = []
    for index, piece in enumerate(pieces):
        half = core if index < count else 1 - core
        at = pl.multiple_of((scalars[4 + index % count] * n_var + half + 1) * step, step)
        for s in range(n_head):
            copy = pltpu.make_async_copy(
                piece.at[s], rows.at[s, pl.ds(at, step)], sems.at[index, s]
            )
            copy.start()
            copies.append(copy)
    rows[:, 0:step] = jnp.zeros((n_head, step, width), jnp.bfloat16)
    rows[:, tokens + step :] = jnp.zeros((n_head, step, width), jnp.bfloat16)
    columns = weights.shape[1]
    given_copy.wait()
    for s, back in enumerate(head_order(n_head)):
        source = pl.ds(pl.multiple_of(lax.rem(ours + n_head - back, n_head) * width, ALIGN), width)
        into = slice(s * width, (s + 1) * width)
        for h in range(heads):
            low, key, value = h * (2 * HD + VD), h * HD, heads * HD + h * VP
            query = heads * (HD + VP) + h * HD
            weights[into, key : key + HD] = given[source, low + HD : low + 2 * HD]
            weights[into, value : value + VD] = given[source, low + 2 * HD : low + 2 * HD + VD]
            weights[into, value + VD : value + VP] = jnp.zeros((width, VP - VD), jnp.bfloat16)
            weights[into, query : query + HD] = given[source, low : low + HD]
    at = lax.broadcasted_iota(jnp.int32, (1, columns), 1)
    ones = jnp.zeros((1, columns), jnp.float32)
    scale = jnp.where(at >= heads * (HD + VP), QSCALE, 1.0)
    for h in range(heads):
        ones = jnp.where(at == heads * HD + h * VP + VD, 1.0, ones)
    low_taps = []
    for s, back in enumerate(head_order(n_head)):
        place = jnp.bitwise_xor(ours, lax.rem(ours + n_head - back, n_head)) if n_head == 4 else s
        low_taps.append(taps[place].astype(jnp.bfloat16))
    for copy in copies:
        copy.wait()

    def make(stage, into):
        for part in range(2):
            start = (stage * 2 + part) * step
            for s in range(n_head):
                into[part * step : (part + 1) * step, s * width : (s + 1) * width] = trunk_of(
                    low_taps[s],
                    *(
                        rows[s, pl.ds(pl.multiple_of(start + shift, step), step), :]
                        for shift in (0, step, 2 * step)
                    ),
                )

    def product_of(block):
        product = jnp.dot(block, weights[...], preferred_element_type=jnp.float32)
        return (product * scale + ones).astype(jnp.bfloat16)

    def project(stage, block):
        product = product_of(block[...])
        for part in range(2):
            at = stage * 2 + part
            rows_here = slice(part * step, (part + 1) * step)
            out[pl.ds(pl.multiple_of(at * step, step), step)] = product[rows_here]
            pooled_out[pl.ds(pl.multiple_of(at * size, size), size)] = jnp.dot(
                pool_matrix(step), block[rows_here, 0:width], preferred_element_type=jnp.float32
            )

    def window(index):
        start = (first // ALIGN) * ALIGN + (index - 1) * step
        return pl.multiple_of(jnp.clip(start, 0, tokens - WIN), ALIGN)

    def make_windows(into):
        for index in range(3):
            start = window(index)
            at = start + lax.broadcasted_iota(jnp.int32, (WIN, 1), 0)
            kept = [
                jnp.where(
                    jnp.logical_or(at + shift < first, at + shift >= last), 1.0, 0.0
                ).astype(jnp.bfloat16)
                for shift in (-step, 0, step)
            ]
            for s in range(n_head):
                into[index * WIN : (index + 1) * WIN, s * width : (s + 1) * width] = trunk_of(
                    low_taps[s],
                    *(
                        rows[s, pl.ds(pl.multiple_of(start + shift, ALIGN), WIN), :] * keep
                        for shift, keep in zip((0, step, 2 * step), kept)
                    ),
                )

    stages = tokens // (2 * step)
    make(0, left)

    def two_stages(n, carry):
        make(2 * n + 1, right)
        project(2 * n, left)
        make(2 * n + 2, left)
        project(2 * n + 1, right)
        return carry

    if stages > 2:
        lax.fori_loop(0, stages // 2 - 1, two_stages, 0)
    make(stages - 1, right)
    project(stages - 2, left)
    make_windows(left)
    project(stages - 1, right)
    product = product_of(left[0 : 3 * WIN])
    for index in range(3):
        rows_here = slice(index * WIN, (index + 1) * WIN)
        out[pl.ds(window(index), WIN)] = product[rows_here]
        small = pl.multiple_of(window(index) // POOL, ALIGN // POOL)
        pooled_out[pl.ds(small, WIN // POOL)] = jnp.dot(
            pool_matrix(WIN), left[rows_here, 0:width], preferred_element_type=jnp.float32
        )


def attend_kernel(heads, own, given, order, kvq, pooled, *refs):
    mixing, out = refs[:given], refs[given]
    *mix_out, scores_a, scores_b, top_a, top_b, total, parts = refs[given + 1 :]
    if mix_out:
        w_out, w_pair = mixing[:2]
        (w_mix,) = mix_out
        width = w_pair.shape[0]
        for s in range(given - 1):
            parts[order[out.shape[0] + s]] = mixing[1 + s][...]
        for h in range(heads):
            mix = jnp.zeros((VD, w_pair.shape[1]), jnp.float32)
            for k in range(given - 1):
                mix += jnp.dot(
                    w_out[h * VD : (h + 1) * VD, k * width : (k + 1) * width],
                    parts[k],
                    preferred_element_type=jnp.float32,
                )
            w_mix[h, 0:VD] = mix.astype(jnp.bfloat16)
            w_mix[h, VD:] = jnp.zeros((VP - VD, w_pair.shape[1]), jnp.bfloat16)
    else:
        w_mix, w_pair = mixing
    tokens = kvq.shape[0]
    chunk = scores_a.shape[2]
    steps = tokens // chunk
    key_cols, value_cols = heads * HD, heads * (HD + VP)
    pool = pool_matrix(own)
    scores, tops = (scores_a, scores_b), (top_a, top_b)
    chains = [(n, h) for n in range(out.shape[0]) for h in range(heads)]

    def score(index, c):
        n, h = chains[index]
        low = value_cols + h * HD
        found = lax.dot_general(
            kvq[pl.ds(pl.multiple_of(order[n] * own, own), own), low : low + HD],
            kvq[pl.ds(pl.multiple_of(c * chunk, chunk), chunk), h * HD : (h + 1) * HD],
            (((1,), (1,)), ((), ())),
            preferred_element_type=jnp.float32,
        )
        scores[index % 2][c] = found
        best = found[:, 0:128]
        for low in range(128, chunk, 128):
            best = jnp.maximum(best, found[:, low : low + 128])
        top = tops[index % 2]
        top[...] = jnp.maximum(top[...], best)

    def clear(index):
        tops[index % 2][...] = jnp.full(top_a.shape, -jnp.inf, jnp.float32)

    clear(0)

    def first_scores(c, carry):
        score(0, c)
        return carry

    lax.fori_loop(0, steps, first_scores, 0)
    for index, (n, h) in enumerate(chains):
        more = index + 1 < len(chains)
        if more:
            clear(index + 1)
        row_max = jnp.max(tops[index % 2][...], axis=1, keepdims=True)
        total[...] = jnp.zeros(total.shape, jnp.float32)
        low = key_cols + h * VP

        def weigh(c, carry):
            weights = jnp.exp2((scores[index % 2][c] - row_max).astype(jnp.bfloat16))
            if more:
                score(index + 1, c)
            total[...] += jnp.dot(
                weights,
                kvq[pl.ds(pl.multiple_of(c * chunk, chunk), chunk), low : low + VP],
                preferred_element_type=jnp.float32,
            )
            return carry

        lax.fori_loop(0, steps, weigh, 0)
        mixed = total[...]
        mixed = (mixed * (1.0 / mixed[:, VD : VD + 1])).astype(jnp.bfloat16)
        mixed = jnp.dot(pool, mixed, preferred_element_type=jnp.float32).astype(jnp.bfloat16)
        if h == 0:
            size = own // POOL
            pair = jnp.dot(
                pooled[pl.ds(pl.multiple_of(order[n] * size, size), size)].astype(jnp.bfloat16),
                w_pair[...],
                preferred_element_type=jnp.float32,
            )
        pair = pair + jnp.dot(mixed, w_mix[h], preferred_element_type=jnp.float32)
        if h == heads - 1:
            out[n] = pair.astype(out.dtype)


def pair_kernel(
    variants, order, dist_table, row_feats, col_feats,
    out, rows, cols, table, span, blocks, sems,
):
    side = cols.shape[1]
    count = rows.shape[1]
    for s in range(variants):
        rows[order[s]] = row_feats[s].astype(jnp.float32)
        cols[order[variants + s]] = col_feats[s]

    offset = order[2 * variants] + count - 1
    bucket = lax.broadcasted_iota(jnp.int32, (count + side, NB), 1)
    distance = jnp.abs(offset - lax.broadcasted_iota(jnp.int32, (count + side, NB), 0))
    above = distance >= jnp.where(bucket == 0, 0, jnp.left_shift(1, jnp.maximum(bucket - 1, 0)))
    below = jnp.logical_or(bucket == NB - 1, distance < jnp.left_shift(1, bucket))
    one_hot = jnp.where(jnp.logical_and(above, below), 1.0, 0.0).astype(jnp.bfloat16)
    span[...] = jnp.dot(
        one_hot, dist_table[...].astype(jnp.bfloat16), preferred_element_type=jnp.float32
    )
    for s in range(SHIFTS):
        table[s] = span[s : s + count + side - SHIFTS].astype(jnp.bfloat16)

    def write(block, slot, variant):
        into = out.at[variant, pl.ds(block * ROWS, ROWS)]
        return pltpu.make_async_copy(blocks.at[slot, variant], into, sems.at[slot, variant])

    def one_block(block, carry):
        slot = lax.rem(block, 2)
        for variant in range(variants):
            pl.when(block >= 2)(write(block, slot, variant).wait)
            row_block = rows[variant, pl.ds(pl.multiple_of(block * ROWS, ROWS), ROWS), :]
            for r in range(ROWS):
                back = count - 1 - (block * ROWS + r)
                low = pl.multiple_of((back // SHIFTS) * SHIFTS, SHIFTS)
                relative = table[(count - 1 - r) % SHIFTS, pl.ds(low, side), :]
                row = jnp.broadcast_to(row_block[r : r + 1], (SHIFTS, C)).astype(jnp.bfloat16)
                found = (cols[variant] + relative).reshape(side // SHIFTS, SHIFTS, C) + row[None]
                blocks[slot, variant, r] = found.reshape(side, C)
            write(block, slot, variant).start()
        return carry

    total = count // ROWS
    lax.fori_loop(0, total, one_block, 0)
    for block in range(max(total - 2, 0), total):
        for variant in range(variants):
            write(block, block % 2, variant).wait()


def in_hbm(array):
    return pltpu.with_memory_space_constraint(array, pltpu.HBM)


def whole(memory=pltpu.VMEM):
    return pl.BlockSpec(memory_space=memory)


def shifts(array, axis):
    size = lax.axis_size(axis)
    return [array] + [
        lax.ppermute(array, axis, [(k, (k + s) % size) for k in range(size)])
        for s in range(1, size)
    ]


def doubled(array, axis):
    size, found, bit = lax.axis_size(axis), array[None], 1
    while bit < size:
        moved = lax.ppermute(found, axis, [(k, k ^ bit) for k in range(size)])
        found, bit = jnp.concatenate([found, moved]), 2 * bit
    return found


def head_order(n_head):
    return [0, 1, 3, 2] if n_head == 4 else list(range(n_head))


def gather_rows(block, taps, n_ctx, n_var, n_head, core):
    crossing = lambda array: lax.ppermute(array, "var", [(0, 1), (1, 0)])
    if n_head == 4:
        shift = lambda array, s: lax.ppermute(array, "head", [(k, (k + s) % 4) for k in range(4)])
        over = lambda array, bit: lax.ppermute(array, "ctx", [(k, k ^ bit) for k in range(4)])
        near = jnp.stack([block, shift(block, 1), shift(block, 3)])
        far = shift(block, 2)[None]
        slab, over_x, over_y = (
            jnp.concatenate(pair)
            for pair in (
                (near, far), (over(near, 1), over(far, 1)), (over(near, 2), over(far, 2))
            )
        )
        pairs = [(2 * k + c, 2 * (k ^ (c + 1)) + c) for k in range(4) for c in range(2)]
        corner = lax.ppermute(jnp.where(core == 0, over_y, over_x), ("ctx", "var"), pairs)
        pieces = [slab, over_x, over_y]
        for bit in (1, 2):
            moved = lax.ppermute(taps, "head", [(k, k ^ bit) for k in range(4)])
            taps = jnp.concatenate([taps, moved])
        corner, crossed, taps = lax.optimization_barrier(
            (corner, [crossing(piece) for piece in pieces], taps)
        )
        return pieces + [corner], crossed + [crossing(corner)], taps
    pieces = shifts(jnp.stack(shifts(block, "head")), "ctx")
    crossed = [crossing(piece) for piece in pieces]
    return pieces, crossed, jnp.concatenate(shifts(taps, "head"))


def local(sequence, deletions, conv_taps, conv_bias, w_proj, w_out, w_pair, dist_table):
    own, width = sequence.shape
    variants = deletions.shape[0]
    heads = w_out.shape[0] // VD
    n_ctx, n_head, n_var = (lax.axis_size(name) for name in ("ctx", "head", "var"))
    if n_ctx != n_head or n_var != 2 or n_ctx % variants:
        raise ValueError("mesh shape")
    step = own // n_var
    tokens = n_ctx * own
    pair_rows = own // POOL
    columns = heads * (2 * HD + VP)
    splits = n_ctx // variants
    mine, ours, core = (lax.axis_index(name) for name in ("ctx", "head", "var"))

    half = lax.dynamic_slice_in_dim(sequence, core * step, step, 0)
    taps = jnp.concatenate([conv_taps, conv_bias[None]], 0)
    pieces, crossed, taps = gather_rows(half, taps, n_ctx, n_var, n_head, core)
    if n_ctx == 4 and n_head == 4:
        blocks = [mine, mine ^ 1, mine ^ 2, mine ^ 3]
    else:
        blocks = [(mine + n_ctx - s) % n_ctx for s in range(n_ctx)]
    scalars = jnp.concatenate(
        [
            jnp.stack([ours, core]).astype(jnp.int32),
            lax.dynamic_index_in_dim(deletions, mine // splits, 0, keepdims=False),
            jnp.stack(blocks).astype(jnp.int32),
        ]
    )
    kvq, pooled = pl.pallas_call(
        functools.partial(project_kernel, heads, n_var, n_head, len(pieces)),
        out_shape=(
            jax.ShapeDtypeStruct((tokens, columns), jnp.bfloat16),
            jax.ShapeDtypeStruct((tokens // POOL, width), jnp.float32),
        ),
        in_specs=[whole(pltpu.SMEM), whole(pltpu.HBM)]
        + [whole()]
        + [whole(pltpu.HBM)] * (2 * len(pieces)),
        out_specs=(whole(), whole()),
        scratch_shapes=[
            pltpu.VMEM(w_proj.shape, jnp.bfloat16),
            pltpu.VMEM((n_head * width, columns), jnp.bfloat16),
            pltpu.VMEM((n_head, tokens + 2 * step, width), jnp.bfloat16),
            pltpu.VMEM((2 * step, n_head * width), jnp.bfloat16),
            pltpu.VMEM((2 * step, n_head * width), jnp.bfloat16),
            pltpu.SemaphoreType.DMA((2 * len(pieces) + 1, n_head)),
        ],
        compiler_params=pltpu.CompilerParams(vmem_limit_bytes=(34 if splits == 1 else 52) * MIB),
        cost_estimate=pl.CostEstimate(
            flops=2 * (tokens + 3 * WIN) * n_head * width * columns,
            bytes_accessed=4 * tokens * n_head * width,
            transcendentals=tokens * n_head * width,
        ),
        name="project",
    )(
        scalars,
        in_hbm(w_proj),
        taps.reshape(n_head, 4, width),
        *(in_hbm(piece) for piece in pieces + crossed),
    )

    chunk = min(tokens, CHUNK)

    pair_parts = list(doubled(w_pair, "head"))
    order_of_parts = [ours ^ s for s in range(n_head)]

    def attend(order, dtype, w_mix):
        count = order.shape[0]
        mix_shape = jax.ShapeDtypeStruct((heads, VP, 2 * C), jnp.bfloat16)
        out_shape = [jax.ShapeDtypeStruct((count, pair_rows, 2 * C), dtype)]
        if w_mix is None:
            mixing, out_shape = [w_out, *pair_parts], out_shape + [mix_shape]
            order = jnp.concatenate([order, jnp.stack(order_of_parts)])
        else:
            mixing = [w_mix, w_pair]
        return pl.pallas_call(
            functools.partial(attend_kernel, heads, own, len(mixing)),
            out_shape=out_shape,
            in_specs=[whole(pltpu.SMEM)] + [whole()] * (2 + len(mixing)),
            out_specs=[whole()] * len(out_shape),
            scratch_shapes=[
                pltpu.VMEM((tokens // chunk, own, chunk), jnp.float32),
                pltpu.VMEM((tokens // chunk, own, chunk), jnp.float32),
                pltpu.VMEM((own, 128), jnp.float32),
                pltpu.VMEM((own, 128), jnp.float32),
                pltpu.VMEM((own, VP), jnp.float32),
                pltpu.VMEM((n_head, width, 2 * C), jnp.bfloat16),
            ],
            compiler_params=pltpu.CompilerParams(
                vmem_limit_bytes=(22 if splits == 1 else 52) * MIB
            ),
            cost_estimate=pl.CostEstimate(
                flops=2 * count * heads * own * tokens * (2 * HD + VP),
                bytes_accessed=2 * tokens * columns,
                transcendentals=count * heads * own * tokens,
            ),
            name="attend",
        )(order.astype(jnp.int32), kvq, pooled, *mixing)

    if splits == 1:
        sent, w_mix = attend((ours + jnp.arange(1, n_head)) % n_head, jnp.bfloat16, None)
        summed = attend(ours[None], jnp.float32, w_mix)[0][0]
        for s in range(1, n_head):
            pairs = [(k, (k + s) % n_head) for k in range(n_head)]
            summed += lax.ppermute(sent[s - 1], "head", pairs).astype(jnp.float32)
        turned = lax.ppermute(
            summed[:, :C].astype(jnp.bfloat16),
            ("ctx", "head"),
            [(i * n_head + h, h * n_head + i) for i in range(n_ctx) for h in range(n_head)],
        )
        row_feats = doubled(turned, "head")
        col_feats = doubled(summed[:, C:].astype(jnp.bfloat16), "ctx")
        order = [at ^ s for at in (ours, mine) for s in range(variants)]
    else:
        blocks_here = n_ctx // splits
        here = (mine % splits) * blocks_here + jnp.arange(blocks_here)
        part = attend(here, jnp.bfloat16, None)[0]
        feats = lax.all_gather(lax.psum(part, "head"), "ctx", axis=0, tiled=False)
        feats = feats.reshape(variants, n_ctx, pair_rows, 2 * C)
        row_feats = lax.dynamic_index_in_dim(feats, mine, 1, keepdims=False)[:, :, :C]
        col_feats = lax.dynamic_index_in_dim(feats, ours, 1, keepdims=False)[:, :, C:]
        order = list(range(variants)) * 2

    return pl.pallas_call(
        functools.partial(pair_kernel, variants),
        out_shape=jax.ShapeDtypeStruct((variants, pair_rows, pair_rows, C), jnp.bfloat16),
        in_specs=[whole(pltpu.SMEM)] + [whole()] * 3,
        out_specs=whole(pl.ANY),
        scratch_shapes=[
            pltpu.VMEM((variants, pair_rows, C), jnp.float32),
            pltpu.VMEM((variants, pair_rows, C), jnp.bfloat16),
            pltpu.VMEM((SHIFTS, 2 * pair_rows - SHIFTS, C), jnp.bfloat16),
            pltpu.VMEM((2 * pair_rows, C), jnp.float32),
            pltpu.VMEM((2, variants, ROWS, pair_rows, C), jnp.bfloat16),
            pltpu.SemaphoreType.DMA((2, variants)),
        ],
        compiler_params=pltpu.CompilerParams(vmem_limit_bytes=24 * MIB),
        name="pair_map",
    )(
        jnp.stack([*order, (mine - ours) * pair_rows]).astype(jnp.int32),
        dist_table,
        row_feats,
        col_feats,
    )


def solution(mesh):
    in_specs = (
        P("ctx", "head"),
        P("var", None),
        P(None, "head"),
        P("head"),
        P(None, "head"),
        P("head", None),
        P("head", None),
        P(),
    )
    out_specs = P("var", "ctx", "head", None)
    return jax.shard_map(local, mesh=mesh, in_specs=in_specs, out_specs=out_specs, check_vma=False)
```
